32 devices in a mesh: rows: 4 (over y, core), cols: 8 (over z, x).
Axes of the slice: x: 2, y: 2, z: 4, core: 2. Of those that a mesh axis runs over, the one named last changes fastest.
Arguments:
- tokens: bfloat16 [2048, 2048], P('rows', 'cols'), may hold values from -6 to 6
- cotangent: bfloat16 [2048, 2048], P('rows', 'cols'), may hold values from -6 to 6
- lengths: int32 [4, 3], P('rows'), may hold values from 1 to 256, 512 in all within a row
- decay_rate: float32 [16], P('cols'), may hold values from 0.003 to 0.06
- query_weight: bfloat16 [2048, 2048], P('rows', 'cols'), may hold values from -0.125 to 0.125
- key_weight: bfloat16 [2048, 2048], P('rows', 'cols'), may hold values from -0.125 to 0.125
- value_weight: bfloat16 [2048, 2048], P('rows', 'cols'), may hold values from -0.125 to 0.125
- gate_weight: bfloat16 [2048, 2048], P('rows', 'cols'), may hold values from -0.125 to 0.125
- out_weight: bfloat16 [2048, 2048], P('cols', 'rows'), may hold values from -0.25 to 0.25
- first_weight: bfloat16 [2048, 5632], P('rows', 'cols'), may hold values from -0.125 to 0.125
- second_weight: bfloat16 [2048, 5632], P('rows', 'cols'), may hold values from -0.125 to 0.125
- down_weight: bfloat16 [5632, 2048], P('cols', 'rows'), may hold values from -0.078125 to 0.078125
Outputs:
- layer_out: bfloat16 [2048, 2048], P('rows', 'cols')
- token_grad: float32 [2048, 2048], P('rows', 'cols')
- query_grad: float32 [2048, 2048], P('rows', 'cols')
- key_grad: float32 [2048, 2048], P('rows', 'cols')
- value_grad: float32 [2048, 2048], P('rows', 'cols')
- gate_grad: float32 [2048, 2048], P('rows', 'cols')
- out_grad: float32 [2048, 2048], P('cols', 'rows')
- first_grad: float32 [2048, 5632], P('rows', 'cols')
- second_grad: float32 [2048, 5632], P('rows', 'cols')
- down_grad: float32 [5632, 2048], P('cols', 'rows')
The draws below stay inside these ranges and needn't reach their ends.
Inputs may be any that keep to these rules, and one draw needn't show every extreme that they name: Each group's lengths add up to 512, and in every group the longest is exactly 256.
All inputs are finite; a program needn't handle non-finite values.
Results may differ from the reference program's by a relative error of at most 0.014.
Values may be sent and summed in bfloat16 or wider, within the bound.
No kernel may reach another device: no remote copies, remote signals or barrier semaphores. Data moves between devices by JAX's collectives and lax.ppermute only.
A program may use at most 192 MiB of HBM per device.

```python
import math
import jax
import jax.numpy as jnp
import numpy as np
from jax import lax

D = 2048
HEADS = 16
HEAD = 128
FF = 5632
TOK_DEV = 512
LONGEST = 256
SEQS = 3
TOKENS = 2048
N_ROWS = 4


def block_scale(key, shape, split, low, largest):
    def one(dim, parts):
        steps = jax.random.uniform(jax.random.fold_in(jax.random.fold_in(key, 6), dim), (parts,), jnp.float32, low / len(split), largest / len(split))
        return jnp.repeat(jnp.exp(steps), shape[dim] // parts).reshape((-1,) + (1,) * (len(shape) - dim - 1))

    factor_of = one(*split[0])
    for cut in split[1:]:
        factor_of = factor_of * one(*cut)
    return factor_of


def split_up(number_of, total, reach, lean):
    portions = [(1 << 20) // math.isqrt(standing ** lean) + 1 for standing in range(2, number_of + 1)]
    spare, holding = total - reach - (number_of - 1), [1] * (number_of - 1)
    while spare > 0:
        free = [i for i in range(number_of - 1) if holding[i] < reach]
        whole, budget = sum([portions[i] for i in free]), spare
        for i in free:
            addition = min(reach - holding[i], max(1, budget * portions[i] // whole), spare)
            holding[i] = holding[i] + addition
            spare = spare - addition
    return np.array([reach] + holding)


def uneven_parts(key, amount, total, most, lean):
    if amount == 2:
        one = jax.random.randint(key, (), max(1, total - most), min(most, total - 1) + 1)
        return jnp.stack([one, total - one])
    sizes = jnp.asarray(split_up(amount, total, most, lean), jnp.int32)
    couples = (amount - 1) // 2
    giver, taker = sizes[1:1 + 2 * couples:2], sizes[2:2 + 2 * couples:2]
    room = jnp.minimum(giver - 1, most - taker)
    shifted = jax.random.randint(jax.random.fold_in(key, 1), (couples,), 0, 1 << 20) % (room + 1)
    sizes = sizes.at[1:1 + 2 * couples:2].set(giver - shifted).at[2:2 + 2 * couples:2].set(taker + shifted)
    return sizes[jax.random.permutation(jax.random.fold_in(key, 2), amount)]


def bell_draw(rng, shape, spread, limit, pieces=(), kind=jnp.bfloat16):
    drawn = spread * jax.random.normal(rng, shape, jnp.float32)
    if pieces:
        drawn = drawn * block_scale(rng, shape, pieces, -0.22, 0.18)
    return jnp.clip(drawn, -limit, limit).astype(kind)


def setup_inputs(seed: int = 0) -> dict:
    seeds = jax.random.split(jax.random.key(seed), 13)
    return {
        "tokens": bell_draw(seeds[0], (TOKENS, D), 1.0, 6.0, ((0, 4), (1, 8))),
        "cotangent": bell_draw(seeds[1], (TOKENS, D), 1.0, 6.0, ((0, 4), (1, 8))),
        "lengths": jax.vmap(lambda own: uneven_parts(own, SEQS, TOK_DEV, LONGEST, 2))(jax.random.split(seeds[2], N_ROWS)).reshape((N_ROWS, SEQS)).astype(jnp.int32),
        "decay_rate": jnp.clip(jnp.exp(math.log(0.06) - 2.9957322 * jax.random.uniform(seeds[3], (HEADS,), jnp.float32) ** block_scale(seeds[3], (HEADS,), ((0, 8),), -0.2, 0.2)), 0.003, 0.06),
        "query_weight": bell_draw(seeds[4], (D, D), D ** -0.5, 0.125, ((0, 4), (1, 8))),
        "key_weight": bell_draw(seeds[5], (D, D), D ** -0.5, 0.125, ((0, 4), (1, 8))),
        "value_weight": bell_draw(seeds[6], (D, D), D ** -0.5, 0.125, ((0, 4), (1, 8))),
        "gate_weight": bell_draw(seeds[7], (D, D), D ** -0.5, 0.125, ((0, 4), (1, 8))),
        "out_weight": bell_draw(seeds[8], (D, D), (D // 4) ** -0.5, 0.25, ((0, 8), (1, 4))),
        "first_weight": bell_draw(seeds[9], (D, FF), D ** -0.5, 0.125, ((0, 4), (1, 8))),
        "second_weight": bell_draw(seeds[10], (D, FF), D ** -0.5, 0.125, ((0, 4), (1, 8))),
        "down_weight": bell_draw(seeds[11], (FF, D), FF ** -0.5, 0.078125, ((0, 8), (1, 4))),
    }


EPSILON = 1e-06
HIGHEST = lax.Precision.HIGHEST

@jax.custom_vjp
def low(v):
    return lax.optimization_barrier(v.astype(jnp.bfloat16)).astype(jnp.float32)

@jax.custom_vjp
def low_back(v):
    return v

def low_keep(v):
    return (low(v), None)

def low_pass(kept, grad):
    return (grad,)

def back_keep(v):
    return (v, None)

def back_low(kept, grad):
    return (low(grad),)
low.defvjp(low_keep, low_pass)
low_back.defvjp(back_keep, back_low)

def product(left_side, right_side):
    return jnp.dot(left_side, right_side, precision=HIGHEST, preferred_element_type=jnp.float32)

def rms_scaled(values):
    return values * lax.rsqrt(lax.optimization_barrier(jnp.mean(values * values, axis=-1, keepdims=True)) + EPSILON)

def split_heads(array):
    return array.reshape(TOK_DEV, HEADS, HEAD).transpose(1, 0, 2)

def layer_group(inputs, weight_list, group_lengths, decay_rate):
    query_weight, key_weight, value_weight, gate_weight, out_weight, first_weight, second_weight, down_weight = weight_list
    normed = low(rms_scaled(inputs))
    pre_query = low_back(product(normed, query_weight))
    pre_key = low_back(product(normed, key_weight))
    pre_value = low_back(product(normed, value_weight))
    pre_gate = low_back(product(normed, gate_weight))
    queries = low(jax.nn.silu(pre_query))
    keys = low(jax.nn.silu(pre_key))
    values = low(jax.nn.silu(pre_value))
    places = jnp.arange(TOK_DEV, dtype=jnp.int32)
    bounds = jnp.cumsum(group_lengths)
    member = lax.optimization_barrier(jnp.sum((places[:, None] >= bounds[None, :]).astype(jnp.int32), axis=1))
    distance = (places[:, None] - places[None, :]).astype(jnp.float32)
    allowed = (member[:, None] == member[None, :]) & (distance >= 0)

    def one_head(operands):
        head_query, head_key, head_value, head_rate = operands
        scores = low_back(product(head_query, head_key.T))
        weights = jnp.where(allowed, jnp.exp(-head_rate * jnp.maximum(distance, 0.0)), 0.0)
        score_mix = low(scores * weights)
        return low_back(product(score_mix, head_value))
    per_head = lax.map(jax.checkpoint(one_head), (split_heads(queries), split_heads(keys), split_heads(values), decay_rate))
    attended = per_head.transpose(1, 0, 2).reshape(TOK_DEV, D)
    gated = low(rms_scaled(attended) * jax.nn.sigmoid(pre_gate))
    branch = low_back(product(gated, out_weight))
    middle = inputs + branch
    normed_two = low(rms_scaled(low(middle)))
    first_act = low_back(product(normed_two, first_weight))
    second_act = low_back(product(normed_two, second_weight))
    hidden = low(first_act * second_act)
    return middle + low_back(product(hidden, down_weight))

def reference(tokens, cotangent, lengths, decay_rate, query_weight, key_weight, value_weight, gate_weight, out_weight, first_weight, second_weight, down_weight):
    matrices = (query_weight.astype(jnp.float32), key_weight.astype(jnp.float32), value_weight.astype(jnp.float32), gate_weight.astype(jnp.float32), out_weight.astype(jnp.float32), first_weight.astype(jnp.float32), second_weight.astype(jnp.float32), down_weight.astype(jnp.float32))
    inputs_all = tokens.astype(jnp.float32).reshape(N_ROWS, TOK_DEV, D)
    cot_all = cotangent.astype(jnp.float32).reshape(N_ROWS, TOK_DEV, D)
    rates = decay_rate.astype(jnp.float32)

    def group_step(running, slices):
        group_inputs, group_cot, group_lengths = slices

        def forward(inputs, *weight_list):
            return layer_group(inputs, weight_list, group_lengths, rates)
        result, pullback = jax.vjp(forward, group_inputs, *matrices)
        gradients = pullback(group_cot)
        updated = tuple((before + update for before, update in zip(running, gradients[1:])))
        return (updated, (result, gradients[0]))
    zeros_start = tuple((jnp.zeros(matrix.shape, jnp.float32) for matrix in matrices))
    sums, (outputs, input_grads) = lax.scan(group_step, zeros_start, (inputs_all, cot_all, lengths))
    layer_out = outputs.reshape(TOKENS, D).astype(jnp.bfloat16)
    token_grad = input_grads.reshape(TOKENS, D)
    return (layer_out, token_grad, sums[0], sums[1], sums[2], sums[3], sums[4], sums[5], sums[6], sums[7])
```

```python
import jax
import jax.numpy as jnp
from jax import lax
from jax.sharding import PartitionSpec as P

HEAD = 128
LEN_CAP = 1024


EPSILON = 1e-06


def rms_scaled(values):
    inverse_rms = lax.rsqrt(jnp.mean(values * values, axis=-1, keepdims=True) + EPSILON)
    return (values * inverse_rms, inverse_rms)


def contract_rows(left_side, right_side):
    return lax.dot_general(
        left_side, right_side, (((0,), (0,)), ((), ())), preferred_element_type=jnp.float32
    )


def contract_cols(left_side, right_side):
    return lax.dot_general(
        left_side, right_side, (((1,), (1,)), ((), ())), preferred_element_type=jnp.float32
    )


def silu_slope(values):
    sigmoid_of = jax.nn.sigmoid(values)
    return sigmoid_of * (1.0 + values * (1.0 - sigmoid_of))


def decay_block(first_row, block_rows, key_start, key_rows, member, decay_rates):
    key_places = key_start + jnp.arange(key_rows, dtype=jnp.int32)
    rows_here = first_row + jnp.arange(block_rows, dtype=jnp.int32)
    distance = (rows_here[:, None] - key_places[None, :]).astype(jnp.float32)
    allowed = (member[:, None] == member[None, :]) & (distance >= 0)
    return jnp.where(
        allowed[None], jnp.exp(-decay_rates[:, None, None] * jnp.maximum(distance, 0.0)[None]), 0.0
    )


def shards(
    tokens,
    cotangent,
    lengths,
    decay_rate,
    query_weight,
    key_weight,
    value_weight,
    gate_weight,
    out_weight,
    first_weight,
    second_weight,
    down_weight,
):
    gathered, grad_rows = (
        lax.all_gather(tokens, "cols", axis=1, tiled=True),
        lax.all_gather(cotangent, "cols", axis=1, tiled=True),
    )
    full_weights = (
        lax.all_gather(query_weight, "rows", axis=0, tiled=True),
        lax.all_gather(key_weight, "rows", axis=0, tiled=True),
        lax.all_gather(value_weight, "rows", axis=0, tiled=True),
        lax.all_gather(gate_weight, "rows", axis=0, tiled=True),
        lax.all_gather(out_weight, "rows", axis=1, tiled=True),
        lax.all_gather(first_weight, "rows", axis=0, tiled=True),
        lax.all_gather(second_weight, "rows", axis=0, tiled=True),
        lax.all_gather(down_weight, "rows", axis=1, tiled=True),
    )
    query_full, key_full, value_full, gate_full, out_full, first_full, second_full, down_full = (
        full_weights
    )
    token_count, model_width = gathered.shape
    local_width = tokens.shape[1]
    head_width = query_full.shape[1]
    local_heads = head_width // HEAD
    hidden_local = first_full.shape[1]
    column_start = lax.axis_index("cols") * local_width

    def to_heads(array):
        return array.reshape(token_count, local_heads, HEAD)

    inputs_full = gathered.astype(jnp.float32)
    normed, inverse_first = rms_scaled(inputs_full)
    normed_low = normed.astype(jnp.bfloat16)
    proj_weights = jnp.concatenate((query_full, key_full, value_full, gate_full), axis=1)
    projected = jnp.dot(normed_low, proj_weights, preferred_element_type=jnp.float32)
    pre_query = projected[:, :head_width]
    pre_key = projected[:, head_width : 2 * head_width]
    pre_value = projected[:, 2 * head_width : 3 * head_width]
    pre_gate = projected[:, 3 * head_width :]
    queries = to_heads(jax.nn.silu(pre_query).astype(jnp.bfloat16))
    keys = to_heads(jax.nn.silu(pre_key).astype(jnp.bfloat16))
    values = to_heads(jax.nn.silu(pre_value).astype(jnp.bfloat16))
    sequence_places = jnp.arange(lengths.shape[1], dtype=jnp.int32)
    bounds = jnp.sum(
        jnp.where(sequence_places[None, :] <= sequence_places[:, None], lengths[0][None, :], 0), axis=1
    )
    places = jnp.arange(token_count, dtype=jnp.int32)
    member = jnp.sum((places[:, None] >= bounds[None, :]).astype(jnp.int32), axis=1)
    block_rows = min(512, token_count)
    window = min(token_count, block_rows + min(LEN_CAP, token_count // 2))
    block_starts = jnp.arange(token_count // block_rows, dtype=jnp.int32) * block_rows

    def window_start(first_row):
        return jnp.maximum(first_row + block_rows - window, 0)

    def attend(first_row):
        key_start = window_start(first_row)
        weights = decay_block(first_row, block_rows, key_start, window, member, decay_rate)
        scores = jnp.einsum("qhd,khd->hqk", queries, keys, preferred_element_type=jnp.float32)
        score_mix = (scores * weights).astype(jnp.bfloat16)
        return jnp.einsum("hqk,khd->qhd", score_mix, values, preferred_element_type=jnp.float32)

    attended = lax.map(attend, block_starts).reshape(token_count, head_width)
    square_sums = lax.psum(jnp.sum(attended * attended, axis=1), "cols")
    inverse_attn = lax.rsqrt(square_sums / model_width + EPSILON)[:, None]
    attn_normed = attended * inverse_attn
    gate_value = jax.nn.sigmoid(pre_gate)
    gated_low = (attn_normed * gate_value).astype(jnp.bfloat16)
    partial_attn = jnp.dot(gated_low, out_full, preferred_element_type=jnp.float32)
    branch = lax.psum_scatter(partial_attn, "cols", scatter_dimension=1, tiled=True)
    middle = tokens.astype(jnp.float32) + branch
    middle_low = lax.all_gather(middle.astype(jnp.bfloat16), "cols", axis=1, tiled=True)
    normed_two, inverse_second = rms_scaled(middle_low.astype(jnp.float32))
    normed_two_low = normed_two.astype(jnp.bfloat16)
    pair_weights = jnp.concatenate((first_full, second_full), axis=1)
    pair = jnp.dot(normed_two_low, pair_weights, preferred_element_type=jnp.float32)
    first_act = pair[:, :hidden_local]
    second_act = pair[:, hidden_local:]
    hidden_low = (first_act * second_act).astype(jnp.bfloat16)
    ffn_out = lax.psum_scatter(
        jnp.dot(hidden_low, down_full, preferred_element_type=jnp.float32),
        "cols",
        scatter_dimension=1,
        tiled=True,
    )
    layer_out = (middle + ffn_out).astype(jnp.bfloat16)
    hidden_grad = contract_cols(grad_rows, down_full)
    down_grad = contract_rows(hidden_low, grad_rows)
    first_low = (hidden_grad * second_act).astype(jnp.bfloat16)
    second_low = (hidden_grad * first_act).astype(jnp.bfloat16)
    pair_grad = jnp.concatenate((first_low, second_low), axis=1)
    pair_weight_grad = contract_rows(normed_two_low, pair_grad)
    normed_two_grad = lax.psum_scatter(
        contract_cols(pair_grad, pair_weights), "cols", scatter_dimension=1, tiled=True
    )
    normed_two_here = lax.dynamic_slice_in_dim(normed_two, column_start, local_width, 1)
    second_stat = lax.psum(jnp.sum(normed_two_grad * normed_two_here, axis=1), "cols")
    middle_grad = cotangent.astype(jnp.float32) + inverse_second * (
        normed_two_grad - normed_two_here * (second_stat / model_width)[:, None]
    )
    branch_rows = lax.all_gather(middle_grad.astype(jnp.bfloat16), "cols", axis=1, tiled=True)
    gated_grad = contract_cols(branch_rows, out_full)
    out_grad = contract_rows(gated_low, branch_rows)
    normed_attn_grad = gated_grad * gate_value
    pre_gate_grad = gated_grad * attn_normed * gate_value * (1.0 - gate_value)
    first_stat = lax.psum(jnp.sum(normed_attn_grad * attn_normed, axis=1), "cols")
    attended_grad = inverse_attn * (
        normed_attn_grad - attn_normed * (first_stat / model_width)[:, None]
    )
    attended_low = to_heads(attended_grad.astype(jnp.bfloat16))

    def attend_back(carry, first_row):
        key_sum, value_sum = carry
        key_start = window_start(first_row)
        weights = decay_block(first_row, block_rows, key_start, window, member, decay_rate)
        scores = jnp.einsum("qhd,khd->hqk", queries, keys, preferred_element_type=jnp.float32)
        score_mix = (scores * weights).astype(jnp.bfloat16)
        score_grad = jnp.einsum(
            "qhd,khd->hqk", attended_low, values, preferred_element_type=jnp.float32
        )
        raw_grad = (score_grad * weights).astype(jnp.bfloat16)
        query_part = jnp.einsum("hqk,khd->qhd", raw_grad, keys, preferred_element_type=jnp.float32)
        key_part = jnp.einsum("hqk,qhd->khd", raw_grad, queries, preferred_element_type=jnp.float32)
        value_part = jnp.einsum(
            "hqk,qhd->khd", score_mix, attended_low, preferred_element_type=jnp.float32
        )
        key_sum = key_sum + key_part
        value_sum = value_sum + value_part
        return ((key_sum, value_sum), query_part)

    zero_heads = jnp.zeros((token_count, local_heads, HEAD), jnp.float32)
    (key_total, value_total), query_parts = lax.scan(
        attend_back, (zero_heads, zero_heads), block_starts
    )
    query_total = query_parts.reshape(token_count, head_width)
    key_flat = key_total.reshape(token_count, head_width)
    value_flat = value_total.reshape(token_count, head_width)
    proj_grad = jnp.concatenate(
        (
            (query_total * silu_slope(pre_query)).astype(jnp.bfloat16),
            (key_flat * silu_slope(pre_key)).astype(jnp.bfloat16),
            (value_flat * silu_slope(pre_value)).astype(jnp.bfloat16),
            pre_gate_grad.astype(jnp.bfloat16),
        ),
        axis=1,
    )
    proj_weight_grad = contract_rows(normed_low, proj_grad)
    normed_grad = lax.psum_scatter(
        contract_cols(proj_grad, proj_weights), "cols", scatter_dimension=1, tiled=True
    )
    normed_here = lax.dynamic_slice_in_dim(normed, column_start, local_width, 1)
    zero_stat = lax.psum(jnp.sum(normed_grad * normed_here, axis=1), "cols")
    token_grad = middle_grad + inverse_first * (
        normed_grad - normed_here * (zero_stat / model_width)[:, None]
    )
    summed = (
        lax.psum_scatter(proj_weight_grad[:, :head_width], "rows", scatter_dimension=0, tiled=True),
        lax.psum_scatter(
            proj_weight_grad[:, head_width : 2 * head_width],
            "rows",
            scatter_dimension=0,
            tiled=True,
        ),
        lax.psum_scatter(
            proj_weight_grad[:, 2 * head_width : 3 * head_width],
            "rows",
            scatter_dimension=0,
            tiled=True,
        ),
        lax.psum_scatter(
            proj_weight_grad[:, 3 * head_width :], "rows", scatter_dimension=0, tiled=True
        ),
        lax.psum_scatter(out_grad, "rows", scatter_dimension=1, tiled=True),
        lax.psum_scatter(
            pair_weight_grad[:, :hidden_local], "rows", scatter_dimension=0, tiled=True
        ),
        lax.psum_scatter(
            pair_weight_grad[:, hidden_local:], "rows", scatter_dimension=0, tiled=True
        ),
        lax.psum_scatter(down_grad, "rows", scatter_dimension=1, tiled=True),
    )
    return (
        layer_out,
        token_grad,
        summed[0],
        summed[1],
        summed[2],
        summed[3],
        summed[4],
        summed[5],
        summed[6],
        summed[7],
    )


def solution(mesh):
    placed = (
        P("rows", "cols"),
        P("rows", "cols"),
        P("rows", None),
        P("cols"),
        P("rows", "cols"),
        P("rows", "cols"),
        P("rows", "cols"),
        P("rows", "cols"),
        P("cols", "rows"),
        P("rows", "cols"),
        P("rows", "cols"),
        P("cols", "rows"),
    )
    return jax.shard_map(
        shards,
        mesh=mesh,
        in_specs=placed,
        out_specs=(
            P("rows", "cols"),
            P("rows", "cols"),
            P("rows", "cols"),
            P("rows", "cols"),
            P("rows", "cols"),
            P("rows", "cols"),
            P("cols", "rows"),
            P("rows", "cols"),
            P("rows", "cols"),
            P("cols", "rows"),
        ),
        check_vma=False,
    )
```

```python
import functools

import jax
import jax.numpy as jnp
import numpy as np
from jax import lax
from jax.experimental import pallas as pl
from jax.experimental.pallas import tpu as pltpu
from jax.sharding import PartitionSpec as P

HEAD = 128
EPSILON = 1e-06
F32, BF16 = jnp.float32, jnp.bfloat16
NN, NT, TN = ((1,), (0,)), ((1,), (1,)), ((0,), (0,))
ANY = pl.BlockSpec(memory_space=pl.ANY)
VMEM = pl.BlockSpec(memory_space=pltpu.VMEM)
SMEM = pl.BlockSpec(memory_space=pltpu.SMEM)
MIB = 1 << 20


def dot(left, right, dims):
    return lax.dot_general(left, right, (dims, ((), ())), preferred_element_type=F32)


def silu_slope(values):
    sigmoid_of = jax.nn.sigmoid(values)
    return sigmoid_of * (1.0 + values * (1.0 - sigmoid_of))


def to_row(column):
    return jnp.broadcast_to(column, (column.shape[0], 128)).T[:8]


def to_column(row):
    return jnp.broadcast_to(row[:1], (128, row.shape[1])).T[:, :1]


def tiles(size, step=256):
    return [(at, min(step, size - at)) for at in range(0, size, step)]


def fetch(sources, target, axis, places, semaphores):
    copies = []
    for i, source in enumerate(sources):
        size = source.shape[axis]
        where = pl.ds(pl.multiple_of(places[i] * size, size), size)
        spot = target.at[:, where] if axis else target.at[where]
        copies.append(pltpu.make_async_copy(source, spot, semaphores.at[i]))
        copies[-1].start()
    return copies


def landed(copies):
    for copy in copies:
        copy.wait()


def normalize(array, inverse_out, step=32):
    def some(i, carry):
        rows = pl.ds(pl.multiple_of(i * step, step), step)
        values = array[rows, :].astype(F32)
        inverse = lax.rsqrt(jnp.mean(values * values, axis=1, keepdims=True) + EPSILON)
        array[rows, :] = (values * inverse).astype(BF16)
        inverse_out[rows, :] = jnp.broadcast_to(inverse, (step, inverse_out.shape[1]))
        return carry

    lax.fori_loop(0, array.shape[0] // step, some, 0)


def split_blocks(array, row_places, keep, send):
    block = keep.shape[1] // (len(row_places) // 2)
    for dy in range(len(row_places) // 2):
        for dc, out in ((0, keep), (1, send)):
            at = pl.ds(pl.multiple_of(row_places[dy * 2 + dc] * block, block), block)
            out[:, dy * block : (dy + 1) * block] = array[:, at]


def decay(first, rows, keys, bounds, count, rate):
    t = first + lax.broadcasted_iota(jnp.int32, (rows, keys), 0)
    s = lax.broadcasted_iota(jnp.int32, (rows, keys), 1)
    start = jnp.zeros((rows, keys), jnp.int32)
    for i in range(count):
        start = jnp.where(t >= bounds[i], bounds[i], start)
    distance = (t - s).astype(F32)
    allowed = (s >= start) & (s <= t)
    return jnp.where(allowed, jnp.exp(-rate * jnp.maximum(distance, 0.0)), 0.0)


def front_kernel(n, r, count, idx, bounds, rate, *refs):
    x, wp, wo = refs[:n], refs[n : n + r], refs[n + r : n + 2 * r]
    refs = refs[n + 2 * r :]
    keep, send, inverse, pre, qkv, attended, squares, gate_low = refs[:8]
    parts, (full, w_full, wo_full, sx, sw, so) = refs[8 : 8 + n], refs[8 + n :]
    col_places = [idx[i] for i in range(n)]
    row_places = [idx[n + j] for j in range(r)]
    token_count = full.shape[0]
    width = wo_full.shape[0]
    copies_x = fetch(x, full, 1, col_places, sx)
    copies_w = fetch(wp, w_full, 0, row_places, sw)
    copies_o = fetch(wo, wo_full, 1, row_places, so)
    landed(copies_x)
    normalize(full, inverse)
    landed(copies_w)
    for part in range(4):
        at = slice(part * width, (part + 1) * width)
        values = dot(full[...], w_full[:, at], NN)
        pre[:, at] = values
        if part < 3:
            qkv[:, at] = (values * jax.nn.sigmoid(values)).astype(BF16)
    block = min(256, token_count)
    for head in range(width // HEAD):
        q, k, v = (slice(p * width + head * HEAD, p * width + (head + 1) * HEAD) for p in range(3))
        for first in range(0, token_count, block):
            keys = first + block
            weights = decay(first, block, keys, bounds, count, rate[head])
            scores = dot(qkv[first:keys, q], qkv[:keys, k], NT)
            mix = (scores * weights).astype(BF16)
            attended[first:keys, head * HEAD : (head + 1) * HEAD] = dot(mix, qkv[:keys, v], NN)
    values = attended[...]
    squares[...] = to_row(jnp.sum(values * values, axis=1, keepdims=True))
    gate_low[...] = (values * jax.nn.sigmoid(pre[:, 3 * width :])).astype(BF16)
    landed(copies_o)
    for i in range(n):
        at = pl.ds(pl.multiple_of(col_places[i] * width, width), width)
        parts[i][...] = dot(gate_low[...], wo_full[:, at], NN).astype(parts[i].dtype)
    split_blocks(full, row_places, keep, send)


def middle_kernel(model_width, tokens, squares, own, forward, backward, middle, middle_low):
    inverse = to_column(lax.rsqrt(squares[...] / model_width + EPSILON))
    total = own[...] + forward[...].astype(F32) + backward[...].astype(F32)
    value = tokens[...].astype(F32) + total * inverse
    middle[...] = value
    middle_low[...] = value.astype(BF16)


def ffn_kernel(n, r, idx, *refs):
    m, dy = refs[:n], refs[n : 2 * n]
    w1, w2, wd = (refs[2 * n + j * r : 2 * n + (j + 1) * r] for j in range(3))
    refs = refs[2 * n + 3 * r :]
    m_keep, m_send, dy_keep, dy_send, inverse, hidden, low1, low2, stat = refs[:9]
    parts, scratch = refs[9 : 9 + n], refs[9 + n :]
    m_full, dy_full, w1_full, w2_full, wd_full, sm, sd, s1, s2, s3 = scratch
    col_places = [idx[i] for i in range(n)]
    row_places = [idx[n + j] for j in range(r)]
    width = m[0].shape[1]
    copies_m = fetch(m, m_full, 1, col_places, sm)
    copies_1 = fetch(w1, w1_full, 0, row_places, s1)
    copies_2 = fetch(w2, w2_full, 0, row_places, s2)
    copies_y = fetch(dy, dy_full, 1, col_places, sd)
    copies_d = fetch(wd, wd_full, 1, row_places, s3)
    landed(copies_m)
    normalize(m_full, inverse)
    landed(copies_1)
    landed(copies_2)
    landed(copies_y)
    landed(copies_d)
    total = None
    for first, size in tiles(hidden.shape[1]):
        at = slice(first, first + size)
        act1 = dot(m_full[...], w1_full[:, at], NN)
        act2 = dot(m_full[...], w2_full[:, at], NN)
        grad = dot(dy_full[...], wd_full[at, :], NT)
        product = act1 * act2
        hidden[:, at] = product.astype(BF16)
        low1[:, at] = (grad * act2).astype(BF16)
        low2[:, at] = (grad * act1).astype(BF16)
        part = jnp.sum(grad * product, axis=1, keepdims=True)
        total = part if total is None else total + part
    stat[...] = to_row(2.0 * total)
    for i in range(n):
        at = pl.ds(pl.multiple_of(col_places[i] * width, width), width)
        value = dot(low1[...], w1_full[at, :], NT) + dot(low2[...], w2_full[at, :], NT)
        parts[i][...] = value.astype(parts[i].dtype)
    split_blocks(m_full, row_places, m_keep, m_send)
    split_blocks(dy_full, row_places, dy_keep, dy_send)


def down_kernel(n, r, idx, hidden, *refs):
    wd, parts, (wd_full, sem) = refs[:r], refs[r : r + n], refs[r + n :]
    landed(fetch(wd, wd_full, 1, [idx[n + j] for j in range(r)], sem))
    width = parts[0].shape[1]
    for i in range(n):
        at = pl.ds(pl.multiple_of(idx[i] * width, width), width)
        parts[i][...] = dot(hidden[...], wd_full[:, at], NN).astype(parts[i].dtype)


def middle_grad_kernel(
    model_width, cotangent, tokens, middle, middle_low, inverse, stat, own, forward, backward, grad, grad_low, next_stat
):
    inverse_two = inverse[:, :1]
    mean = to_column(stat[...] / model_width)
    normed = middle_low[...].astype(F32) * inverse_two
    total = own[...] + forward[...].astype(F32) + backward[...].astype(F32)
    value = cotangent[...].astype(F32) + inverse_two * (total - normed * mean)
    low = value.astype(BF16)
    grad[...] = value
    grad_low[...] = low
    branch = middle[...] - tokens[...].astype(F32)
    next_stat[...] = to_row(jnp.sum(low.astype(F32) * branch, axis=1, keepdims=True))


def back_kernel(n, r, count, model_width, idx, bounds, rate, pre, qkv, attended, squares, stat, *refs):
    br, wo, wp = refs[:n], refs[n : n + r], refs[n + r : n + 2 * r]
    refs = refs[n + 2 * r :]
    keep, send, proj, gated, next_stat = refs[:5]
    parts, scratch = refs[5 : 5 + n], refs[5 + n :]
    full, wo_full, w_full, att_low, key_sum, value_sum, sb, so, sw = scratch
    col_places = [idx[i] for i in range(n)]
    row_places = [idx[n + j] for j in range(r)]
    token_count = full.shape[0]
    width = wo_full.shape[0]
    copies_b = fetch(br, full, 1, col_places, sb)
    copies_o = fetch(wo, wo_full, 1, row_places, so)
    copies_w = fetch(wp, w_full, 0, row_places, sw)
    landed(copies_b)
    landed(copies_o)
    gated_grad = dot(full[...], wo_full[...], NT)
    inverse = to_column(lax.rsqrt(squares[...] / model_width + EPSILON))
    mean = to_column(stat[...] / model_width)
    pre_gate = pre[:, 3 * width :]
    gate = jax.nn.sigmoid(pre_gate)
    normed = attended[...] * inverse
    gated[...] = (normed * gate).astype(BF16)
    inner = gated_grad * gate
    gate_grad = inner * normed * (1.0 - gate)
    proj[:, 3 * width :] = gate_grad.astype(BF16)
    att_low[...] = (inverse * (inner - normed * mean)).astype(BF16)
    total = jnp.sum(gate_grad * pre_gate, axis=1, keepdims=True)
    next_stat[...] = to_row(total)
    block = min(256, token_count)
    for head in range(width // HEAD):
        here = slice(head * HEAD, (head + 1) * HEAD)
        q, k, v = (slice(p * width + head * HEAD, p * width + (head + 1) * HEAD) for p in range(3))
        key_sum[...] = jnp.zeros_like(key_sum)
        value_sum[...] = jnp.zeros_like(value_sum)
        for first in range(0, token_count, block):
            keys = first + block
            rows = slice(first, keys)
            weights = decay(first, block, keys, bounds, count, rate[head])
            scores = dot(qkv[rows, q], qkv[:keys, k], NT)
            mix = (scores * weights).astype(BF16)
            score_grad = dot(att_low[rows, here], qkv[:keys, v], NT)
            raw = (score_grad * weights).astype(BF16)
            query_sum = dot(raw, qkv[:keys, k], NN)
            values = pre[rows, q]
            proj[rows, q] = (query_sum * silu_slope(values)).astype(BF16)
            key_sum[:keys] += dot(raw, qkv[rows, q], TN)
            value_sum[:keys] += dot(mix, att_low[rows, here], TN)
        proj[:, k] = (key_sum[...] * silu_slope(pre[:, k])).astype(BF16)
        proj[:, v] = (value_sum[...] * silu_slope(pre[:, v])).astype(BF16)
    for part in range(3):
        at = slice(part * width, (part + 1) * width)
        total = total + jnp.sum(proj[:, at].astype(F32) * pre[:, at], axis=1, keepdims=True)
    next_stat[...] = to_row(total)
    landed(copies_w)
    for i in range(n):
        at = pl.ds(pl.multiple_of(col_places[i] * width, width), width)
        parts[i][...] = dot(proj[...], w_full[at, :], NT).astype(parts[i].dtype)
    split_blocks(full, row_places, keep, send)


def token_grad_kernel(model_width, middle_grad, tokens, inverse, stat, own, forward, backward, out):
    inverse_first = inverse[:, :1]
    mean = to_column(stat[...] / model_width)
    normed = tokens[...].astype(F32) * inverse_first
    total = own[...] + forward[...].astype(F32) + backward[...].astype(F32)
    out[...] = middle_grad[...] + inverse_first * (total - normed * mean)


def weight_grad_kernel(y_size, pairs, flipped, act, act_other, *refs):
    lows, others, outs = refs[:pairs], refs[pairs : 2 * pairs], refs[2 * pairs :]
    block = act.shape[1] // y_size
    for p in range(pairs):
        for dy in range(y_size):
            at = slice(dy * block, (dy + 1) * block)
            out = outs[p * y_size + dy]
            if flipped:
                for first, size in tiles(block):
                    here = slice(at.start + first, at.start + first + size)
                    value = dot(lows[p][...], act[:, here], TN) + dot(others[p][...], act_other[:, here], TN)
                    out[:, first : first + size] = value.astype(out.dtype)
            else:
                for first, size in tiles(lows[p].shape[1]):
                    here = slice(first, first + size)
                    value = dot(act[:, at], lows[p][:, here], TN) + dot(act_other[:, at], others[p][:, here], TN)
                    out[:, here] = value.astype(out.dtype)


def ring_order(mesh):
    n = mesh.shape["cols"]
    plain = list(range(n))
    try:
        devices = np.moveaxis(mesh.devices, mesh.axis_names.index("cols"), -1)
        devices = devices.reshape(-1, n)[0]
        coords = [tuple(d.coords) for d in devices]
    except (AttributeError, TypeError):
        return plain
    varying = [d for d in range(len(coords[0])) if len({c[d] for c in coords}) > 1]
    if len(varying) != 2:
        return plain
    a, b = varying
    sizes = [len({c[d] for c in coords}) for d in (a, b)]
    if sizes[0] % 2:
        a, b, sizes = b, a, sizes[::-1]
    if sizes[0] % 2 or sizes[0] * sizes[1] != n or sizes[1] < 2:
        return plain
    lows = [min(c[d] for c in coords) for d in (a, b)]
    index = {(c[a] - lows[0], c[b] - lows[1]): i for i, c in enumerate(coords)}
    walk = []
    for i in range(sizes[0]):
        across = range(1, sizes[1])
        walk += [(i, j) for j in (across if i % 2 == 0 else reversed(across))]
    walk += [(i, 0) for i in reversed(range(sizes[0]))]
    if set(walk) != set(index):
        return plain
    return [index[spot] for spot in walk]


def call(kernel, outs, scratch, limit, flops, moved, *args):
    specs = [spec for spec, _ in args]
    return pl.pallas_call(
        kernel,
        out_shape=[jax.ShapeDtypeStruct(s, t) for s, t in outs],
        in_specs=specs,
        out_specs=[VMEM] * len(outs),
        scratch_shapes=scratch,
        compiler_params=pltpu.CompilerParams(vmem_limit_bytes=limit),
        cost_estimate=pl.CostEstimate(flops=int(flops), bytes_accessed=int(moved), transcendentals=0),
    )(*[arg for _, arg in args])


def each(spec, arrays):
    return [(spec, a) for a in arrays]


def shards(cycle, y_size, *args):
    (
        tokens,
        cotangent,
        lengths,
        decay_rate,
        query_weight,
        key_weight,
        value_weight,
        gate_weight,
        out_weight,
        first_weight,
        second_weight,
        down_weight,
    ) = args
    n, r = len(cycle), 2 * y_size
    half = n // 2
    token_count, width = tokens.shape
    model_width = width * n
    block = query_weight.shape[0]
    hidden_width = first_weight.shape[1]
    count = lengths.shape[1]
    dma = pltpu.SemaphoreType.DMA

    ahead = [(cycle[i], cycle[(i + 1) % n]) for i in range(n)]
    back = [(b, a) for a, b in ahead]
    core_swap = [(i, i ^ 1) for i in range(r)]

    def y_shift(by):
        return [(y * 2 + c, (y + by) % y_size * 2 + c) for y in range(y_size) for c in range(2)]

    place = {c: i for i, c in enumerate(cycle)}
    col_table = np.array([[cycle[(place[c] + i) % n] for i in range(n)] for c in range(n)], np.int32)
    row_table = np.array(
        [[((q // 2 + j // 2) % y_size) * 2 + ((q % 2) ^ (j % 2)) for j in range(r)] for q in range(r)], np.int32
    )
    idx = jnp.concatenate(
        [
            lax.dynamic_index_in_dim(jnp.asarray(col_table), lax.axis_index("cols"), 0, False),
            lax.dynamic_index_in_dim(jnp.asarray(row_table), lax.axis_index("rows"), 0, False),
        ]
    )
    places = jnp.arange(count, dtype=jnp.int32)
    bounds = jnp.sum(jnp.where(places[None, :] <= places[:, None], lengths[0][None, :], 0), axis=1)

    def ring_gather(array):
        parts = [array] + [None] * (n - 1)
        forward = backward = array
        for k in range(1, half + 1):
            forward = lax.ppermute(forward, "cols", ahead)
            parts[n - k] = forward
            if k < n - half:
                backward = lax.ppermute(backward, "cols", back)
                parts[k] = backward
        return parts

    def add(a, b):
        return (a.astype(F32) + b.astype(F32)).astype(BF16)

    def ring_scatter(parts):
        forward, backward = parts[half], parts[half + 1]
        for k in range(half):
            forward = lax.ppermute(forward, "cols", ahead)
            if half - 1 - k > 0:
                forward = add(forward, parts[half - 1 - k])
            if k < half - 1:
                backward = lax.ppermute(backward, "cols", back)
                if half + 2 + k < n:
                    backward = add(backward, parts[half + 2 + k])
        return parts[0], forward, backward

    def sum_over_cols(stat):
        by = 1
        while by < n:
            stat = stat + lax.ppermute(stat, "cols", [(i, i ^ by) for i in range(n)])
            by *= 2
        return stat

    def rows_gather(array):
        column = [array] + [lax.ppermute(array, "rows", y_shift(-dy)) for dy in range(1, y_size)]
        blocks = []
        for a in column:
            blocks += [a, lax.ppermute(a, "rows", core_swap)]
        return blocks

    def swap(array):
        return lax.ppermute(array, "rows", core_swap)

    def y_sum(outs):
        total = outs[0]
        for dy in range(1, y_size):
            total = total + lax.ppermute(outs[dy], "rows", y_shift(dy)).astype(F32)
        return total

    proj_weight = jnp.concatenate((query_weight, key_weight, value_weight, gate_weight), axis=1)
    proj_blocks = rows_gather(proj_weight)
    token_parts = ring_gather(tokens)
    out_blocks = rows_gather(out_weight)
    first_blocks = rows_gather(first_weight)
    second_blocks = rows_gather(second_weight)
    down_blocks = rows_gather(down_weight)
    grad_parts = ring_gather(cotangent)

    token_half = (token_count, model_width // 2)
    local = (token_count, width)
    row = (8, token_count)
    part_shapes = [(local, F32)] + [(local, BF16)] * (n - 1)
    full_shape = (token_count, model_width)

    normed_keep, normed_send, inverse_first, pre, qkv, attended, squares, gate_low, *partial = call(
        functools.partial(front_kernel, n, r, count),
        [
            (token_half, BF16),
            (token_half, BF16),
            ((token_count, 128), F32),
            ((token_count, 4 * width), F32),
            ((token_count, 3 * width), BF16),
            (local, F32),
            (row, F32),
            (local, BF16),
            *part_shapes,
        ],
        [
            pltpu.VMEM(full_shape, BF16),
            pltpu.VMEM((model_width, 4 * width), BF16),
            pltpu.VMEM((width, model_width), BF16),
            dma((n,)),
            dma((r,)),
            dma((r,)),
        ],
        40 * MIB,
        2 * token_count * model_width * width * 5,
        16 * MIB,
        (SMEM, idx),
        (SMEM, bounds),
        (SMEM, decay_rate),
        *each(ANY, token_parts),
        *each(ANY, proj_blocks),
        *each(ANY, out_blocks),
    )
    squares = sum_over_cols(squares)
    own, forward, backward = ring_scatter(partial)
    middle, middle_low = call(
        functools.partial(middle_kernel, model_width),
        [(local, F32), (local, BF16)],
        [],
        16 * MIB,
        0,
        3 * MIB,
        *each(VMEM, (tokens, squares, own, forward, backward)),
    )
    middle_parts = ring_gather(middle_low)
    wide = (token_count, hidden_width)
    m_keep, m_send, dy_keep, dy_send, inverse_second, hidden, low1, low2, second_stat, *partial = call(
        functools.partial(ffn_kernel, n, r),
        [
            (token_half, BF16),
            (token_half, BF16),
            (token_half, BF16),
            (token_half, BF16),
            ((token_count, 128), F32),
            (wide, BF16),
            (wide, BF16),
            (wide, BF16),
            (row, F32),
            *part_shapes,
        ],
        [
            pltpu.VMEM(full_shape, BF16),
            pltpu.VMEM(full_shape, BF16),
            pltpu.VMEM((model_width, hidden_width), BF16),
            pltpu.VMEM((model_width, hidden_width), BF16),
            pltpu.VMEM((hidden_width, model_width), BF16),
            dma((n,)),
            dma((n,)),
            dma((r,)),
            dma((r,)),
            dma((r,)),
        ],
        48 * MIB,
        2 * token_count * model_width * hidden_width * 5,
        24 * MIB,
        (SMEM, idx),
        *each(ANY, middle_parts),
        *each(ANY, grad_parts),
        *each(ANY, first_blocks),
        *each(ANY, second_blocks),
        *each(ANY, down_blocks),
    )
    second_stat = sum_over_cols(second_stat)
    own, forward, backward = ring_scatter(partial)
    middle_grad, middle_grad_low, attn_stat = call(
        functools.partial(middle_grad_kernel, model_width),
        [(local, F32), (local, BF16), (row, F32)],
        [],
        16 * MIB,
        0,
        4 * MIB,
        *each(VMEM, (cotangent, tokens, middle, middle_low, inverse_second, second_stat, own, forward, backward)),
    )
    branch_parts = ring_gather(middle_grad_low)
    attn_stat = sum_over_cols(attn_stat)

    ffn_partial = call(
        functools.partial(down_kernel, n, r),
        part_shapes,
        [pltpu.VMEM((hidden_width, model_width), BF16), dma((r,))],
        24 * MIB,
        2 * token_count * model_width * hidden_width,
        8 * MIB,
        (SMEM, idx),
        (VMEM, hidden),
        *each(ANY, down_blocks),
    )
    own, forward, backward = ring_scatter(ffn_partial)
    layer_out = (middle + (own + forward.astype(F32) + backward.astype(F32))).astype(BF16)

    def weight_grads(act, act_other, lows, flipped):
        pairs = len(lows)
        shape = [
            ((low.shape[1], block) if flipped else (block, low.shape[1])) for low in lows
        ]
        outs = call(
            functools.partial(weight_grad_kernel, y_size, pairs, flipped),
            [(s, F32 if dy == 0 else BF16) for s in shape for dy in range(y_size)],
            [],
            40 * MIB,
            4 * token_count * block * y_size * sum(low.shape[1] for low in lows),
            12 * MIB,
            *each(VMEM, (act, act_other, *lows, *[swap(low) for low in lows])),
        )
        return [y_sum(outs[p * y_size : (p + 1) * y_size]) for p in range(pairs)]

    dy_other = swap(dy_send)
    m_other = swap(m_send)
    [down_grad] = weight_grads(dy_keep, dy_other, [hidden], True)
    first_grad, second_grad = weight_grads(m_keep, m_other, [low1, low2], False)

    br_keep, br_send, proj, gated, first_stat, *partial = call(
        functools.partial(back_kernel, n, r, count, model_width),
        [
            (token_half, BF16),
            (token_half, BF16),
            ((token_count, 4 * width), BF16),
            (local, BF16),
            (row, F32),
            *part_shapes,
        ],
        [
            pltpu.VMEM(full_shape, BF16),
            pltpu.VMEM((width, model_width), BF16),
            pltpu.VMEM((model_width, 4 * width), BF16),
            pltpu.VMEM(local, BF16),
            pltpu.VMEM((token_count, HEAD), F32),
            pltpu.VMEM((token_count, HEAD), F32),
            dma((n,)),
            dma((r,)),
            dma((r,)),
        ],
        40 * MIB,
        2 * token_count * model_width * width * 5,
        16 * MIB,
        (SMEM, idx),
        (SMEM, bounds),
        (SMEM, decay_rate),
        *each(VMEM, (pre, qkv, attended, squares, attn_stat)),
        *each(ANY, branch_parts),
        *each(ANY, out_blocks),
        *each(ANY, proj_blocks),
    )
    first_stat = sum_over_cols(first_stat)
    own, forward, backward = ring_scatter(partial)
    [token_grad] = call(
        functools.partial(token_grad_kernel, model_width),
        [(local, F32)],
        [],
        16 * MIB,
        0,
        3 * MIB,
        *each(VMEM, (middle_grad, tokens, inverse_first, first_stat, own, forward, backward)),
    )
    [out_grad] = weight_grads(br_keep, swap(br_send), [gated], True)
    [proj_grad] = weight_grads(normed_keep, swap(normed_send), [proj], False)
    return (
        layer_out,
        token_grad,
        *(proj_grad[:, i * width : (i + 1) * width] for i in range(4)),
        out_grad,
        first_grad,
        second_grad,
        down_grad,
    )


def solution(mesh):
    both, flipped = P("rows", "cols"), P("cols", "rows")
    return jax.shard_map(
        functools.partial(shards, ring_order(mesh), mesh.shape["rows"] // 2),
        mesh=mesh,
        in_specs=(both, both, P("rows", None), P("cols"), both, both, both, both, flipped, both, both, flipped),
        out_specs=(both, both, both, both, both, both, flipped, both, both, flipped),
        check_vma=False,
    )
```

```python
import functools

import jax
import jax.numpy as jnp
import numpy as np
from jax import lax
from jax.experimental import pallas as pl
from jax.experimental.pallas import tpu as pltpu
from jax.sharding import PartitionSpec as P

HEAD = 128
EPSILON = 1e-06
F32, BF16 = jnp.float32, jnp.bfloat16
NN, NT, TN = ((1,), (0,)), ((1,), (1,)), ((0,), (0,))
ANY = pl.BlockSpec(memory_space=pltpu.HBM)
VMEM = pl.BlockSpec(memory_space=pltpu.VMEM)
SMEM = pl.BlockSpec(memory_space=pltpu.SMEM)
MIB = 1 << 20


def dot(left, right, dims):
    return lax.dot_general(left, right, (dims, ((), ())), preferred_element_type=F32)


def silu_slope(values):
    sigmoid_of = jax.nn.sigmoid(values)
    return sigmoid_of * (1.0 + values * (1.0 - sigmoid_of))


def to_row(column):
    return jnp.broadcast_to(column, (column.shape[0], 128)).T[:8]


def to_column(row):
    return jnp.broadcast_to(row[:1], (128, row.shape[1])).T[:, :1]


def tiles(size, step=256):
    return [(at, min(step, size - at)) for at in range(0, size, step)]


def fetch(sources, target, axis, places, semaphores):
    copies = []
    for i, source in enumerate(sources):
        size = source.shape[axis]
        where = pl.ds(pl.multiple_of(places[i] * size, size), size)
        spot = target.at[:, where] if axis else target.at[where]
        copies.append(pltpu.make_async_copy(source, spot, semaphores.at[i]))
        copies[-1].start()
    return copies


def landed(copies):
    for copy in copies:
        copy.wait()


def normalize(array, inverse_out, step=32):
    def some(i, carry):
        rows = pl.ds(pl.multiple_of(i * step, step), step)
        values = array[rows, :].astype(F32)
        inverse = lax.rsqrt(jnp.mean(values * values, axis=1, keepdims=True) + EPSILON)
        array[rows, :] = (values * inverse).astype(BF16)
        inverse_out[rows, :] = jnp.broadcast_to(inverse, (step, inverse_out.shape[1]))
        return carry

    lax.fori_loop(0, array.shape[0] // step, some, 0)


def split_blocks(array, row_places, keep, send):
    block = keep.shape[1] // (len(row_places) // 2)
    for dy in range(len(row_places) // 2):
        for dc, out in ((0, keep), (1, send)):
            at = pl.ds(pl.multiple_of(row_places[dy * 2 + dc] * block, block), block)
            out[:, dy * block : (dy + 1) * block] = array[:, at]


def decay(first, rows, keys, bounds, count, rate):
    t = first + lax.broadcasted_iota(jnp.int32, (rows, keys), 0)
    s = lax.broadcasted_iota(jnp.int32, (rows, keys), 1)
    start = jnp.zeros((rows, keys), jnp.int32)
    for i in range(count):
        start = jnp.where(t >= bounds[i], bounds[i], start)
    distance = (t - s).astype(F32)
    allowed = (s >= start) & (s <= t)
    return jnp.where(allowed, jnp.exp(-rate * jnp.maximum(distance, 0.0)), 0.0)


def pack_kernel(parts, *refs):
    sources, out, semaphores = refs[:parts], refs[parts], refs[parts + 1]
    landed(fetch(sources, out, 1, range(parts), semaphores))


def front_kernel(n, r, count, idx, bounds, rate, *refs):
    x, wp = refs[:n], refs[n : n + r]
    keep, send, inverse, pre, qkv, attended, squares, gate_low, full, w_full, sx, sw = refs[n + r :]
    token_count = full.shape[0]
    width = gate_low.shape[1]
    copies_x = fetch(x, full, 1, [idx[i] for i in range(n)], sx)
    row_places = [idx[n + j] for j in range(r)]
    copies_w = fetch(wp, w_full, 0, row_places, sw)
    landed(copies_x)
    normalize(full, inverse)
    landed(copies_w)
    for part in range(4):
        at = slice(part * width, (part + 1) * width)
        values = dot(full[...], w_full[:, at], NN)
        pre[:, at] = values
        if part < 3:
            qkv[:, at] = (values * jax.nn.sigmoid(values)).astype(BF16)
    block = min(256, token_count)
    for head in range(width // HEAD):
        q, k, v = (slice(p * width + head * HEAD, p * width + (head + 1) * HEAD) for p in range(3))
        for first in range(0, token_count, block):
            keys = first + block
            weights = decay(first, block, keys, bounds, count, rate[head])
            scores = dot(qkv[first:keys, q], qkv[:keys, k], NT)
            mix = (scores * weights).astype(BF16)
            attended[first:keys, head * HEAD : (head + 1) * HEAD] = dot(mix, qkv[:keys, v], NN)
    values = attended[...]
    squares[...] = to_row(jnp.sum(values * values, axis=1, keepdims=True))
    gate_low[...] = (values * jax.nn.sigmoid(pre[:, 3 * width :])).astype(BF16)
    split_blocks(full, row_places, keep, send)


def middle_kernel(model_width, tokens, squares, own, forward, backward, middle, middle_low):
    inverse = to_column(lax.rsqrt(squares[...] / model_width + EPSILON))
    total = own[...] + forward[...].astype(F32) + backward[...].astype(F32)
    value = tokens[...].astype(F32) + total * inverse
    middle[...] = value
    middle_low[...] = value.astype(BF16)


def ffn_kernel(n, r, hidden, idx, *refs):
    m, dy = refs[:n], refs[n : 2 * n]
    w1, w2, wd = (refs[2 * n + j * r : 2 * n + (j + 1) * r] for j in range(3))
    refs = refs[2 * n + 3 * r :]
    m_keep, m_send, dy_keep, dy_send, inverse, lows, stat = refs[:7]
    parts, scratch = refs[7 : 7 + n], refs[7 + n :]
    m_full, dy_full, w1_full, w2_full, wd_full, sm, sd, s1, s2, s3 = scratch
    col_places = [idx[i] for i in range(n)]
    row_places = [idx[n + j] for j in range(r)]
    width = m[0].shape[1]
    padded = lows.shape[1] // 3
    copies_m = fetch(m, m_full, 1, col_places, sm)
    copies_1 = fetch(w1, w1_full, 1, row_places, s1)
    copies_2 = fetch(w2, w2_full, 1, row_places, s2)
    copies_y = fetch(dy, dy_full, 1, col_places, sd)
    copies_d = fetch(wd, wd_full, 1, row_places, s3)
    landed(copies_m)
    normalize(m_full, inverse)
    landed(copies_1)
    landed(copies_2)
    landed(copies_y)
    landed(copies_d)
    total = None
    for first, size in tiles(hidden):
        at = slice(first, first + size)
        act1 = dot(m_full[...], w1_full[at, :], NT)
        act2 = dot(m_full[...], w2_full[at, :], NT)
        grad = dot(dy_full[...], wd_full[at, :], NT)
        product = act1 * act2
        for j, value in enumerate((product, grad * act2, grad * act1)):
            lows[:, j * padded + first : j * padded + first + size] = value.astype(BF16)
        part = jnp.sum(grad * product, axis=1, keepdims=True)
        total = part if total is None else total + part
    if padded > hidden:
        for j in range(3):
            blank = jnp.zeros((lows.shape[0], padded - hidden), BF16)
            lows[:, j * padded + hidden : (j + 1) * padded] = blank
    stat[...] = to_row(2.0 * total)
    for i in range(n):
        at = pl.ds(pl.multiple_of(col_places[i] * width, width), width)
        value = dot(lows[:, padded : padded + hidden], w1_full[:, at], NN)
        value = value + dot(lows[:, 2 * padded : 2 * padded + hidden], w2_full[:, at], NN)
        parts[i][...] = value.astype(parts[i].dtype)
    split_blocks(m_full, row_places, m_keep, m_send)
    split_blocks(dy_full, row_places, dy_keep, dy_send)


def product_kernel(n, r, depth, idx, low, *refs):
    blocks, parts, (full, sem) = refs[:r], refs[r : r + n], refs[r + n :]
    landed(fetch(blocks, full, 1, [idx[n + j] for j in range(r)], sem))
    width = parts[0].shape[1]
    for i in range(n):
        at = pl.ds(pl.multiple_of(idx[i] * width, width), width)
        parts[i][...] = dot(low[:, :depth], full[:, at], NN).astype(parts[i].dtype)


def middle_grad_kernel(
    model_width, cotangent, tokens, middle, middle_low, inverse, stat, own, forward, backward, grad, grad_low, next_stat
):
    inverse_two = inverse[:, :1]
    mean = to_column(stat[...] / model_width)
    normed = middle_low[...].astype(F32) * inverse_two
    total = own[...] + forward[...].astype(F32) + backward[...].astype(F32)
    value = cotangent[...].astype(F32) + inverse_two * (total - normed * mean)
    low = value.astype(BF16)
    grad[...] = value
    grad_low[...] = low
    branch = middle[...] - tokens[...].astype(F32)
    next_stat[...] = to_row(jnp.sum(low.astype(F32) * branch, axis=1, keepdims=True))


def back_kernel(n, r, count, model_width, idx, bounds, rate, pre, qkv, attended, squares, stat, *refs):
    br, wo, wp = refs[:n], refs[n : n + r], refs[n + r : n + 2 * r]
    refs = refs[n + 2 * r :]
    keep, send, proj, next_stat = refs[:4]
    parts, scratch = refs[4 : 4 + n], refs[4 + n :]
    full, wo_full, w_full, att_low, key_sum, value_sum, sb, so, sw = scratch
    col_places = [idx[i] for i in range(n)]
    row_places = [idx[n + j] for j in range(r)]
    token_count = full.shape[0]
    width = wo_full.shape[0]
    copies_b = fetch(br, full, 1, col_places, sb)
    copies_o = fetch(wo, wo_full, 1, row_places, so)
    copies_w = fetch(wp, w_full, 0, row_places, sw)
    landed(copies_b)
    landed(copies_o)
    gated_grad = dot(full[...], wo_full[...], NT)
    inverse = to_column(lax.rsqrt(squares[...] / model_width + EPSILON))
    mean = to_column(stat[...] / model_width)
    pre_gate = pre[:, 3 * width :]
    gate = jax.nn.sigmoid(pre_gate)
    normed = attended[...] * inverse
    proj[:, 4 * width :] = (normed * gate).astype(BF16)
    inner = gated_grad * gate
    gate_grad = inner * normed * (1.0 - gate)
    proj[:, 3 * width : 4 * width] = gate_grad.astype(BF16)
    att_low[...] = (inverse * (inner - normed * mean)).astype(BF16)
    total = jnp.sum(gate_grad * pre_gate, axis=1, keepdims=True)
    next_stat[...] = to_row(total)
    block = min(256, token_count)
    for head in range(width // HEAD):
        here = slice(head * HEAD, (head + 1) * HEAD)
        q, k, v = (slice(p * width + head * HEAD, p * width + (head + 1) * HEAD) for p in range(3))
        key_sum[...] = jnp.zeros_like(key_sum)
        value_sum[...] = jnp.zeros_like(value_sum)
        for first in range(0, token_count, block):
            keys = first + block
            rows = slice(first, keys)
            weights = decay(first, block, keys, bounds, count, rate[head])
            scores = dot(qkv[rows, q], qkv[:keys, k], NT)
            mix = (scores * weights).astype(BF16)
            score_grad = dot(att_low[rows, here], qkv[:keys, v], NT)
            raw = (score_grad * weights).astype(BF16)
            query_sum = dot(raw, qkv[:keys, k], NN)
            values = pre[rows, q]
            proj[rows, q] = (query_sum * silu_slope(values)).astype(BF16)
            key_sum[:keys] += dot(raw, qkv[rows, q], TN)
            value_sum[:keys] += dot(mix, att_low[rows, here], TN)
        proj[:, k] = (key_sum[...] * silu_slope(pre[:, k])).astype(BF16)
        proj[:, v] = (value_sum[...] * silu_slope(pre[:, v])).astype(BF16)
    for part in range(3):
        at = slice(part * width, (part + 1) * width)
        total = total + jnp.sum(proj[:, at].astype(F32) * pre[:, at], axis=1, keepdims=True)
    next_stat[...] = to_row(total)
    landed(copies_w)
    for i in range(n):
        at = pl.ds(pl.multiple_of(col_places[i] * width, width), width)
        parts[i][...] = dot(proj[:, : 4 * width], w_full[at, :], NT).astype(parts[i].dtype)
    split_blocks(full, row_places, keep, send)


def token_grad_kernel(model_width, middle_grad, tokens, inverse, stat, own, forward, backward, out):
    inverse_first = inverse[:, :1]
    mean = to_column(stat[...] / model_width)
    normed = tokens[...].astype(F32) * inverse_first
    total = own[...] + forward[...].astype(F32) + backward[...].astype(F32)
    out[...] = middle_grad[...] + inverse_first * (total - normed * mean)


def weight_grad_kernel(y_size, columns, flipped, act, act_other, low, low_other, *outs):
    block = act.shape[1] // y_size
    for p, (start, width) in enumerate(columns):
        for dy in range(y_size):
            out = outs[p * y_size + dy]
            for first, size in tiles(block if flipped else width):
                if flipped:
                    a = slice(dy * block + first, dy * block + first + size)
                    l = slice(start, start + width)
                    value = dot(low[:, l], act[:, a], TN) + dot(low_other[:, l], act_other[:, a], TN)
                else:
                    a = slice(dy * block, (dy + 1) * block)
                    l = slice(start + first, start + first + size)
                    value = dot(act[:, a], low[:, l], TN) + dot(act_other[:, a], low_other[:, l], TN)
                out[:, first : first + size] = value.astype(out.dtype)


def ring_order(mesh):
    n = mesh.shape["cols"]
    plain = list(range(n))
    try:
        devices = np.moveaxis(mesh.devices, mesh.axis_names.index("cols"), -1)
        devices = devices.reshape(-1, n)[0]
        coords = [tuple(d.coords) for d in devices]
    except (AttributeError, TypeError):
        return plain
    varying = [d for d in range(len(coords[0])) if len({c[d] for c in coords}) > 1]
    if len(varying) != 2:
        return plain
    a, b = varying
    sizes = [len({c[d] for c in coords}) for d in (a, b)]
    if sizes[0] % 2:
        a, b, sizes = b, a, sizes[::-1]
    if sizes[0] % 2 or sizes[0] * sizes[1] != n or sizes[1] < 2:
        return plain
    lows = [min(c[d] for c in coords) for d in (a, b)]
    index = {(c[a] - lows[0], c[b] - lows[1]): i for i, c in enumerate(coords)}
    walk = []
    for i in range(sizes[0]):
        across = range(1, sizes[1])
        walk += [(i, j) for j in (across if i % 2 == 0 else reversed(across))]
    walk += [(i, 0) for i in reversed(range(sizes[0]))]
    if set(walk) != set(index):
        return plain
    return [index[spot] for spot in walk]


def call(kernel, outs, scratch, limit, flops, moved, *args, out_spec=VMEM):
    specs = [spec for spec, _ in args]
    return pl.pallas_call(
        kernel,
        out_shape=[jax.ShapeDtypeStruct(s, t) for s, t in outs],
        in_specs=specs,
        out_specs=[out_spec] * len(outs),
        scratch_shapes=scratch,
        compiler_params=pltpu.CompilerParams(vmem_limit_bytes=limit),
        cost_estimate=pl.CostEstimate(flops=int(flops), bytes_accessed=int(moved), transcendentals=0),
    )(*[pltpu.with_memory_space_constraint(arg, pltpu.HBM) if spec is ANY else arg for spec, arg in args])


def each(spec, arrays):
    return [(spec, a) for a in arrays]


def shards(cycle, y_size, *args):
    (
        tokens,
        cotangent,
        lengths,
        decay_rate,
        query_weight,
        key_weight,
        value_weight,
        gate_weight,
        out_weight,
        first_weight,
        second_weight,
        down_weight,
    ) = args
    n, r = len(cycle), 2 * y_size
    half = n // 2
    token_count, width = tokens.shape
    model_width = width * n
    block = query_weight.shape[0]
    hidden_width = first_weight.shape[1]
    count = lengths.shape[1]
    dma = pltpu.SemaphoreType.DMA

    ahead = [(cycle[i], cycle[(i + 1) % n]) for i in range(n)]
    back = [(b, a) for a, b in ahead]
    core_swap = [(i, i ^ 1) for i in range(r)]

    def y_shift(by):
        return [(y * 2 + c, (y + by) % y_size * 2 + c) for y in range(y_size) for c in range(2)]

    place = {c: i for i, c in enumerate(cycle)}
    col_table = np.array([[cycle[(place[c] + i) % n] for i in range(n)] for c in range(n)], np.int32)
    row_table = np.array(
        [[((q // 2 + j // 2) % y_size) * 2 + ((q % 2) ^ (j % 2)) for j in range(r)] for q in range(r)], np.int32
    )
    idx = jnp.concatenate(
        [
            lax.dynamic_index_in_dim(jnp.asarray(col_table), lax.axis_index("cols"), 0, False),
            lax.dynamic_index_in_dim(jnp.asarray(row_table), lax.axis_index("rows"), 0, False),
        ]
    )
    places = jnp.arange(count, dtype=jnp.int32)
    bounds = jnp.sum(jnp.where(places[None, :] <= places[:, None], lengths[0][None, :], 0), axis=1)

    def cols(array, pairs):
        return lax.ppermute(array, "cols", pairs)

    def swap(array):
        return lax.ppermute(array, "rows", core_swap)

    def add(a, b):
        return (a.astype(F32) + b.astype(F32)).astype(BF16)

    plan, due, done = {}, {}, {}

    def task(slot, name, until, inputs, work):
        plan.setdefault(slot, []).append((name, until, inputs, work))

    def clock(slot, array):
        ending = due.pop(slot, [])
        if ending or slot not in plan:
            array, *results = lax.optimization_barrier((array, *[done[name] for name in ending]))
            done.update(zip(ending, results))
        for name, until, inputs, work in plan.pop(slot, []):
            array, *given = lax.optimization_barrier((array, *inputs()))
            done[name] = work(*given)
            due.setdefault(until, []).append(name)
        return array

    def ring_gather(array, letter):
        parts = [array] + [None] * (n - 1)
        moving = (array, array)
        for k in range(1, half + 1):
            forward, backward = clock(f"{letter}{k - 1}", moving)
            parts[n - k] = forward = cols(forward, ahead)
            if k < half:
                parts[k] = backward = cols(backward, back)
            moving = (forward, backward)
        return parts

    def ring_scatter(parts, letter):
        moving = (parts[half], parts[half + 1])
        for k in range(half):
            forward, backward = clock(f"{letter}{k}", moving)
            forward = cols(forward, ahead)
            if k < half - 1:
                forward = add(forward, parts[half - 1 - k])
                backward = cols(backward, back)
                if k < half - 2:
                    backward = add(backward, parts[half + 2 + k])
            moving = (forward, backward)
        return (parts[0], *moving)

    def sum_over_cols(name, stat, spots):
        done[name] = stat
        steps = n.bit_length() - 1
        for by, (start, end) in enumerate(spread(spots, steps)):

            def inputs(by=by):
                if by:
                    done[name] = done[name] + done[f"{name}_{by - 1}"]
                return [done[name]]

            pairs = [(i, i ^ (1 << by)) for i in range(n)]
            task(start, f"{name}_{by}", end, inputs, functools.partial(cols, pairs=pairs))

        def total():
            return done[name] + done[f"{name}_{steps - 1}"]

        return total

    def spread(spots, count):
        return [spots[min(k, len(spots) - 1)] for k in range(count)]

    def side_gather(name, array, back_spots, ahead_spots):
        for way, pairs, spots in (("b", back, spread(back_spots, half)), ("f", ahead, spread(ahead_spots, half - 1))):
            for k, (start, end) in enumerate(spots, 1):
                before = f"{name}_{way}{k - 1}"
                task(
                    start,
                    f"{name}_{way}{k}",
                    end,
                    lambda before=before: [done.get(before, array)],
                    functools.partial(cols, pairs=pairs),
                )

    def side_gathered(name, array):
        return [
            array,
            *(done[f"{name}_b{k}"] for k in range(1, half + 1)),
            *(done[f"{name}_f{n - k}"] for k in range(half + 1, n)),
        ]

    def side_scatter(name, parts_name, back_spots, ahead_spots):
        for way, pairs, spots, first, by in (
            ("b", back, spread(back_spots, half), half, 1),
            ("f", ahead, spread(ahead_spots, half - 1), half - 1, -1),
        ):
            for k, (start, end) in enumerate(spots):

                def inputs(way=way, k=k, first=first, by=by):
                    mine = done[parts_name][first + by * k]
                    return [add(done[f"{name}_{way}{k - 1}"], mine) if k else mine]

                task(start, f"{name}_{way}{k}", end, inputs, functools.partial(cols, pairs=pairs))

    def gather_rows(name, array, y_spot, own_spot, other_spot):
        task(
            y_spot[0],
            name + "_y",
            y_spot[1],
            lambda: [array],
            lambda a: [lax.ppermute(a, "rows", y_shift(-dy)) for dy in range(1, y_size)],
        )
        task(own_spot[0], name + "_own", own_spot[1], lambda: [array], swap)
        task(
            other_spot[0],
            name + "_other",
            other_spot[1],
            lambda: done[name + "_y"],
            lambda *a: [swap(v) for v in a],
        )

    def blocks_of(name, array):
        blocks = [array, done[name + "_own"]]
        for a, b in zip(done[name + "_y"], done[name + "_other"]):
            blocks += [a, b]
        return blocks

    def send_y(name, source, p, start, end):
        task(
            start,
            name,
            end,
            lambda: done[source][p * y_size + 1 : (p + 1) * y_size],
            lambda *a: [lax.ppermute(v, "rows", y_shift(dy)) for dy, v in enumerate(a, 1)],
        )

    def y_total(name, source, p):
        total = done[source][p * y_size]
        for value in done[name]:
            total = total + value.astype(F32)
        return total

    first_across, second_across = first_weight.T, second_weight.T
    [packed] = call(
        functools.partial(pack_kernel, 4),
        [((block, 4 * width), BF16)],
        [dma((4,))],
        4 * MIB,
        0,
        4 * MIB,
        *each(ANY, (query_weight, key_weight, value_weight, gate_weight)),
        out_spec=ANY,
    )
    end = half - 1
    gather_rows("proj", packed, ("T0", f"T{end}"), ("T1", "T2"), (f"T{end}", "F"))
    gather_rows("out", out_weight, (f"T{end}", "F"), ("T2", f"T{end}"), ("F", "O"))
    gather_rows("first", first_across, ("F", "R1"), ("R0", "R1"), ("R1", "R2"))
    gather_rows("second", second_across, ("R1", f"R{end}"), ("R2", f"R{end}"), (f"R{end}", "A0"))
    gather_rows("down", down_weight, (f"R{end}", "A1"), ("A0", "A1"), ("A1", "A2"))
    side_gather(
        "dy",
        cotangent,
        [(f"T{end}", "F"), ("F", "O"), ("R0", "R1"), (f"A{end}", "G")],
        [("F", "O"), ("R2", f"R{end}"), ("A2", f"A{end}")],
    )

    token_half = (token_count, model_width // 2)
    local = (token_count, width)
    row = (8, token_count)
    part_shapes = [(local, F32)] + [(local, BF16)] * (n - 1)
    full_shape = (token_count, model_width)
    dense = token_count * model_width * width

    token_parts = ring_gather(tokens, "T")
    token_parts[0] = clock("F", token_parts[0])
    normed_keep, normed_send, inverse_first, pre, qkv, attended, squares, gate_low = call(
        functools.partial(front_kernel, n, r, count),
        [
            (token_half, BF16),
            (token_half, BF16),
            ((token_count, 128), F32),
            ((token_count, 4 * width), F32),
            ((token_count, 3 * width), BF16),
            (local, F32),
            (row, F32),
            (local, BF16),
        ],
        [pltpu.VMEM(full_shape, BF16), pltpu.VMEM((model_width, 4 * width), BF16), dma((n,)), dma((r,))],
        40 * MIB,
        8 * dense,
        24 * MIB,
        (SMEM, idx),
        (SMEM, bounds),
        (SMEM, decay_rate),
        *each(ANY, token_parts),
        *each(ANY, blocks_of("proj", packed)),
    )
    gate_low = clock("O", gate_low)

    def product(low, blocks, depth):
        return call(
            functools.partial(product_kernel, n, r, depth),
            part_shapes,
            [pltpu.VMEM((depth, model_width), BF16), dma((r,))],
            24 * MIB,
            2 * token_count * model_width * depth,
            8 * MIB,
            (SMEM, idx),
            (VMEM, low),
            *each(ANY, blocks),
        )

    out_blocks = blocks_of("out", out_weight)
    partial = product(gate_low, out_blocks, width)
    squares_total = sum_over_cols("squares", squares, [("R0", "R1"), ("R1", "R2"), ("R2", f"R{end}")])
    own, forward, backward = ring_scatter(partial, "R")
    squares_sum = squares_total()
    middle, middle_low = call(
        functools.partial(middle_kernel, model_width),
        [(local, F32), (local, BF16)],
        [],
        16 * MIB,
        0,
        3 * MIB,
        *each(VMEM, (tokens, squares_sum, own, forward, backward)),
    )
    task("A2", "normed_swap", f"A{end}", lambda: [normed_send], swap)
    middle_parts = ring_gather(middle_low, "A")
    middle_parts[0] = clock("G", middle_parts[0])
    padded = -(-hidden_width // 128) * 128
    m_keep, m_send, dy_keep, dy_send, inverse_second, lows, second_stat, *partial = call(
        functools.partial(ffn_kernel, n, r, hidden_width),
        [
            (token_half, BF16),
            (token_half, BF16),
            (token_half, BF16),
            (token_half, BF16),
            ((token_count, 128), F32),
            ((token_count, 3 * padded), BF16),
            (row, F32),
            *part_shapes,
        ],
        [
            pltpu.VMEM(full_shape, BF16),
            pltpu.VMEM(full_shape, BF16),
            pltpu.VMEM((hidden_width, model_width), BF16),
            pltpu.VMEM((hidden_width, model_width), BF16),
            pltpu.VMEM((hidden_width, model_width), BF16),
            dma((n,)),
            dma((n,)),
            dma((r,)),
            dma((r,)),
            dma((r,)),
        ],
        48 * MIB,
        10 * token_count * model_width * hidden_width,
        24 * MIB,
        (SMEM, idx),
        *each(ANY, middle_parts),
        *each(ANY, side_gathered("dy", cotangent)),
        *each(ANY, blocks_of("first", first_across)),
        *each(ANY, blocks_of("second", second_across)),
        *each(ANY, blocks_of("down", down_weight)),
    )
    second_total = sum_over_cols("second_stat", second_stat, [("Q0", "Q1"), ("Q1", "Q2"), ("Q2", f"Q{end}")])

    def weight_grads(columns, flipped):
        def work(act, act_other, low, low_other):
            shapes = [(w, block) if flipped else (block, w) for _, w in columns]
            return call(
                functools.partial(weight_grad_kernel, y_size, columns, flipped),
                [(s, F32 if dy == 0 else BF16) for s in shapes for dy in range(y_size)],
                [],
                40 * MIB,
                4 * token_count * block * y_size * sum(w for _, w in columns),
                8 * MIB,
                *each(VMEM, (act, act_other, low, low_other)),
            )

        return work

    down_blocks = blocks_of("down", down_weight)
    task("Q0", "dy_swap", "Q1", lambda: [dy_send], swap)
    task("Q0", "lows_swap", "Q1", lambda: [lows], swap)
    task("Q0", "ffn_parts", "Q1", lambda: [lows], lambda low: product(low, down_blocks, hidden_width))
    task("Q1", "m_swap", "Q2", lambda: [m_send], swap)
    for slot, until, name, act, other, at in (
        ("Q1", "Q2", "down", dy_keep, "dy_swap", 0),
        ("Q2", f"Q{end}", "first", m_keep, "m_swap", padded),
        (f"Q{end}", "B0", "second", m_keep, "m_swap", 2 * padded),
    ):
        task(
            slot,
            name + "_grad",
            until,
            lambda act=act, other=other: [act, done[other], lows, done["lows_swap"]],
            weight_grads([(at, hidden_width)], True),
        )
    send_y("down_sent", "down_grad", 0, "Q2", "B0")
    send_y("first_sent", "first_grad", 0, "B0", "B2")
    send_y("second_sent", "second_grad", 0, "B2", "K")
    side_scatter(
        "ffn",
        "ffn_parts",
        [("Q2", f"Q{end}"), (f"B{end}", "K"), ("K", "N0"), ("N0", "N1")],
        [("B1", "B2"), ("K", "N0"), ("N2", f"N{end}")],
    )
    own, forward, backward = ring_scatter(partial, "Q")
    middle_grad, middle_grad_low, attn_stat = call(
        functools.partial(middle_grad_kernel, model_width),
        [(local, F32), (local, BF16), (row, F32)],
        [],
        16 * MIB,
        0,
        4 * MIB,
        *each(VMEM, (cotangent, tokens, middle, middle_low, inverse_second, second_total(), own, forward, backward)),
    )
    attn_total = sum_over_cols("attn_stat", attn_stat, [("B0", "B1"), ("B1", "B2"), ("B2", f"B{end}")])
    branch_parts = ring_gather(middle_grad_low, "B")
    branch_parts[0] = clock("K", branch_parts[0])
    br_keep, br_send, proj, first_stat, *partial = call(
        functools.partial(back_kernel, n, r, count, model_width),
        [
            (token_half, BF16),
            (token_half, BF16),
            ((token_count, 5 * width), BF16),
            (row, F32),
            *part_shapes,
        ],
        [
            pltpu.VMEM(full_shape, BF16),
            pltpu.VMEM((width, model_width), BF16),
            pltpu.VMEM((model_width, 4 * width), BF16),
            pltpu.VMEM(local, BF16),
            pltpu.VMEM((token_count, HEAD), F32),
            pltpu.VMEM((token_count, HEAD), F32),
            dma((n,)),
            dma((r,)),
            dma((r,)),
        ],
        40 * MIB,
        10 * dense,
        24 * MIB,
        (SMEM, idx),
        (SMEM, bounds),
        (SMEM, decay_rate),
        *each(VMEM, (pre, qkv, attended, squares_sum, attn_total())),
        *each(ANY, branch_parts),
        *each(ANY, out_blocks),
        *each(ANY, blocks_of("proj", packed)),
    )
    first_total = sum_over_cols("first_stat", first_stat, [("N0", "N1"), ("N1", "N2"), ("N2", f"N{end}")])
    task("N0", "proj_swap", "N1", lambda: [proj], swap)
    task("N0", "br_swap", "N1", lambda: [br_send], swap)
    task(
        "N1",
        "proj_grad",
        "N2",
        lambda: [normed_keep, done["normed_swap"], proj, done["proj_swap"]],
        weight_grads([(0, 4 * width)], False),
    )
    send_y("proj_sent", "proj_grad", 0, "N2", "END")
    task(
        "N2",
        "out_grad",
        f"N{end}",
        lambda: [br_keep, done["br_swap"], proj, done["proj_swap"]],
        weight_grads([(4 * width, width)], True),
    )
    send_y("out_sent", "out_grad", 0, f"N{end}", "END")
    own, forward, backward = ring_scatter(partial, "N")
    [token_grad] = call(
        functools.partial(token_grad_kernel, model_width),
        [(local, F32)],
        [],
        16 * MIB,
        0,
        3 * MIB,
        *each(VMEM, (middle_grad, tokens, inverse_first, first_total(), own, forward, backward)),
    )
    token_grad = clock("END", token_grad)
    ffn_total = done["ffn_parts"][0] + done[f"ffn_b{half - 1}"].astype(F32) + done[f"ffn_f{half - 2}"].astype(F32)
    layer_out = (middle + ffn_total).astype(BF16)
    proj_grad = y_total("proj_sent", "proj_grad", 0)
    return (
        layer_out,
        token_grad,
        *(proj_grad[:, i * width : (i + 1) * width] for i in range(4)),
        y_total("out_sent", "out_grad", 0),
        y_total("first_sent", "first_grad", 0).T,
        y_total("second_sent", "second_grad", 0).T,
        y_total("down_sent", "down_grad", 0),
    )


def solution(mesh):
    both, flipped = P("rows", "cols"), P("cols", "rows")
    return jax.shard_map(
        functools.partial(shards, ring_order(mesh), mesh.shape["rows"] // 2),
        mesh=mesh,
        in_specs=(both, both, P("rows", None), P("cols"), both, both, both, both, flipped, both, both, flipped),
        out_specs=(both, both, both, both, both, both, flipped, both, both, flipped),
        check_vma=False,
    )
```

```python
import functools

import jax
import jax.numpy as jnp
import numpy as np
from jax import lax
from jax.experimental import pallas as pl
from jax.experimental.pallas import tpu as pltpu
from jax.sharding import PartitionSpec as P

HEAD = 128
EPSILON = 1e-06
F32, BF16 = jnp.float32, jnp.bfloat16
NN, NT, TN = ((1,), (0,)), ((1,), (1,)), ((0,), (0,))
ANY = pl.BlockSpec(memory_space=pltpu.HBM)
FREE = pl.BlockSpec(memory_space=pl.ANY)
VMEM = pl.BlockSpec(memory_space=pltpu.VMEM)
SMEM = pl.BlockSpec(memory_space=pltpu.SMEM)
MIB = 1 << 20


def dot(left, right, dims):
    return lax.dot_general(left, right, (dims, ((), ())), preferred_element_type=F32)


def silu_slope(values):
    sigmoid_of = jax.nn.sigmoid(values)
    return sigmoid_of * (1.0 + values * (1.0 - sigmoid_of))


def to_row(column):
    return jnp.broadcast_to(column, (column.shape[0], 128)).T[:8]


def to_column(row):
    return jnp.broadcast_to(row[:1], (128, row.shape[1])).T[:, :1]


def tiles(size, step=256):
    return [(at, min(step, size - at)) for at in range(0, size, step)]


class Copies:
    def __init__(self, semaphores):
        self.semaphores, self.started, self.waited = semaphores, [], 0

    def start(self, source, target):
        copy = pltpu.make_async_copy(source, target, self.semaphores.at[len(self.started)])
        copy.start()
        self.started.append(copy)

    def land(self):
        for copy in self.started[self.waited :]:
            copy.wait()
        self.waited = len(self.started)


def span(place, size):
    return pl.ds(pl.multiple_of(place * size, size), size)


def fetch_chunks(copies, chunks, target, places):
    rows, width = target.shape[0], chunks[0].shape[1]
    for chunk, place in zip(chunks, places):
        source = chunk if chunk.shape[0] == rows else chunk.at[:rows]
        copies.start(source, target.at[:, span(place, width)])


def fetch_out(copies, packs, target, places):
    width = target.shape[0]
    for pack, place in zip(packs, places):
        pieces = pack.shape[0] // width
        for p in range(pieces):
            source = pack.at[p * width : (p + 1) * width, width:]
            copies.start(source, target.at[:, span(place * pieces + p, width)])


def fetch_down(copies, packs, columns, target, places):
    for pack, place in zip(packs, places):
        rows = span(place, pack.shape[0]) if not isinstance(place, int) else slice(place * pack.shape[0], (place + 1) * pack.shape[0])
        copies.start(pack.at[:, columns], target.at[rows])


def fetch_across(copies, blocks, target, places):
    for block, place in zip(blocks, places):
        copies.start(block, target.at[:, span(place, block.shape[1])])


def stat_block(row, rows, width, slot):
    pieces = row.shape[1] // width
    at = lax.broadcasted_iota(jnp.int32, (rows, width), 0)
    block = jnp.zeros((rows, width), F32)
    for k in range(pieces):
        value = row[:, k * width : (k + 1) * width]
        high = value.astype(BF16).astype(F32)
        for j, part in enumerate((high, value - high)):
            here = at == slot * 2 * pieces + j * pieces + k
            block = jnp.where(here, jnp.broadcast_to(part, (rows, width)), block)
    return block.astype(BF16)


def stat_total(block, tokens):
    rows, width = block.shape
    pieces = tokens // width
    at = lax.rem(lax.broadcasted_iota(jnp.int32, (rows, width), 0), pieces)
    values = block.astype(F32)
    parts = [jnp.sum(jnp.where(at == k, values, 0.0), axis=0, keepdims=True) for k in range(pieces)]
    return jnp.concatenate(parts, axis=1)


def normalize(array, inverse_out, step=32):
    def some(i, carry):
        rows = pl.ds(pl.multiple_of(i * step, step), step)
        values = array[rows, :].astype(F32)
        inverse = lax.rsqrt(jnp.mean(values * values, axis=1, keepdims=True) + EPSILON)
        array[rows, :] = (values * inverse).astype(BF16)
        inverse_out[rows, :] = jnp.broadcast_to(inverse, (step, inverse_out.shape[1]))
        return carry

    lax.fori_loop(0, array.shape[0] // step, some, 0)


def split_blocks(copies, array, row_places, keep, send):
    block = keep.shape[1] // (len(row_places) // 2)
    for dy in range(len(row_places) // 2):
        for dc, out in ((0, keep), (1, send)):
            copies.start(array.at[:, span(row_places[dy * 2 + dc], block)], out.at[:, dy * block : (dy + 1) * block])


def decay(first, rows, keys, bounds, count, rate):
    t = first + lax.broadcasted_iota(jnp.int32, (rows, keys), 0)
    s = lax.broadcasted_iota(jnp.int32, (rows, keys), 1)
    start = jnp.zeros((rows, keys), jnp.int32)
    for i in range(count):
        start = jnp.where(t >= bounds[i], bounds[i], start)
    distance = (t - s).astype(F32)
    allowed = (s >= start) & (s <= t)
    return jnp.where(allowed, jnp.exp(-rate * jnp.maximum(distance, 0.0)), 0.0)


def pack_kernel(query, key, value, gate, out, first, second, sems):
    copies = Copies(sems)
    width = query.shape[1]
    for p, weight in enumerate((query, key, value)):
        copies.start(weight, first.at[:, p * width : (p + 1) * width])
    copies.start(gate, second.at[:, :width])
    for p in range(out.shape[1] // width):
        at = slice(p * width, (p + 1) * width)
        copies.start(out.at[:, at], second.at[at, width:])
    copies.land()


def front_kernel(n, r, count, idx, bounds, rate, *refs):
    x, weights = refs[:n], refs[n : n + r]
    keep, send, inverse, pre_out, qkv_out, attended, squares, full, w_full, pre, qkv, sems, out_sems = refs[n + r :]
    token_count = full.shape[0]
    width = attended.shape[1]
    row_places = [idx[n + j] for j in range(r)]
    copies, sent = Copies(sems), Copies(out_sems)
    fetch_chunks(copies, x, full, [idx[i] for i in range(n)])
    copies.land()
    fetch_down(copies, weights, slice(0, 3 * width), w_full, row_places)
    normalize(full, inverse)
    split_blocks(sent, full, row_places, keep, send)
    copies.land()
    for p in range(3):
        at = slice(p * width, (p + 1) * width)
        values = dot(full[...], w_full[:, at], NN)
        pre[:, at] = values
        qkv[:, at] = (values * jax.nn.sigmoid(values)).astype(BF16)
    sent.start(pre, pre_out)
    sent.start(qkv, qkv_out)
    block = min(256, token_count)
    for head in range(width // HEAD):
        q, k, v = (slice(p * width + head * HEAD, p * width + (head + 1) * HEAD) for p in range(3))
        for first in range(0, token_count, block):
            keys = first + block
            decays = decay(first, block, keys, bounds, count, rate[head])
            scores = dot(qkv[first:keys, q], qkv[:keys, k], NT)
            mix = (scores * decays).astype(BF16)
            attended[first:keys, head * HEAD : (head + 1) * HEAD] = dot(mix, qkv[:keys, v], NN)
    values = attended[...]
    squares[...] = to_row(jnp.sum(values * values, axis=1, keepdims=True))
    sent.land()


def put_parts(parts, product, stat, n):
    for i, part in enumerate(parts):
        value = product(i)
        tokens, width = value.shape
        part[:tokens] = value.astype(part.dtype)
        if i and stat is not None:
            part[tokens:] = stat_block(stat, part.shape[0] - tokens, width, min(i, n - i) - 1)


def gate_kernel(n, r, idx, keep, send, attended, stat, *refs):
    packs, refs = refs[:r], refs[r:]
    pre_gate, gate_low = refs[:2]
    parts, (w_gate, full, sems) = refs[2 : 2 + n], refs[2 + n :]
    width = attended.shape[1]
    size = w_gate.shape[0] // r
    copies = Copies(sems)
    fetch_down(copies, packs, slice(0, width), w_gate, range(r))
    fetch_out(copies, packs, full, [idx[n + j] for j in range(r)])
    copies.land()
    total = None
    for j in range(r):
        source = (keep, send)[j % 2]
        value = dot(source[:, j // 2 * size : (j // 2 + 1) * size], w_gate[j * size : (j + 1) * size, :], NN)
        total = value if total is None else total + value
    pre_gate[...] = total
    low = (attended[...] * jax.nn.sigmoid(total)).astype(BF16)
    gate_low[...] = low
    put_parts(parts, lambda i: dot(gate_low[...], full[:, span(idx[i], width)], NN), stat[:1], n)


def down_kernel(n, r, depth, idx, low, *refs):
    blocks, parts, (full, sems) = refs[:r], refs[r : r + n], refs[r + n :]
    copies = Copies(sems)
    fetch_across(copies, blocks, full, [idx[n + j] for j in range(r)])
    copies.land()
    width = parts[0].shape[1]
    put_parts(parts, lambda i: dot(low[:, :depth], full[:, span(idx[i], width)], NN), None, n)


def middle_kernel(model_width, tokens, squares, own, forward, backward, middle, middle_low, inverse_row):
    t = tokens.shape[0]
    total = squares[:1] + stat_total(forward[t:], t) + stat_total(backward[t:], t)
    inverse = lax.rsqrt(total / model_width + EPSILON)
    inverse_row[...] = jnp.broadcast_to(inverse, inverse_row.shape)
    summed = own[...] + forward[:t].astype(F32) + backward[:t].astype(F32)
    value = tokens[...].astype(F32) + summed * to_column(inverse)
    middle[...] = value
    middle_low[...] = value.astype(BF16)


def ffn_kernel(n, r, hidden, idx, *refs):
    m, dy, refs = refs[:n], refs[n : 2 * n], refs[2 * n :]
    (w1, w2, wd), refs = (refs[j * r : (j + 1) * r] for j in range(3)), refs[3 * r :]
    m_keep, m_send, dy_keep, dy_send, lows_out, inverse, stat = refs[:7]
    parts, (m_full, dy_full, w1_full, w2_full, wd_full, lows, sems, out_sems) = refs[7 : 7 + n], refs[7 + n :]
    col_places = [idx[i] for i in range(n)]
    row_places = [idx[n + j] for j in range(r)]
    width = m[0].shape[1]
    padded = lows.shape[1] // 3
    copies, sent = Copies(sems), Copies(out_sems)
    fetch_chunks(copies, m, m_full, col_places)
    copies.land()
    fetch_across(copies, w1, w1_full, row_places)
    fetch_across(copies, w2, w2_full, row_places)
    fetch_chunks(copies, dy, dy_full, col_places)
    fetch_across(copies, wd, wd_full, row_places)
    normalize(m_full, inverse)
    split_blocks(sent, m_full, row_places, m_keep, m_send)
    copies.land()
    split_blocks(sent, dy_full, row_places, dy_keep, dy_send)
    total = None
    for first, size in tiles(hidden):
        at = slice(first, first + size)
        act1 = dot(m_full[...], w1_full[at, :], NT)
        act2 = dot(m_full[...], w2_full[at, :], NT)
        grad = dot(dy_full[...], wd_full[at, :], NT)
        product = act1 * act2
        for j, value in enumerate((product, grad * act2, grad * act1)):
            lows[:, j * padded + first : j * padded + first + size] = value.astype(BF16)
        part = jnp.sum(grad * product, axis=1, keepdims=True)
        total = part if total is None else total + part
    if padded > hidden:
        for j in range(3):
            blank = jnp.zeros((lows.shape[0], padded - hidden), BF16)
            lows[:, j * padded + hidden : (j + 1) * padded] = blank
    sent.start(lows, lows_out)
    row = to_row(2.0 * total)
    stat[...] = row

    def product(i):
        at = span(col_places[i], width)
        value = dot(lows[:, padded : padded + hidden], w1_full[:, at], NN)
        return value + dot(lows[:, 2 * padded : 2 * padded + hidden], w2_full[:, at], NN)

    put_parts(parts, product, row[:1], n)
    sent.land()


def middle_grad_kernel(
    model_width, cotangent, tokens, middle, middle_low, inverse, stat, own, forward, backward, grad, grad_low
):
    t = tokens.shape[0]
    inverse_two = inverse[:, :1]
    total = stat[:1] + stat_total(forward[t:], t) + stat_total(backward[t:], t)
    mean = to_column(total / model_width)
    normed = middle_low[...].astype(F32) * inverse_two
    summed = own[...] + forward[:t].astype(F32) + backward[:t].astype(F32)
    value = cotangent[...].astype(F32) + inverse_two * (summed - normed * mean)
    low = value.astype(BF16)
    grad[...] = value
    grad_low[:t] = low
    branch = middle[...] - tokens[...].astype(F32)
    row = to_row(jnp.sum(low.astype(F32) * branch, axis=1, keepdims=True))[:1]
    grad_low[t:] = stat_block(row, grad_low.shape[0] - t, grad_low.shape[1], 0)


def back_kernel(n, r, count, model_width, idx, bounds, rate, pre, pre_gate, qkv, attended, inverse_row, *refs):
    br, packs, gate_packs, refs = refs[:n], refs[n : n + r], refs[n + r : n + 2 * r], refs[n + 2 * r :]
    keep, send, proj_out, next_stat = refs[:4]
    parts, scratch = refs[4 : 4 + n], refs[4 + n :]
    full, wo_full, w_full, proj, stats, att_low, key_sum, value_sum, sems, out_sems = scratch
    col_places = [idx[i] for i in range(n)]
    row_places = [idx[n + j] for j in range(r)]
    token_count = full.shape[0]
    width = wo_full.shape[0]
    copies, sent = Copies(sems), Copies(out_sems)
    fetch_chunks(copies, br, full, col_places)
    extra = stats.shape[1]
    for i in range(n):
        copies.start(br[i].at[token_count:], stats.at[i])
    fetch_out(copies, gate_packs, wo_full, row_places)
    copies.land()
    fetch_down(copies, packs, slice(0, 3 * width), w_full.at[:, : 3 * width], row_places)
    fetch_down(copies, gate_packs, slice(0, width), w_full.at[:, 3 * width :], row_places)
    split_blocks(sent, full, row_places, keep, send)
    gated_grad = dot(full[...], wo_full[...], NT)
    inverse = to_column(inverse_row[...])
    mean = to_column(stat_total(stats[...].reshape(n * extra, width), token_count) / model_width)
    values = pre_gate[...]
    gate = jax.nn.sigmoid(values)
    normed = attended[...] * inverse
    proj[:, 4 * width :] = (normed * gate).astype(BF16)
    inner = gated_grad * gate
    gate_grad = inner * normed * (1.0 - gate)
    proj[:, 3 * width : 4 * width] = gate_grad.astype(BF16)
    att_low[...] = (inverse * (inner - normed * mean)).astype(BF16)
    total = jnp.sum(gate_grad * values, axis=1, keepdims=True)
    block = min(256, token_count)
    for head in range(width // HEAD):
        here = slice(head * HEAD, (head + 1) * HEAD)
        q, k, v = (slice(p * width + head * HEAD, p * width + (head + 1) * HEAD) for p in range(3))
        key_sum[...] = jnp.zeros_like(key_sum)
        value_sum[...] = jnp.zeros_like(value_sum)
        for first in range(0, token_count, block):
            keys = first + block
            rows = slice(first, keys)
            decays = decay(first, block, keys, bounds, count, rate[head])
            scores = dot(qkv[rows, q], qkv[:keys, k], NT)
            mix = (scores * decays).astype(BF16)
            score_grad = dot(att_low[rows, here], qkv[:keys, v], NT)
            raw = (score_grad * decays).astype(BF16)
            query_sum = dot(raw, qkv[:keys, k], NN)
            proj[rows, q] = (query_sum * silu_slope(pre[rows, q])).astype(BF16)
            key_sum[:keys] += dot(raw, qkv[rows, q], TN)
            value_sum[:keys] += dot(mix, att_low[rows, here], TN)
        proj[:, k] = (key_sum[...] * silu_slope(pre[:, k])).astype(BF16)
        proj[:, v] = (value_sum[...] * silu_slope(pre[:, v])).astype(BF16)
    sent.start(proj, proj_out)
    for p in range(3):
        at = slice(p * width, (p + 1) * width)
        total = total + jnp.sum(proj[:, at].astype(F32) * pre[:, at], axis=1, keepdims=True)
    row = to_row(total)
    next_stat[...] = row
    copies.land()
    put_parts(
        parts, lambda i: dot(proj[:, : 4 * width], w_full[span(col_places[i], width), :], NT), row[:1], n
    )
    sent.land()


def token_grad_kernel(model_width, middle_grad, tokens, inverse, stat, own, forward, backward, out):
    t = tokens.shape[0]
    inverse_first = inverse[:, :1]
    total = stat[:1] + stat_total(forward[t:], t) + stat_total(backward[t:], t)
    mean = to_column(total / model_width)
    normed = tokens[...].astype(F32) * inverse_first
    summed = own[...] + forward[:t].astype(F32) + backward[:t].astype(F32)
    out[...] = middle_grad[...] + inverse_first * (summed - normed * mean)


def weight_grad_kernel(y_size, columns, flipped, act, act_other, low, low_other, *outs):
    block = act.shape[1] // y_size
    outs = iter(outs)
    for start, width in columns:
        for dy in range(y_size):
            out = next(outs)
            for first, size in tiles(block if flipped else width):
                if flipped:
                    a = slice(dy * block + first, dy * block + first + size)
                    l = slice(start, start + width)
                    value = dot(low[:, l], act[:, a], TN) + dot(low_other[:, l], act_other[:, a], TN)
                else:
                    a = slice(dy * block, (dy + 1) * block)
                    l = slice(start + first, start + first + size)
                    value = dot(act[:, a], low[:, l], TN) + dot(act_other[:, a], low_other[:, l], TN)
                out[:, first : first + size] = value.astype(out.dtype)


def ring_order(mesh):
    n = mesh.shape["cols"]
    plain = list(range(n))
    try:
        devices = np.moveaxis(mesh.devices, mesh.axis_names.index("cols"), -1)
        devices = devices.reshape(-1, n)[0]
        coords = [tuple(d.coords) for d in devices]
    except (AttributeError, TypeError):
        return plain
    varying = [d for d in range(len(coords[0])) if len({c[d] for c in coords}) > 1]
    if len(varying) != 2:
        return plain
    a, b = varying
    sizes = [len({c[d] for c in coords}) for d in (a, b)]
    if sizes[0] % 2:
        a, b, sizes = b, a, sizes[::-1]
    if sizes[0] % 2 or sizes[0] * sizes[1] != n or sizes[1] < 2:
        return plain
    lows = [min(c[d] for c in coords) for d in (a, b)]
    index = {(c[a] - lows[0], c[b] - lows[1]): i for i, c in enumerate(coords)}
    walk = []
    for i in range(sizes[0]):
        across = range(1, sizes[1])
        walk += [(i, j) for j in (across if i % 2 == 0 else reversed(across))]
    walk += [(i, 0) for i in reversed(range(sizes[0]))]
    if set(walk) != set(index):
        return plain
    return [index[spot] for spot in walk]


def call(kernel, outs, scratch, limit, flops, moved, *args):
    return pl.pallas_call(
        kernel,
        out_shape=[jax.ShapeDtypeStruct(out[0], out[1]) for out in outs],
        in_specs=[spec for spec, _ in args],
        out_specs=[(*out, VMEM)[2] for out in outs],
        scratch_shapes=scratch,
        compiler_params=pltpu.CompilerParams(vmem_limit_bytes=limit),
        cost_estimate=pl.CostEstimate(flops=int(flops), bytes_accessed=int(moved), transcendentals=0),
    )(*[pltpu.with_memory_space_constraint(arg, pltpu.HBM) if spec is ANY else arg for spec, arg in args])


def each(spec, arrays):
    return [(spec, a) for a in arrays]


def shards(cycle, y_size, *args):
    (
        tokens,
        cotangent,
        lengths,
        decay_rate,
        query_weight,
        key_weight,
        value_weight,
        gate_weight,
        out_weight,
        first_weight,
        second_weight,
        down_weight,
    ) = args
    n, r = len(cycle), 2 * y_size
    half = n // 2
    token_count, width = tokens.shape
    model_width = width * n
    block = query_weight.shape[0]
    hidden_width = first_weight.shape[1]
    count = lengths.shape[1]
    dma = pltpu.SemaphoreType.DMA

    ahead = [(cycle[i], cycle[(i + 1) % n]) for i in range(n)]
    back = [(b, a) for a, b in ahead]
    core_swap = [(i, i ^ 1) for i in range(r)]

    def y_shift(by):
        return [(y * 2 + c, (y + by) % y_size * 2 + c) for y in range(y_size) for c in range(2)]

    place = {c: i for i, c in enumerate(cycle)}
    col_table = np.array([[cycle[(place[c] + i) % n] for i in range(n)] for c in range(n)], np.int32)
    row_table = np.array(
        [[((q // 2 + j // 2) % y_size) * 2 + ((q % 2) ^ (j % 2)) for j in range(r)] for q in range(r)], np.int32
    )
    idx = jnp.concatenate(
        [
            lax.dynamic_index_in_dim(jnp.asarray(col_table), lax.axis_index("cols"), 0, False),
            lax.dynamic_index_in_dim(jnp.asarray(row_table), lax.axis_index("rows"), 0, False),
        ]
    )
    places = jnp.arange(count, dtype=jnp.int32)
    bounds = jnp.sum(jnp.where(places[None, :] <= places[:, None], lengths[0][None, :], 0), axis=1)

    def cols(array, pairs):
        return lax.ppermute(array, "cols", pairs)

    def swap(array):
        return lax.ppermute(array, "rows", core_swap)

    def add(a, b):
        return (a.astype(F32) + b.astype(F32)).astype(BF16)

    plan, due, done = {}, {}, {}

    def task(slot, name, until, inputs, work):
        plan.setdefault(slot, []).append((name, until, inputs, work))

    def clock(slot, array, backward=None):
        tie = lax.optimization_barrier
        ending = due.pop(slot, [])
        if ending or backward is not None:
            array, backward, results = tie((array, backward, [done[name] for name in ending]))
            done.update(zip(ending, results))
        for name, until, inputs, work in plan.pop(slot, []):
            _, given = tie((array, inputs()))
            done[name] = work(*given)
            due.setdefault(until, []).append(name)
        return array if backward is None else (array, backward)

    def ring_gather(array, letter):
        parts = [array] + [None] * (n - 1)
        forward = backward = array
        for k in range(1, half + 1):
            if k < half:
                forward, backward = clock(f"{letter}{k - 1}", forward, backward)
                parts[k] = backward = cols(backward, back)
            else:
                forward, backward = lax.optimization_barrier((forward, backward))
                forward = clock(f"{letter}{k - 1}", forward)
            parts[n - k] = forward = cols(forward, ahead)
        return parts

    def ring_scatter(parts, letter):
        forward, backward = parts[half], parts[half + 1]
        for k in range(half - 1):
            forward, backward = clock(f"{letter}{k}", forward, backward)
            forward = add(cols(forward, ahead), parts[half - 1 - k])
            backward = cols(backward, back)
            if k < half - 2:
                backward = add(backward, parts[half + 2 + k])
        forward, backward = lax.optimization_barrier((forward, backward))
        forward = cols(clock(f"{letter}{half - 1}", forward), ahead)
        return parts[0], forward, backward

    def spread(spots, count):
        return [spots[min(k, len(spots) - 1)] for k in range(count)]

    def side_gather(name, array, back_spots, ahead_spots):
        for way, pairs, spots in (("b", back, spread(back_spots, half)), ("f", ahead, spread(ahead_spots, half - 1))):
            for k, (start, until) in enumerate(spots, 1):

                def inputs(before=f"{name}_{way}{k - 1}"):
                    return [done.get(before, array)]

                task(start, f"{name}_{way}{k}", until, inputs, functools.partial(cols, pairs=pairs))

    def side_gathered(name, array):
        return [
            array,
            *(done[f"{name}_b{k}"] for k in range(1, half + 1)),
            *(done[f"{name}_f{n - k}"] for k in range(half + 1, n)),
        ]

    def side_scatter(name, parts_name, back_spots, ahead_spots):
        for way, pairs, spots, first, by in (
            ("b", back, spread(back_spots, half), half, 1),
            ("f", ahead, spread(ahead_spots, half - 1), half - 1, -1),
        ):
            for k, (start, until) in enumerate(spots):

                def inputs(k=k, way=way, first=first, by=by):
                    mine = done[parts_name][first + by * k]
                    return [add(done[f"{name}_{way}{k - 1}"], mine) if k else mine]

                task(start, f"{name}_{way}{k}", until, inputs, functools.partial(cols, pairs=pairs))

    def send_y(name, source, first, start, until):
        task(
            start,
            name,
            until,
            lambda: [done[source][first + dy] for dy in range(1, y_size)],
            lambda *a: [lax.ppermute(v, "rows", y_shift(dy)) for dy, v in enumerate(a, 1)],
        )

    def y_total(name, source, first):
        total = done[source][first]
        for value in done[name]:
            total = total + value.astype(F32)
        return total

    first_across, second_across = first_weight.T, second_weight.T
    end = half - 1
    packs = call(
        pack_kernel,
        [((block, 3 * width), BF16, ANY), ((block, 2 * width), BF16, ANY)],
        [dma((4 + block // width,))],
        4 * MIB,
        0,
        MIB,
        *each(ANY, (query_weight, key_weight, value_weight, gate_weight, out_weight)),
    )
    y_gather = lambda a: [lax.ppermute(a, "rows", y_shift(-dy)) for dy in range(1, y_size)]
    for name, pack, y_spot, own_spot, other_spot in (
        ("pack", packs[0], ("T0", "T2"), ("T1", "T2"), ("T2", f"T{end}")),
        ("gate_pack", packs[1], ("T2", "O"), ("T2", f"T{end}"), ("O", "P")),
        ("first", first_across, ("F", "R0"), ("T1", "T2"), ("R1", "R2")),
        ("second", second_across, ("R0", "R2"), ("T2", f"T{end}"), ("R2", f"R{end}")),
        ("down", down_weight, ("R2", "A0"), (f"T{end}", "F"), ("A0", "A1")),
    ):
        task(y_spot[0], name + "_y", y_spot[1], lambda pack=pack: [pack], y_gather)
        task(own_spot[0], name + "_own", own_spot[1], lambda pack=pack: [pack], swap)
        task(
            other_spot[0],
            name + "_other",
            other_spot[1],
            lambda name=name: done[name + "_y"],
            lambda *a: [swap(v) for v in a],
        )

    def blocks_of(name, pack):
        blocks = [pack, done[name + "_own"]]
        for a, b in zip(done[name + "_y"], done[name + "_other"]):
            blocks += [a, b]
        return blocks

    side_gather(
        "dy",
        cotangent,
        [(f"T{end}", "F"), ("F", "O"), ("O", "R0"), (f"A{end}", "G")],
        [("F", "O"), ("O", "R0"), ("R0", "R1")],
    )

    token_half = (token_count, model_width // 2)
    local = (token_count, width)
    row = (8, token_count)
    stat_rows = 2 * token_count // width
    with_stat = [(local, F32)] + [((token_count + half * stat_rows, width), BF16)] * (n - 1)
    full_shape = (token_count, model_width)
    dense = token_count * model_width * width

    token_parts = ring_gather(tokens, "T")
    token_parts[0] = clock("F", token_parts[0])
    normed_keep, normed_send, inverse_first, pre, qkv, attended, squares = call(
        functools.partial(front_kernel, n, r, count),
        [
            (token_half, BF16, ANY),
            (token_half, BF16, ANY),
            ((token_count, 128), F32),
            ((token_count, 3 * width), F32, ANY),
            ((token_count, 3 * width), BF16, ANY),
            (local, F32),
            (row, F32),
        ],
        [
            pltpu.VMEM(full_shape, BF16),
            pltpu.VMEM((model_width, 3 * width), BF16),
            pltpu.VMEM((token_count, 3 * width), F32),
            pltpu.VMEM((token_count, 3 * width), BF16),
            dma((n + r,)),
            dma((r + 2,)),
        ],
        20 * MIB,
        dense // 8,
        MIB,
        (SMEM, idx),
        (SMEM, bounds),
        (SMEM, decay_rate),
        *each(FREE, token_parts),
        *each(ANY, blocks_of("pack", packs[0])),
    )
    attended = clock("O", attended)
    attended = clock("P", attended)
    gate_blocks = blocks_of("gate_pack", packs[1])
    pre_gate, gate_low, *partial = call(
        functools.partial(gate_kernel, n, r),
        [(local, F32), (local, BF16), *with_stat],
        [pltpu.VMEM((model_width, width), BF16), pltpu.VMEM((width, model_width), BF16), dma((r + n,))],
        14 * MIB,
        dense // 8,
        MIB,
        (SMEM, idx),
        *each(VMEM, (normed_keep, normed_send, attended, squares)),
        *each(ANY, gate_blocks),
    )
    own, forward, backward = ring_scatter(partial, "R")
    middle, middle_low, inverse_attn = call(
        functools.partial(middle_kernel, model_width),
        [(local, F32), (local, BF16), (row, F32)],
        [],
        8 * MIB,
        0,
        MIB,
        *each(VMEM, (tokens, squares, own, forward, backward)),
    )
    task(f"A{end}", "normed_swap", "G", lambda: [normed_send], swap)
    middle_parts = ring_gather(middle_low, "A")
    middle_parts[0] = clock("G", middle_parts[0])
    padded = -(-hidden_width // 128) * 128
    grad_parts = side_gathered("dy", cotangent)
    down_blocks = blocks_of("down", down_weight)
    m_keep, m_send, dy_keep, dy_send, lows, inverse_second, second_stat, *partial = call(
        functools.partial(ffn_kernel, n, r, hidden_width),
        [
            *[(token_half, BF16, ANY)] * 4,
            ((token_count, 3 * padded), BF16, ANY),
            ((token_count, 128), F32),
            (row, F32),
            *with_stat,
        ],
        [
            pltpu.VMEM(full_shape, BF16),
            pltpu.VMEM(full_shape, BF16),
            pltpu.VMEM((hidden_width, model_width), BF16),
            pltpu.VMEM((hidden_width, model_width), BF16),
            pltpu.VMEM((hidden_width, model_width), BF16),
            pltpu.VMEM((token_count, 3 * padded), BF16),
            dma((2 * n + 3 * r,)),
            dma((2 * r + 1,)),
        ],
        32 * MIB,
        dense // 8,
        MIB,
        (SMEM, idx),
        *each(FREE, middle_parts),
        *each(FREE, grad_parts),
        *each(ANY, (*blocks_of("first", first_across), *blocks_of("second", second_across), *down_blocks)),
    )

    def weight_grads(columns, flipped):
        def work(act, act_other, low, low_other):
            shapes = [(w, block) if flipped else (block, w) for _, w in columns]
            return call(
                functools.partial(weight_grad_kernel, y_size, columns, flipped),
                [(shape, BF16 if dy else F32) for shape in shapes for dy in range(y_size)],
                [],
                14 * MIB,
                4 * token_count * block * y_size * sum(w for _, w in columns),
                8 * MIB,
                *each(VMEM, (act, act_other, low, low_other)),
            )

        return work

    task("Q0", "dy_swap", "Q1", lambda: [dy_send], swap)
    task("Q0", "lows_swap", "Q1", lambda: [lows], swap)
    task(
        "Q0",
        "ffn_parts",
        "Q1",
        lambda: [lows],
        lambda low: call(
            functools.partial(down_kernel, n, r, hidden_width),
            [(local, F32), *[(local, BF16)] * (n - 1)],
            [pltpu.VMEM((hidden_width, model_width), BF16), dma((r,))],
            14 * MIB,
            2 * token_count * model_width * hidden_width,
            8 * MIB,
            (SMEM, idx),
            (VMEM, low),
            *each(ANY, down_blocks),
        ),
    )
    task("Q1", "m_swap", "Q2", lambda: [m_send], swap)
    for slot, until, name, act, other, at in (
        ("Q1", "Q2", "down", dy_keep, "dy_swap", 0),
        ("Q2", f"Q{end}", "first", m_keep, "m_swap", padded),
        (f"Q{end}", "B0", "second", m_keep, "m_swap", 2 * padded),
    ):
        task(
            slot,
            name + "_grad",
            until,
            lambda act=act, other=other: [act, done[other], lows, done["lows_swap"]],
            weight_grads([(at, hidden_width)], True),
        )
    send_y("down_sent", "down_grad", 0, "Q2", "B0")
    send_y("first_sent", "first_grad", 0, "B0", "B2")
    send_y("second_sent", "second_grad", 0, "B2", "N0")
    side_scatter(
        "ffn",
        "ffn_parts",
        [(f"Q{end}", "B0"), (f"B{end}", "K"), ("K", "N0"), (f"N{end}", "E")],
        [("Q2", f"Q{end}"), ("K", "N0"), (f"N{end}", "E")],
    )
    own, forward, backward = ring_scatter(partial, "Q")
    low_rows = -(-stat_rows // 16) * 16
    middle_grad, middle_grad_low = call(
        functools.partial(middle_grad_kernel, model_width),
        [(local, F32), ((token_count + low_rows, width), BF16)],
        [],
        8 * MIB,
        0,
        MIB,
        *each(VMEM, (cotangent, tokens, middle, middle_low, inverse_second, second_stat, own, forward, backward)),
    )
    branch_parts = ring_gather(middle_grad_low, "B")
    branch_parts[0] = clock("K", branch_parts[0])
    br_keep, br_send, proj, first_stat, *partial = call(
        functools.partial(back_kernel, n, r, count, model_width),
        [
            (token_half, BF16, ANY),
            (token_half, BF16, ANY),
            ((token_count, 5 * width), BF16, ANY),
            (row, F32),
            *with_stat,
        ],
        [
            pltpu.VMEM(full_shape, BF16),
            pltpu.VMEM((width, model_width), BF16),
            pltpu.VMEM((model_width, 4 * width), BF16),
            pltpu.VMEM((token_count, 5 * width), BF16),
            pltpu.VMEM((n, low_rows, width), BF16),
            pltpu.VMEM(local, BF16),
            pltpu.VMEM((token_count, HEAD), F32),
            pltpu.VMEM((token_count, HEAD), F32),
            dma((3 * n + 2 * r,)),
            dma((r + 1,)),
        ],
        22 * MIB,
        dense // 8,
        MIB,
        (SMEM, idx),
        (SMEM, bounds),
        (SMEM, decay_rate),
        *each(VMEM, (pre, pre_gate, qkv, attended, inverse_attn)),
        *each(FREE, branch_parts),
        *each(ANY, blocks_of("pack", packs[0])),
        *each(ANY, gate_blocks),
    )
    task("N0", "proj_swap", "N1", lambda: [proj], swap)
    task("N0", "br_swap", "N1", lambda: [br_send], swap)
    task(
        "N1",
        "proj_grad",
        "N2",
        lambda: [normed_keep, done["normed_swap"], proj, done["proj_swap"]],
        weight_grads([(0, 2 * width), (2 * width, 2 * width)], False),
    )
    task(
        "N1",
        "out_grad",
        "N2",
        lambda: [br_keep, done["br_swap"], proj, done["proj_swap"]],
        weight_grads([(4 * width, width)], True),
    )
    for i, (start, until) in enumerate([("N1", f"N{end}"), ("N2", "E")]):
        send_y(f"proj_sent{i}", "proj_grad", i * y_size, start, until)
    send_y("out_sent", "out_grad", 0, f"N{end}", "E")
    own, forward, backward = ring_scatter(partial, "N")
    [token_grad] = call(
        functools.partial(token_grad_kernel, model_width),
        [(local, F32)],
        [],
        8 * MIB,
        0,
        MIB,
        *each(VMEM, (middle_grad, tokens, inverse_first, first_stat, own, forward, backward)),
    )
    token_grad = clock("E", token_grad)
    ffn_total = done["ffn_parts"][0] + done[f"ffn_b{half - 1}"].astype(F32) + done[f"ffn_f{half - 2}"].astype(F32)
    layer_out = (middle + ffn_total).astype(BF16)
    pairs_of_grads = [y_total(f"proj_sent{i}", "proj_grad", i * y_size) for i in range(2)]
    return (
        layer_out,
        token_grad,
        *(pairs_of_grads[i // 2][:, i % 2 * width : (i % 2 + 1) * width] for i in range(4)),
        y_total("out_sent", "out_grad", 0),
        y_total("first_sent", "first_grad", 0).T,
        y_total("second_sent", "second_grad", 0).T,
        y_total("down_sent", "down_grad", 0),
    )


def solution(mesh):
    both, flipped = P("rows", "cols"), P("cols", "rows")
    return jax.shard_map(
        functools.partial(shards, ring_order(mesh), mesh.shape["rows"] // 2),
        mesh=mesh,
        in_specs=(both, both, P("rows", None), P("cols"), both, both, both, both, flipped, both, both, flipped),
        out_specs=(both, both, both, both, both, both, flipped, both, both, flipped),
        check_vma=False,
    )
```

```python
import functools

import jax
import jax.numpy as jnp
import numpy as np
from jax import lax
from jax.experimental import pallas as pl
from jax.experimental.pallas import tpu as pltpu
from jax.sharding import PartitionSpec as P

HEAD = 128
EPSILON = 1e-06
F32, BF16 = jnp.float32, jnp.bfloat16
NN, NT, TN = ((1,), (0,)), ((1,), (1,)), ((0,), (0,))
ANY = pl.BlockSpec(memory_space=pltpu.HBM)
FREE = pl.BlockSpec(memory_space=pl.ANY)
VMEM = pl.BlockSpec(memory_space=pltpu.VMEM)
SMEM = pl.BlockSpec(memory_space=pltpu.SMEM)
MIB = 1 << 20


def dot(left, right, dims):
    return lax.dot_general(left, right, (dims, ((), ())), preferred_element_type=F32)


def silu_slope(values):
    sigmoid_of = jax.nn.sigmoid(values)
    return sigmoid_of * (1.0 + values * (1.0 - sigmoid_of))


def to_row(column):
    return jnp.broadcast_to(column, (column.shape[0], 128)).T[:8]


def to_column(row):
    return jnp.broadcast_to(row[:1], (128, row.shape[1])).T[:, :1]


def tiles(size, step=256):
    return [(at, min(step, size - at)) for at in range(0, size, step)]


class Copies:
    def __init__(self, semaphores):
        self.semaphores, self.started, self.waited = semaphores, [], 0

    def start(self, source, target):
        copy = pltpu.make_async_copy(source, target, self.semaphores.at[len(self.started)])
        copy.start()
        self.started.append(copy)

    def land(self):
        for copy in self.started[self.waited :]:
            copy.wait()
        self.waited = len(self.started)


def span(place, size):
    return pl.ds(pl.multiple_of(place * size, size), size)


def fetch_chunks(copies, chunks, target, places):
    rows, width = target.shape[0], chunks[0].shape[1]
    for chunk, place in zip(chunks, places):
        source = chunk if chunk.shape[0] == rows else chunk.at[:rows]
        copies.start(source, target.at[:, span(place, width)])


def fetch_out(copies, packs, target, places):
    width = target.shape[0]
    for pack, place in zip(packs, places):
        pieces = pack.shape[0] // width
        for p in range(pieces):
            source = pack.at[p * width : (p + 1) * width, width:]
            copies.start(source, target.at[:, span(place * pieces + p, width)])


def fetch_down(copies, packs, columns, target, places):
    for pack, place in zip(packs, places):
        rows = span(place, pack.shape[0]) if not isinstance(place, int) else slice(place * pack.shape[0], (place + 1) * pack.shape[0])
        copies.start(pack.at[:, columns], target.at[rows])


def fetch_across(copies, blocks, target, places):
    for block, place in zip(blocks, places):
        copies.start(block, target.at[:, span(place, block.shape[1])])


def stat_block(row, rows, width, slot):
    pieces = row.shape[1] // width
    at = lax.broadcasted_iota(jnp.int32, (rows, width), 0)
    block = jnp.zeros((rows, width), F32)
    for k in range(pieces):
        value = row[:, k * width : (k + 1) * width]
        high = value.astype(BF16).astype(F32)
        for j, part in enumerate((high, value - high)):
            here = at == slot * 2 * pieces + j * pieces + k
            block = jnp.where(here, jnp.broadcast_to(part, (rows, width)), block)
    return block.astype(BF16)


def stat_total(block, tokens):
    rows, width = block.shape
    pieces = tokens // width
    at = lax.rem(lax.broadcasted_iota(jnp.int32, (rows, width), 0), pieces)
    values = block.astype(F32)
    parts = [jnp.sum(jnp.where(at == k, values, 0.0), axis=0, keepdims=True) for k in range(pieces)]
    return jnp.concatenate(parts, axis=1)


def normalize(array, inverse_out, step=32):
    def some(i, carry):
        rows = pl.ds(pl.multiple_of(i * step, step), step)
        values = array[rows, :].astype(F32)
        inverse = lax.rsqrt(jnp.mean(values * values, axis=1, keepdims=True) + EPSILON)
        array[rows, :] = (values * inverse).astype(BF16)
        inverse_out[rows, :] = jnp.broadcast_to(inverse, (step, inverse_out.shape[1]))
        return carry

    lax.fori_loop(0, array.shape[0] // step, some, 0)


def split_blocks(copies, array, row_places, keep, send):
    block = keep.shape[1] // (len(row_places) // 2)
    for dy in range(len(row_places) // 2):
        for dc, out in ((0, keep), (1, send)):
            copies.start(array.at[:, span(row_places[dy * 2 + dc], block)], out.at[:, dy * block : (dy + 1) * block])


def decay(first, rows, keys, bounds, count, rate):
    t = first + lax.broadcasted_iota(jnp.int32, (rows, keys), 0)
    s = lax.broadcasted_iota(jnp.int32, (rows, keys), 1)
    start = jnp.zeros((rows, keys), jnp.int32)
    for i in range(count):
        start = jnp.where(t >= bounds[i], bounds[i], start)
    distance = (t - s).astype(F32)
    allowed = (s >= start) & (s <= t)
    return jnp.where(allowed, jnp.exp(-rate * jnp.maximum(distance, 0.0)), 0.0)


def pack_kernel(query, key, value, gate, out, first, second, sems):
    copies = Copies(sems)
    width = query.shape[1]
    for p, weight in enumerate((query, key, value)):
        copies.start(weight, first.at[:, p * width : (p + 1) * width])
    copies.start(gate, second.at[:, :width])
    for p in range(out.shape[1] // width):
        at = slice(p * width, (p + 1) * width)
        copies.start(out.at[:, at], second.at[at, width:])
    copies.land()


def front_kernel(n, r, count, idx, bounds, rate, *refs):
    x, weights = refs[:n], refs[n : n + r]
    keep, send, inverse, pre_out, qkv_out, attended, squares, full, w_full, pre, qkv, sems, out_sems = refs[n + r :]
    token_count = full.shape[0]
    width = attended.shape[1]
    row_places = [idx[n + j] for j in range(r)]
    copies, sent = Copies(sems), Copies(out_sems)
    fetch_chunks(copies, x, full, [idx[i] for i in range(n)])
    copies.land()
    fetch_down(copies, weights, slice(0, 3 * width), w_full, row_places)
    normalize(full, inverse)
    split_blocks(sent, full, row_places, keep, send)
    copies.land()
    for p in range(3):
        at = slice(p * width, (p + 1) * width)
        values = dot(full[...], w_full[:, at], NN)
        pre[:, at] = values
        qkv[:, at] = (values * jax.nn.sigmoid(values)).astype(BF16)
    sent.start(pre, pre_out)
    sent.start(qkv, qkv_out)
    block = min(256, token_count)
    for head in range(width // HEAD):
        q, k, v = (slice(p * width + head * HEAD, p * width + (head + 1) * HEAD) for p in range(3))
        for first in range(0, token_count, block):
            keys = first + block
            decays = decay(first, block, keys, bounds, count, rate[head])
            scores = dot(qkv[first:keys, q], qkv[:keys, k], NT)
            mix = (scores * decays).astype(BF16)
            attended[first:keys, head * HEAD : (head + 1) * HEAD] = dot(mix, qkv[:keys, v], NN)
    values = attended[...]
    squares[...] = to_row(jnp.sum(values * values, axis=1, keepdims=True))
    sent.land()


def put_parts(parts, product, stat, n):
    for i, part in enumerate(parts):
        value = product(i)
        tokens, width = value.shape
        part[:tokens] = value.astype(part.dtype)
        if i and stat is not None:
            part[tokens:] = stat_block(stat, part.shape[0] - tokens, width, min(i, n - i) - 1)


def gate_kernel(n, r, idx, keep, send, attended, stat, *refs):
    packs, refs = refs[:r], refs[r:]
    pre_gate, gate_low = refs[:2]
    parts, (w_gate, full, sems) = refs[2 : 2 + n], refs[2 + n :]
    width = attended.shape[1]
    size = w_gate.shape[0] // r
    copies = Copies(sems)
    fetch_down(copies, packs, slice(0, width), w_gate, range(r))
    fetch_out(copies, packs, full, [idx[n + j] for j in range(r)])
    copies.land()
    total = None
    for j in range(r):
        source = (keep, send)[j % 2]
        value = dot(source[:, j // 2 * size : (j // 2 + 1) * size], w_gate[j * size : (j + 1) * size, :], NN)
        total = value if total is None else total + value
    pre_gate[...] = total
    low = (attended[...] * jax.nn.sigmoid(total)).astype(BF16)
    gate_low[...] = low
    put_parts(parts, lambda i: dot(gate_low[...], full[:, span(idx[i], width)], NN), stat[:1], n)


def down_kernel(n, r, depth, idx, low, *refs):
    blocks, parts, (full, sems) = refs[:r], refs[r : r + n], refs[r + n :]
    copies = Copies(sems)
    fetch_across(copies, blocks, full, [idx[n + j] for j in range(r)])
    copies.land()
    width = parts[0].shape[1]
    put_parts(parts, lambda i: dot(low[:, :depth], full[:, span(idx[i], width)], NN), None, n)


def middle_kernel(model_width, tokens, squares, own, forward, backward, middle, middle_low, inverse_row):
    t = tokens.shape[0]
    total = squares[:1] + stat_total(forward[t:], t) + stat_total(backward[t:], t)
    inverse = lax.rsqrt(total / model_width + EPSILON)
    inverse_row[...] = jnp.broadcast_to(inverse, inverse_row.shape)
    summed = own[...] + forward[:t].astype(F32) + backward[:t].astype(F32)
    value = tokens[...].astype(F32) + summed * to_column(inverse)
    middle[...] = value
    middle_low[...] = value.astype(BF16)


def ffn_kernel(n, r, hidden, idx, *refs):
    m, dy, refs = refs[:n], refs[n : 2 * n], refs[2 * n :]
    (w1, w2, wd), refs = (refs[j * r : (j + 1) * r] for j in range(3)), refs[3 * r :]
    m_keep, m_send, dy_keep, dy_send, lows_out, inverse, stat = refs[:7]
    parts, (m_full, dy_full, w1_full, w2_full, wd_full, lows, sems, out_sems) = refs[7 : 7 + n], refs[7 + n :]
    col_places = [idx[i] for i in range(n)]
    row_places = [idx[n + j] for j in range(r)]
    width = m[0].shape[1]
    padded = lows.shape[1] // 3
    copies, sent = Copies(sems), Copies(out_sems)
    fetch_chunks(copies, m, m_full, col_places)
    copies.land()
    fetch_across(copies, w1, w1_full, row_places)
    fetch_across(copies, w2, w2_full, row_places)
    fetch_chunks(copies, dy, dy_full, col_places)
    fetch_across(copies, wd, wd_full, row_places)
    normalize(m_full, inverse)
    split_blocks(sent, m_full, row_places, m_keep, m_send)
    copies.land()
    split_blocks(sent, dy_full, row_places, dy_keep, dy_send)
    total = None
    for first, size in tiles(hidden):
        at = slice(first, first + size)
        act1 = dot(m_full[...], w1_full[at, :], NT)
        act2 = dot(m_full[...], w2_full[at, :], NT)
        grad = dot(dy_full[...], wd_full[at, :], NT)
        product = act1 * act2
        for j, value in enumerate((product, grad * act2, grad * act1)):
            lows[:, j * padded + first : j * padded + first + size] = value.astype(BF16)
        part = jnp.sum(grad * product, axis=1, keepdims=True)
        total = part if total is None else total + part
    if padded > hidden:
        for j in range(3):
            blank = jnp.zeros((lows.shape[0], padded - hidden), BF16)
            lows[:, j * padded + hidden : (j + 1) * padded] = blank
    sent.start(lows, lows_out)
    row = to_row(2.0 * total)
    stat[...] = row

    def product(i):
        at = span(col_places[i], width)
        value = dot(lows[:, padded : padded + hidden], w1_full[:, at], NN)
        return value + dot(lows[:, 2 * padded : 2 * padded + hidden], w2_full[:, at], NN)

    put_parts(parts, product, row[:1], n)
    sent.land()


def middle_grad_kernel(
    model_width, cotangent, tokens, middle, middle_low, inverse, stat, own, forward, backward, grad, grad_low
):
    t = tokens.shape[0]
    inverse_two = inverse[:, :1]
    total = stat[:1] + stat_total(forward[t:], t) + stat_total(backward[t:], t)
    mean = to_column(total / model_width)
    normed = middle_low[...].astype(F32) * inverse_two
    summed = own[...] + forward[:t].astype(F32) + backward[:t].astype(F32)
    value = cotangent[...].astype(F32) + inverse_two * (summed - normed * mean)
    low = value.astype(BF16)
    grad[...] = value
    grad_low[:t] = low
    branch = middle[...] - tokens[...].astype(F32)
    row = to_row(jnp.sum(low.astype(F32) * branch, axis=1, keepdims=True))[:1]
    grad_low[t:] = stat_block(row, grad_low.shape[0] - t, grad_low.shape[1], 0)


def back_kernel(n, r, count, model_width, idx, bounds, rate, pre, pre_gate, qkv, attended, inverse_row, *refs):
    br, packs, gate_packs, refs = refs[:n], refs[n : n + r], refs[n + r : n + 2 * r], refs[n + 2 * r :]
    keep, send, proj_out, next_stat = refs[:4]
    parts, scratch = refs[4 : 4 + n], refs[4 + n :]
    full, wo_full, w_full, proj, stats, att_low, key_sum, value_sum, sems, out_sems = scratch
    col_places = [idx[i] for i in range(n)]
    row_places = [idx[n + j] for j in range(r)]
    token_count = full.shape[0]
    width = wo_full.shape[0]
    copies, sent = Copies(sems), Copies(out_sems)
    fetch_chunks(copies, br, full, col_places)
    extra = stats.shape[1]
    for i in range(n):
        copies.start(br[i].at[token_count:], stats.at[i])
    fetch_out(copies, gate_packs, wo_full, row_places)
    copies.land()
    fetch_down(copies, packs, slice(0, 3 * width), w_full.at[:, : 3 * width], row_places)
    fetch_down(copies, gate_packs, slice(0, width), w_full.at[:, 3 * width :], row_places)
    split_blocks(sent, full, row_places, keep, send)
    gated_grad = dot(full[...], wo_full[...], NT)
    inverse = to_column(inverse_row[...])
    mean = to_column(stat_total(stats[...].reshape(n * extra, width), token_count) / model_width)
    values = pre_gate[...]
    gate = jax.nn.sigmoid(values)
    normed = attended[...] * inverse
    proj[:, 4 * width :] = (normed * gate).astype(BF16)
    inner = gated_grad * gate
    gate_grad = inner * normed * (1.0 - gate)
    proj[:, 3 * width : 4 * width] = gate_grad.astype(BF16)
    att_low[...] = (inverse * (inner - normed * mean)).astype(BF16)
    total = jnp.sum(gate_grad * values, axis=1, keepdims=True)
    block = min(256, token_count)
    for head in range(width // HEAD):
        here = slice(head * HEAD, (head + 1) * HEAD)
        q, k, v = (slice(p * width + head * HEAD, p * width + (head + 1) * HEAD) for p in range(3))
        key_sum[...] = jnp.zeros_like(key_sum)
        value_sum[...] = jnp.zeros_like(value_sum)
        for first in range(0, token_count, block):
            keys = first + block
            rows = slice(first, keys)
            decays = decay(first, block, keys, bounds, count, rate[head])
            scores = dot(qkv[rows, q], qkv[:keys, k], NT)
            mix = (scores * decays).astype(BF16)
            score_grad = dot(att_low[rows, here], qkv[:keys, v], NT)
            raw = (score_grad * decays).astype(BF16)
            query_sum = dot(raw, qkv[:keys, k], NN)
            proj[rows, q] = (query_sum * silu_slope(pre[rows, q])).astype(BF16)
            key_sum[:keys] += dot(raw, qkv[rows, q], TN)
            value_sum[:keys] += dot(mix, att_low[rows, here], TN)
        proj[:, k] = (key_sum[...] * silu_slope(pre[:, k])).astype(BF16)
        proj[:, v] = (value_sum[...] * silu_slope(pre[:, v])).astype(BF16)
    sent.start(proj, proj_out)
    for p in range(3):
        at = slice(p * width, (p + 1) * width)
        total = total + jnp.sum(proj[:, at].astype(F32) * pre[:, at], axis=1, keepdims=True)
    row = to_row(total)
    next_stat[...] = row
    copies.land()
    put_parts(
        parts, lambda i: dot(proj[:, : 4 * width], w_full[span(col_places[i], width), :], NT), row[:1], n
    )
    sent.land()


def token_grad_kernel(model_width, middle_grad, tokens, inverse, stat, own, forward, backward, out):
    t = tokens.shape[0]
    inverse_first = inverse[:, :1]
    total = stat[:1] + stat_total(forward[t:], t) + stat_total(backward[t:], t)
    mean = to_column(total / model_width)
    normed = tokens[...].astype(F32) * inverse_first
    summed = own[...] + forward[:t].astype(F32) + backward[:t].astype(F32)
    out[...] = middle_grad[...] + inverse_first * (summed - normed * mean)


def weight_grad_kernel(y_size, columns, flipped, act, act_other, low, low_other, *outs):
    block = act.shape[1] // y_size
    outs = iter(outs)
    for start, width in columns:
        for dy in range(y_size):
            out = next(outs)
            for first, size in tiles(block if flipped else width):
                if flipped:
                    a = slice(dy * block + first, dy * block + first + size)
                    l = slice(start, start + width)
                    value = dot(low[:, l], act[:, a], TN) + dot(low_other[:, l], act_other[:, a], TN)
                else:
                    a = slice(dy * block, (dy + 1) * block)
                    l = slice(start + first, start + first + size)
                    value = dot(act[:, a], low[:, l], TN) + dot(act_other[:, a], low_other[:, l], TN)
                out[:, first : first + size] = value.astype(out.dtype)


def ring_order(mesh):
    n = mesh.shape["cols"]
    plain = list(range(n))
    try:
        devices = np.moveaxis(mesh.devices, mesh.axis_names.index("cols"), -1)
        devices = devices.reshape(-1, n)[0]
        coords = [tuple(d.coords) for d in devices]
    except (AttributeError, TypeError):
        return plain
    varying = [d for d in range(len(coords[0])) if len({c[d] for c in coords}) > 1]
    if len(varying) != 2:
        return plain
    a, b = varying
    sizes = [len({c[d] for c in coords}) for d in (a, b)]
    if sizes[0] % 2:
        a, b, sizes = b, a, sizes[::-1]
    if sizes[0] % 2 or sizes[0] * sizes[1] != n or sizes[1] < 2:
        return plain
    lows = [min(c[d] for c in coords) for d in (a, b)]
    index = {(c[a] - lows[0], c[b] - lows[1]): i for i, c in enumerate(coords)}
    walk = []
    for i in range(sizes[0]):
        across = range(1, sizes[1])
        walk += [(i, j) for j in (across if i % 2 == 0 else reversed(across))]
    walk += [(i, 0) for i in reversed(range(sizes[0]))]
    if set(walk) != set(index):
        return plain
    return [index[spot] for spot in walk]


def call(kernel, outs, scratch, limit, flops, moved, *args):
    return pl.pallas_call(
        kernel,
        out_shape=[jax.ShapeDtypeStruct(out[0], out[1]) for out in outs],
        in_specs=[spec for spec, _ in args],
        out_specs=[(*out, VMEM)[2] for out in outs],
        scratch_shapes=scratch,
        compiler_params=pltpu.CompilerParams(vmem_limit_bytes=limit),
        cost_estimate=pl.CostEstimate(flops=int(flops), bytes_accessed=int(moved), transcendentals=0),
    )(*[pltpu.with_memory_space_constraint(arg, pltpu.HBM) if spec is ANY else arg for spec, arg in args])


def each(spec, arrays):
    return [(spec, a) for a in arrays]


def shards(cycle, y_size, *args):
    (
        tokens,
        cotangent,
        lengths,
        decay_rate,
        query_weight,
        key_weight,
        value_weight,
        gate_weight,
        out_weight,
        first_weight,
        second_weight,
        down_weight,
    ) = args
    n, r = len(cycle), 2 * y_size
    half = n // 2
    token_count, width = tokens.shape
    model_width = width * n
    block = query_weight.shape[0]
    hidden_width = first_weight.shape[1]
    count = lengths.shape[1]
    dma = pltpu.SemaphoreType.DMA

    ahead = [(cycle[i], cycle[(i + 1) % n]) for i in range(n)]
    back = [(b, a) for a, b in ahead]
    core_swap = [(i, i ^ 1) for i in range(r)]

    def y_shift(by):
        return [(y * 2 + c, (y + by) % y_size * 2 + c) for y in range(y_size) for c in range(2)]

    place = {c: i for i, c in enumerate(cycle)}
    col_table = np.array([[cycle[(place[c] + i) % n] for i in range(n)] for c in range(n)], np.int32)
    row_table = np.array(
        [[((q // 2 + j // 2) % y_size) * 2 + ((q % 2) ^ (j % 2)) for j in range(r)] for q in range(r)], np.int32
    )

    def places_of(lengths):
        idx = jnp.concatenate(
            [
                lax.dynamic_index_in_dim(jnp.asarray(col_table), lax.axis_index("cols"), 0, False),
                lax.dynamic_index_in_dim(jnp.asarray(row_table), lax.axis_index("rows"), 0, False),
            ]
        )
        places = jnp.arange(count, dtype=jnp.int32)
        return idx, jnp.sum(jnp.where(places[None, :] <= places[:, None], lengths[0][None, :], 0), axis=1)

    def cols(array, pairs):
        return lax.ppermute(array, "cols", pairs)

    def swap(array):
        return lax.ppermute(array, "rows", core_swap)

    def add(a, b):
        return (a.astype(F32) + b.astype(F32)).astype(BF16)

    plan, due, done = {}, {}, {}

    def task(slot, name, until, inputs, work):
        plan.setdefault(slot, []).append((name, until, inputs, work))

    def clock(slot, array, backward=None):
        tie = lax.optimization_barrier
        ending = due.pop(slot, [])
        if ending or backward is not None:
            array, backward, results = tie((array, backward, [done[name] for name in ending]))
            done.update(zip(ending, results))
        for name, until, inputs, work in plan.pop(slot, []):
            _, given = tie((array, inputs()))
            done[name] = work(*given)
            due.setdefault(until, []).append(name)
        return array if backward is None else (array, backward)

    def ring_gather(array, letter):
        parts = [array] + [None] * (n - 1)
        forward = backward = array
        for k in range(1, half + 1):
            if k < half:
                forward, backward = clock(f"{letter}{k - 1}", forward, backward)
                parts[k] = backward = cols(backward, back)
            else:
                forward, backward = lax.optimization_barrier((forward, backward))
                forward = clock(f"{letter}{k - 1}", forward)
            parts[n - k] = forward = cols(forward, ahead)
        return parts

    def ring_scatter(parts, letter, long_way=ahead, short_way=back):
        if long_way is back:
            parts = [parts[-i] for i in range(n)]
        forward, backward = parts[half], parts[half + 1]
        for k in range(half - 1):
            forward, backward = clock(f"{letter}{k}", forward, backward)
            forward = add(cols(forward, long_way), parts[half - 1 - k])
            backward = cols(backward, short_way)
            if k < half - 2:
                backward = add(backward, parts[half + 2 + k])
        forward, backward = lax.optimization_barrier((forward, backward))
        forward = cols(clock(f"{letter}{half - 1}", forward), long_way)
        return parts[0], forward, backward

    def spread(spots, count):
        return [spots[min(k, len(spots) - 1)] for k in range(count)]

    def side_gather(name, array, back_spots, ahead_spots):
        for way, pairs, spots in (("b", back, spread(back_spots, half)), ("f", ahead, spread(ahead_spots, half - 1))):
            for k, (start, until) in enumerate(spots, 1):

                def inputs(before=f"{name}_{way}{k - 1}"):
                    return [done.get(before, array)]

                task(start, f"{name}_{way}{k}", until, inputs, functools.partial(cols, pairs=pairs))

    def side_gathered(name, array):
        return [
            array,
            *(done[f"{name}_b{k}"] for k in range(1, half + 1)),
            *(done[f"{name}_f{n - k}"] for k in range(half + 1, n)),
        ]

    def side_scatter(name, parts_name, back_spots, ahead_spots):
        for way, pairs, spots, first, by in (
            ("b", back, spread(back_spots, half), half, 1),
            ("f", ahead, spread(ahead_spots, half - 1), half - 1, -1),
        ):
            for k, (start, until) in enumerate(spots):

                def inputs(k=k, way=way, first=first, by=by):
                    mine = done[parts_name][first + by * k]
                    return [add(done[f"{name}_{way}{k - 1}"], mine) if k else mine]

                task(start, f"{name}_{way}{k}", until, inputs, functools.partial(cols, pairs=pairs))

    def send_y(name, source, first, start, until):
        task(
            start,
            name,
            until,
            lambda: [done[source][first + dy] for dy in range(1, y_size)],
            lambda *a: [lax.ppermute(v, "rows", y_shift(dy)) for dy, v in enumerate(a, 1)],
        )

    def y_total(name, source, first):
        total = done[source][first]
        for value in done[name]:
            total = total + value.astype(F32)
        return total

    first_across, second_across = first_weight.T, second_weight.T
    end = half - 1
    packs = call(
        pack_kernel,
        [((block, 3 * width), BF16, ANY), ((block, 2 * width), BF16, ANY)],
        [dma((4 + block // width,))],
        4 * MIB,
        0,
        MIB,
        *each(ANY, (query_weight, key_weight, value_weight, gate_weight, out_weight)),
    )
    y_gather = lambda a: [lax.ppermute(a, "rows", y_shift(-dy)) for dy in range(1, y_size)]
    for name, pack, y_spot, own_spot, other_spot in (
        ("pack", packs[0], ("T0", f"T{end}"), ("T1", "T2"), (f"T{end}", "F")),
        ("gate_pack", packs[1], ("T2", "O"), ("T2", f"T{end}"), ("O", "P")),
        ("first", first_across, ("F", "R0"), ("T1", "T2"), ("R1", "R2")),
        ("second", second_across, ("R1", f"R{end}"), ("T2", f"T{end}"), (f"R{end}", "A0")),
        ("down", down_weight, (f"R{end}", "A1"), (f"T{end}", "F"), ("A1", "A2")),
    ):
        task(y_spot[0], name + "_y", y_spot[1], lambda pack=pack: [pack], y_gather)
        task(own_spot[0], name + "_own", own_spot[1], lambda pack=pack: [pack], swap)
        task(
            other_spot[0],
            name + "_other",
            other_spot[1],
            lambda name=name: done[name + "_y"],
            lambda *a: [swap(v) for v in a],
        )

    def blocks_of(name, pack):
        blocks = [pack, done[name + "_own"]]
        for a, b in zip(done[name + "_y"], done[name + "_other"]):
            blocks += [a, b]
        return blocks

    side_gather(
        "dy",
        cotangent,
        [(f"T{end}", "F"), ("F", "O"), ("O", "R0"), (f"A{end}", "G")],
        [("F", "O"), ("O", "R0"), (f"R{end}", "A0")],
    )

    token_half = (token_count, model_width // 2)
    local = (token_count, width)
    row = (8, token_count)
    stat_rows = 2 * token_count // width
    with_stat = [(local, F32)] + [((token_count + half * stat_rows, width), BF16)] * (n - 1)
    full_shape = (token_count, model_width)
    dense = token_count * model_width * width

    task("T0", "places", "T1", lambda: [lengths], places_of)
    token_parts = ring_gather(tokens, "T")
    idx, bounds = done["places"]
    token_parts[0] = clock("F", token_parts[0])
    normed_keep, normed_send, inverse_first, pre, qkv, attended, squares = call(
        functools.partial(front_kernel, n, r, count),
        [
            (token_half, BF16, ANY),
            (token_half, BF16, ANY),
            ((token_count, 128), F32),
            ((token_count, 3 * width), F32, ANY),
            ((token_count, 3 * width), BF16, ANY),
            (local, F32),
            (row, F32),
        ],
        [
            pltpu.VMEM(full_shape, BF16),
            pltpu.VMEM((model_width, 3 * width), BF16),
            pltpu.VMEM((token_count, 3 * width), F32),
            pltpu.VMEM((token_count, 3 * width), BF16),
            dma((n + r,)),
            dma((r + 2,)),
        ],
        20 * MIB,
        dense // 8,
        MIB,
        (SMEM, idx),
        (SMEM, bounds),
        (SMEM, decay_rate),
        *each(FREE, token_parts),
        *each(ANY, blocks_of("pack", packs[0])),
    )
    attended = clock("O", attended)
    attended = clock("P", attended)
    gate_blocks = blocks_of("gate_pack", packs[1])
    pre_gate, gate_low, *partial = call(
        functools.partial(gate_kernel, n, r),
        [(local, F32), (local, BF16), *with_stat],
        [pltpu.VMEM((model_width, width), BF16), pltpu.VMEM((width, model_width), BF16), dma((r + n,))],
        14 * MIB,
        dense // 8,
        MIB,
        (SMEM, idx),
        *each(VMEM, (normed_keep, normed_send, attended, squares)),
        *each(ANY, gate_blocks),
    )
    own, forward, backward = ring_scatter(partial, "R", back, ahead)
    middle, middle_low, inverse_attn = call(
        functools.partial(middle_kernel, model_width),
        [(local, F32), (local, BF16), (row, F32)],
        [],
        8 * MIB,
        0,
        MIB,
        *each(VMEM, (tokens, squares, own, forward, backward)),
    )
    task(f"A{end}", "normed_swap", "G", lambda: [normed_send], swap)
    middle_parts = ring_gather(middle_low, "A")
    middle_parts[0] = clock("G", middle_parts[0])
    padded = -(-hidden_width // 128) * 128
    grad_parts = side_gathered("dy", cotangent)
    down_blocks = blocks_of("down", down_weight)
    m_keep, m_send, dy_keep, dy_send, lows, inverse_second, second_stat, *partial = call(
        functools.partial(ffn_kernel, n, r, hidden_width),
        [
            *[(token_half, BF16, ANY)] * 4,
            ((token_count, 3 * padded), BF16, ANY),
            ((token_count, 128), F32),
            (row, F32),
            *with_stat,
        ],
        [
            pltpu.VMEM(full_shape, BF16),
            pltpu.VMEM(full_shape, BF16),
            pltpu.VMEM((hidden_width, model_width), BF16),
            pltpu.VMEM((hidden_width, model_width), BF16),
            pltpu.VMEM((hidden_width, model_width), BF16),
            pltpu.VMEM((token_count, 3 * padded), BF16),
            dma((2 * n + 3 * r,)),
            dma((2 * r + 1,)),
        ],
        32 * MIB,
        dense // 8,
        MIB,
        (SMEM, idx),
        *each(FREE, middle_parts),
        *each(FREE, grad_parts),
        *each(ANY, (*blocks_of("first", first_across), *blocks_of("second", second_across), *down_blocks)),
    )

    def weight_grads(columns, flipped):
        def work(act, act_other, low, low_other):
            shapes = [(w, block) if flipped else (block, w) for _, w in columns]
            return call(
                functools.partial(weight_grad_kernel, y_size, columns, flipped),
                [(shape, BF16 if dy else F32) for shape in shapes for dy in range(y_size)],
                [],
                14 * MIB,
                4 * token_count * block * y_size * sum(w for _, w in columns),
                8 * MIB,
                *each(VMEM, (act, act_other, low, low_other)),
            )

        return work

    task("Q0", "dy_swap", "Q1", lambda: [dy_send], swap)
    task("Q0", "lows_swap", "Q1", lambda: [lows], swap)
    task(
        "Q0",
        "ffn_parts",
        "Q1",
        lambda: [lows],
        lambda low: call(
            functools.partial(down_kernel, n, r, hidden_width),
            [(local, F32), *[(local, BF16)] * (n - 1)],
            [pltpu.VMEM((hidden_width, model_width), BF16), dma((r,))],
            14 * MIB,
            2 * token_count * model_width * hidden_width,
            8 * MIB,
            (SMEM, idx),
            (VMEM, low),
            *each(ANY, down_blocks),
        ),
    )
    task("Q1", "m_swap", "Q2", lambda: [m_send], swap)
    for slot, until, name, act, other, at in (
        ("Q1", "Q2", "down", dy_keep, "dy_swap", 0),
        ("Q2", f"Q{end}", "first", m_keep, "m_swap", padded),
        (f"Q{end}", "B0", "second", m_keep, "m_swap", 2 * padded),
    ):
        task(
            slot,
            name + "_grad",
            until,
            lambda act=act, other=other: [act, done[other], lows, done["lows_swap"]],
            weight_grads([(at, hidden_width)], True),
        )
    send_y("down_sent", "down_grad", 0, "Q2", "B0")
    send_y("first_sent", "first_grad", 0, "B0", "B2")
    send_y("second_sent", "second_grad", 0, "B2", "N0")
    side_scatter(
        "ffn",
        "ffn_parts",
        [(f"B{end}", "K"), ("K", "N0"), (f"N{end}", "E"), ("E", "END")],
        [(f"Q{end}", "B0"), ("K", "N0"), ("E", "END")],
    )
    own, forward, backward = ring_scatter(partial, "Q", back, ahead)
    low_rows = -(-stat_rows // 16) * 16
    middle_grad, middle_grad_low = call(
        functools.partial(middle_grad_kernel, model_width),
        [(local, F32), ((token_count + low_rows, width), BF16)],
        [],
        8 * MIB,
        0,
        MIB,
        *each(VMEM, (cotangent, tokens, middle, middle_low, inverse_second, second_stat, own, forward, backward)),
    )
    branch_parts = ring_gather(middle_grad_low, "B")
    branch_parts[0] = clock("K", branch_parts[0])
    br_keep, br_send, proj, first_stat, *partial = call(
        functools.partial(back_kernel, n, r, count, model_width),
        [
            (token_half, BF16, ANY),
            (token_half, BF16, ANY),
            ((token_count, 5 * width), BF16, ANY),
            (row, F32),
            *with_stat,
        ],
        [
            pltpu.VMEM(full_shape, BF16),
            pltpu.VMEM((width, model_width), BF16),
            pltpu.VMEM((model_width, 4 * width), BF16),
            pltpu.VMEM((token_count, 5 * width), BF16),
            pltpu.VMEM((n, low_rows, width), BF16),
            pltpu.VMEM(local, BF16),
            pltpu.VMEM((token_count, HEAD), F32),
            pltpu.VMEM((token_count, HEAD), F32),
            dma((3 * n + 2 * r,)),
            dma((r + 1,)),
        ],
        22 * MIB,
        dense // 8,
        MIB,
        (SMEM, idx),
        (SMEM, bounds),
        (SMEM, decay_rate),
        *each(VMEM, (pre, pre_gate, qkv, attended, inverse_attn)),
        *each(FREE, branch_parts),
        *each(ANY, blocks_of("pack", packs[0])),
        *each(ANY, gate_blocks),
    )
    task("N0", "proj_swap", "N1", lambda: [proj], swap)
    task("N0", "br_swap", "N1", lambda: [br_send], swap)
    task(
        "N1",
        "proj_grad",
        "N2",
        lambda: [normed_keep, done["normed_swap"], proj, done["proj_swap"]],
        weight_grads([(0, 2 * width), (2 * width, 2 * width)], False),
    )
    task(
        "N1",
        "out_grad",
        "N2",
        lambda: [br_keep, done["br_swap"], proj, done["proj_swap"]],
        weight_grads([(4 * width, width)], True),
    )
    for i, (start, until) in enumerate([("N1", f"N{end}"), ("N2", "END")]):
        send_y(f"proj_sent{i}", "proj_grad", i * y_size, start, until)
    send_y("out_sent", "out_grad", 0, f"N{end}", "END")
    own, forward, backward = ring_scatter(partial, "N")
    forward = clock("E", forward)
    [token_grad] = call(
        functools.partial(token_grad_kernel, model_width),
        [(local, F32)],
        [],
        8 * MIB,
        0,
        MIB,
        *each(VMEM, (middle_grad, tokens, inverse_first, first_stat, own, forward, backward)),
    )
    token_grad = clock("END", token_grad)
    ffn_total = done["ffn_parts"][0] + done[f"ffn_b{half - 1}"].astype(F32) + done[f"ffn_f{half - 2}"].astype(F32)
    layer_out = (middle + ffn_total).astype(BF16)
    pairs_of_grads = [y_total(f"proj_sent{i}", "proj_grad", i * y_size) for i in range(2)]
    return (
        layer_out,
        token_grad,
        *(pairs_of_grads[i // 2][:, i % 2 * width : (i % 2 + 1) * width] for i in range(4)),
        y_total("out_sent", "out_grad", 0),
        y_total("first_sent", "first_grad", 0).T,
        y_total("second_sent", "second_grad", 0).T,
        y_total("down_sent", "down_grad", 0),
    )


def solution(mesh):
    both, flipped = P("rows", "cols"), P("cols", "rows")
    return jax.shard_map(
        functools.partial(shards, ring_order(mesh), mesh.shape["rows"] // 2),
        mesh=mesh,
        in_specs=(both, both, P("rows", None), P("cols"), both, both, both, both, flipped, both, both, flipped),
        out_specs=(both, both, both, both, both, both, flipped, both, both, flipped),
        check_vma=False,
    )
```

```python
import functools

import jax
import jax.numpy as jnp
import numpy as np
from jax import lax
from jax.experimental import pallas as pl
from jax.experimental.pallas import tpu as pltpu
from jax.sharding import PartitionSpec as P

HEAD = 128
EPSILON = 1e-06
F32, BF16 = jnp.float32, jnp.bfloat16
NN, NT, TN = ((1,), (0,)), ((1,), (1,)), ((0,), (0,))
ANY = pl.BlockSpec(memory_space=pltpu.HBM)
FREE = pl.BlockSpec(memory_space=pl.ANY)
VMEM = pl.BlockSpec(memory_space=pltpu.VMEM)
SMEM = pl.BlockSpec(memory_space=pltpu.SMEM)
MIB = 1 << 20


def dot(left, right, dims):
    return lax.dot_general(left, right, (dims, ((), ())), preferred_element_type=F32)


def silu_slope(values):
    sigmoid_of = jax.nn.sigmoid(values)
    return sigmoid_of * (1.0 + values * (1.0 - sigmoid_of))


def to_row(column):
    return jnp.broadcast_to(column, (column.shape[0], 128)).T[:8]


def to_column(row):
    return jnp.broadcast_to(row[:1], (128, row.shape[1])).T[:, :1]


def tiles(size, step=256):
    return [(at, min(step, size - at)) for at in range(0, size, step)]


class Copies:
    def __init__(self, semaphores, first=0):
        self.semaphores, self.first, self.started, self.waited = semaphores, first, [], 0

    def start(self, source, target):
        copy = pltpu.make_async_copy(source, target, self.semaphores.at[self.first + len(self.started)])
        copy.start()
        self.started.append(copy)

    def land(self):
        for copy in self.started[self.waited :]:
            copy.wait()
        self.waited = len(self.started)


def span(place, size):
    return pl.ds(pl.multiple_of(place * size, size), size)


def fetch_chunks(copies, chunks, target, places):
    rows, width = target.shape[0], chunks[0].shape[1]
    for chunk, place in zip(chunks, places):
        source = chunk if chunk.shape[0] == rows else chunk.at[:rows]
        copies.start(source, target.at[:, span(place, width)])


def stat_block(row, rows, width, slot):
    pieces = row.shape[1] // width
    at = lax.broadcasted_iota(jnp.int32, (rows, width), 0)
    block = jnp.zeros((rows, width), F32)
    for k in range(pieces):
        value = row[:, k * width : (k + 1) * width]
        high = value.astype(BF16).astype(F32)
        for j, part in enumerate((high, value - high)):
            here = at == slot * 2 * pieces + j * pieces + k
            block = jnp.where(here, jnp.broadcast_to(part, (rows, width)), block)
    return block.astype(BF16)


def stat_total(block, tokens):
    rows, width = block.shape
    pieces = tokens // width
    at = lax.rem(lax.broadcasted_iota(jnp.int32, (rows, width), 0), pieces)
    values = block.astype(F32)
    parts = [jnp.sum(jnp.where(at == k, values, 0.0), axis=0, keepdims=True) for k in range(pieces)]
    return jnp.concatenate(parts, axis=1)


def by_blocks(array, places, blocks, rows, columns, dims):
    total = None
    for place, block in zip(places, blocks):
        size = block.shape[0 if dims is NN else 1]
        value = dot(array[:, span(place, size)], block[rows, columns], dims)
        total = value if total is None else total + value
    return total


def send_parts(sent, made, parts, places, stat):
    n = len(parts)
    tokens, width = made.shape[1:]
    if stat is not None:
        tokens = stat.shape[1]
        for i in range(1, n):
            made[places[i], tokens:] = stat_block(stat, made.shape[1] - tokens, width, min(i, n - i) - 1)
    for i, part in enumerate(parts):
        rows = part.shape[0]
        sent.start(made.at[places[i], :rows], part)


def inverse_roots(array):
    values = array.astype(F32)
    return lax.rsqrt(jnp.mean(values * values, axis=1, keepdims=True) + EPSILON)


def split_blocks(copies, array, row_places, keep, send):
    block = keep.shape[1] // (len(row_places) // 2)
    for dy in range(len(row_places) // 2):
        for dc, out in ((0, keep), (1, send)):
            copies.start(array.at[:, span(row_places[dy * 2 + dc], block)], out.at[:, dy * block : (dy + 1) * block])


def decay(first, rows, keys, numbers, count, head):
    t = first + lax.broadcasted_iota(jnp.int32, (rows, keys), 0)
    s = lax.broadcasted_iota(jnp.int32, (rows, keys), 1)
    start = jnp.zeros((rows, keys), jnp.int32)
    for i in range(count):
        bound = numbers[i].astype(jnp.int32)
        start = jnp.where(t >= bound, bound, start)
    distance = (t - s).astype(F32)
    allowed = (s >= start) & (s <= t)
    return jnp.where(allowed, jnp.exp(-numbers[count + head] * jnp.maximum(distance, 0.0)), 0.0)


def pack_kernel(query, key, value, gate, out, first, second, sems):
    copies = Copies(sems)
    width = query.shape[1]
    for p, weight in enumerate((query, key, value)):
        copies.start(weight, first.at[:, p * width : (p + 1) * width])
    copies.start(gate, second.at[:, :width])
    for p in range(out.shape[1] // width):
        at = slice(p * width, (p + 1) * width)
        copies.start(out.at[:, at], second.at[at, width:])
    copies.land()


def front_kernel(n, r, count, idx, numbers, *refs):
    x, weights = refs[:n], refs[n : n + r]
    keep, send, inverse, pre_out, qkv_out, attended, squares, full, pre, qkv, sems, out_sems = refs[n + r :]
    token_count = full.shape[0]
    width = attended.shape[1]
    row_places = [idx[n + j] for j in range(r)]
    copies, sent = Copies(sems), Copies(out_sems)
    fetch_chunks(copies, x, full, [idx[i] for i in range(n)])
    copies.land()
    split_blocks(sent, full, row_places, keep, send)
    roots = inverse_roots(full[...])
    inverse[...] = jnp.broadcast_to(roots, inverse.shape)
    for p in range(3):
        at = slice(p * width, (p + 1) * width)
        values = by_blocks(full, row_places, weights, slice(None), at, NN) * roots
        pre[:, at] = values
        qkv[:, at] = (values * jax.nn.sigmoid(values)).astype(BF16)
    sent.start(pre, pre_out)
    sent.start(qkv, qkv_out)
    block = min(256, token_count)
    for head in range(width // HEAD):
        q, k, v = (slice(p * width + head * HEAD, p * width + (head + 1) * HEAD) for p in range(3))
        for first in range(0, token_count, block):
            keys = first + block
            decays = decay(first, block, keys, numbers, count, head)
            scores = dot(qkv[first:keys, q], qkv[:keys, k], NT)
            mix = (scores * decays).astype(BF16)
            attended[first:keys, head * HEAD : (head + 1) * HEAD] = dot(mix, qkv[:keys, v], NN)
    values = attended[...]
    squares[...] = to_row(jnp.sum(values * values, axis=1, keepdims=True))
    sent.land()


def gate_kernel(n, r, idx, keep, send, inverse, attended, stat, *refs):
    packs, pre_gate, parts, (gate_low, made, sems) = refs[:r], refs[r], refs[r + 1 : r + 1 + n], refs[r + 1 + n :]
    token_count, width = attended.shape
    size = packs[0].shape[0]
    pieces = size // width
    sent = Copies(sems)
    total = None
    for j, pack in enumerate(packs):
        source = (keep, send)[j % 2]
        value = dot(source[:, j // 2 * size : (j // 2 + 1) * size], pack[:, :width], NN)
        total = value if total is None else total + value
    total = total * inverse[:, :1]
    pre_gate[...] = total
    gate_low[...] = (attended[...] * jax.nn.sigmoid(total)).astype(BF16)
    for j, pack in enumerate(packs):
        for p in range(pieces):
            value = dot(gate_low[...], pack[p * width : (p + 1) * width, width:], NN)
            made[idx[n + j] * pieces + p, :token_count] = value.astype(BF16)
    send_parts(sent, made, parts, [idx[i] for i in range(n)], stat[:1])
    sent.land()


def down_kernel(n, r, depth, idx, low, *refs):
    blocks, parts, (made, sems) = refs[:r], refs[r : r + n], refs[r + n :]
    width = made.shape[2]
    pieces = blocks[0].shape[1] // width
    sent = Copies(sems)
    for j, block in enumerate(blocks):
        for p in range(pieces):
            value = dot(low[:, :depth], block[:, p * width : (p + 1) * width], NN)
            made[idx[n + j] * pieces + p] = value.astype(BF16)
    send_parts(sent, made, parts, [idx[i] for i in range(n)], None)
    sent.land()


def middle_kernel(model_width, tokens, squares, own, forward, backward, middle, middle_low, inverse_row):
    t = tokens.shape[0]
    total = squares[:1] + stat_total(forward[t:], t) + stat_total(backward[t:], t)
    inverse = lax.rsqrt(total / model_width + EPSILON)
    inverse_row[...] = jnp.broadcast_to(inverse, inverse_row.shape)
    summed = own[...].astype(F32) + forward[:t].astype(F32) + backward[:t].astype(F32)
    value = tokens[...].astype(F32) + summed * to_column(inverse)
    middle[...] = value
    middle_low[...] = value.astype(BF16)


def ffn_kernel(n, r, hidden, idx, *refs):
    m, dy, refs = refs[:n], refs[n : 2 * n], refs[2 * n :]
    (w1, w2, wd), refs = (refs[j * r : (j + 1) * r] for j in range(3)), refs[3 * r :]
    m_keep, m_send, dy_keep, dy_send, lows_out, inverse, stat = refs[:7]
    parts, scratch = refs[7 : 7 + n], refs[7 + n :]
    m_full, dy_full, act1, act2, lows, made, sems, out_sems = scratch
    col_places = [idx[i] for i in range(n)]
    row_places = [idx[n + j] for j in range(r)]
    width = m[0].shape[1]
    padded = lows.shape[1] // 3
    copies, second, sent = Copies(sems), Copies(sems, n), Copies(out_sems)
    fetch_chunks(copies, m, m_full, col_places)
    fetch_chunks(second, dy, dy_full, col_places)
    copies.land()
    split_blocks(sent, m_full, row_places, m_keep, m_send)
    roots = inverse_roots(m_full[...])
    inverse[...] = jnp.broadcast_to(roots, inverse.shape)
    spans = [slice(first, first + size) for first, size in tiles(hidden)]
    for at in spans:
        act1[:, at] = by_blocks(m_full, row_places, w1, at, slice(None), NT) * roots
        act2[:, at] = by_blocks(m_full, row_places, w2, at, slice(None), NT) * roots
        lows[:, at] = (act1[:, at] * act2[:, at]).astype(BF16)
    second.land()
    split_blocks(sent, dy_full, row_places, dy_keep, dy_send)
    total = None
    for at in spans:
        grad = by_blocks(dy_full, row_places, wd, at, slice(None), NT)
        part = jnp.sum(grad * act1[:, at] * act2[:, at], axis=1, keepdims=True)
        total = part if total is None else total + part
        grad = grad * roots
        for j, act in ((1, act2), (2, act1)):
            lows[:, j * padded + at.start : j * padded + at.stop] = (grad * act[:, at]).astype(BF16)
    if padded > hidden:
        for j in range(3):
            blank = jnp.zeros((lows.shape[0], padded - hidden), BF16)
            lows[:, j * padded + hidden : (j + 1) * padded] = blank
    sent.start(lows, lows_out)
    row = to_row(2.0 * total)
    stat[...] = row

    pieces = w1[0].shape[1] // width
    for j, place in enumerate(row_places):
        for p in range(pieces):
            at = slice(p * width, (p + 1) * width)
            value = dot(lows[:, padded : padded + hidden], w1[j][:, at], NN)
            value = value + dot(lows[:, 2 * padded : 2 * padded + hidden], w2[j][:, at], NN)
            made[place * pieces + p, : m_full.shape[0]] = value.astype(BF16)
    send_parts(sent, made, parts, col_places, row[:1])
    sent.land()


def middle_grad_kernel(
    model_width, cotangent, tokens, middle, middle_low, inverse, stat, own, forward, backward, grad, grad_low
):
    t = tokens.shape[0]
    inverse_two = inverse[:, :1]
    total = stat[:1] + stat_total(forward[t:], t) + stat_total(backward[t:], t)
    mean = to_column(total / model_width)
    normed = middle_low[...].astype(F32) * inverse_two
    summed = own[...].astype(F32) + forward[:t].astype(F32) + backward[:t].astype(F32)
    value = cotangent[...].astype(F32) + (summed - inverse_two * normed * mean)
    low = value.astype(BF16)
    grad[...] = value
    grad_low[:t] = low
    branch = middle[...] - tokens[...].astype(F32)
    row = to_row(jnp.sum(low.astype(F32) * branch, axis=1, keepdims=True))[:1]
    grad_low[t:] = stat_block(row, grad_low.shape[0] - t, grad_low.shape[1], 0)


def back_kernel(n, r, count, model_width, idx, numbers, pre, pre_gate, qkv, attended, inverse_row, first_inverse, *refs):
    br, packs, gate_packs, refs = refs[:n], refs[n : n + r], refs[n + r : n + 2 * r], refs[n + 2 * r :]
    keep, send, proj_out, next_stat = refs[:4]
    parts, scratch = refs[4 : 4 + n], refs[4 + n :]
    full, proj, stats, att_low, key_sum, value_sum, totals, made, sems, out_sems = scratch
    col_places = [idx[i] for i in range(n)]
    row_places = [idx[n + j] for j in range(r)]
    token_count, width = attended.shape
    pieces = packs[0].shape[0] // width
    copies, sent = Copies(sems), Copies(out_sems)
    fetch_chunks(copies, br, full, col_places)
    extra = stats.shape[1]
    for i in range(n):
        copies.start(br[i].at[token_count:], stats.at[i])
    copies.land()
    split_blocks(sent, full, row_places, keep, send)
    gated_grad = None
    for j, place in enumerate(row_places):
        for p in range(pieces):
            piece = gate_packs[j][p * width : (p + 1) * width, width:]
            value = dot(full[:, span(place * pieces + p, width)], piece, NT)
            gated_grad = value if gated_grad is None else gated_grad + value
    inverse = to_column(inverse_row[...])
    mean = to_column(stat_total(stats[...].reshape(n * extra, width), token_count) / model_width)
    roots = first_inverse[:, :1]
    values = pre_gate[...]
    gate = jax.nn.sigmoid(values)
    normed = attended[...] * inverse
    proj[:, 4 * width :] = (normed * gate).astype(BF16)
    inner = gated_grad * gate
    gate_grad = inner * normed * (1.0 - gate)
    proj[:, 3 * width : 4 * width] = (gate_grad * roots).astype(BF16)
    att_low[...] = (inverse * (inner - normed * mean)).astype(BF16)
    totals[...] = jnp.broadcast_to(jnp.sum(gate_grad * values, axis=1, keepdims=True), totals.shape)
    block = min(256, token_count)
    for head in range(width // HEAD):
        here = slice(head * HEAD, (head + 1) * HEAD)
        q, k, v = (slice(p * width + head * HEAD, p * width + (head + 1) * HEAD) for p in range(3))
        key_sum[...] = jnp.zeros_like(key_sum)
        value_sum[...] = jnp.zeros_like(value_sum)
        for first in range(0, token_count, block):
            keys = first + block
            rows = slice(first, keys)
            decays = decay(first, block, keys, numbers, count, head)
            scores = dot(qkv[rows, q], qkv[:keys, k], NT)
            mix = (scores * decays).astype(BF16)
            score_grad = dot(att_low[rows, here], qkv[:keys, v], NT)
            raw = (score_grad * decays).astype(BF16)
            query_sum = dot(raw, qkv[:keys, k], NN)
            query_grad = query_sum * silu_slope(pre[rows, q])
            totals[rows] += jnp.sum(query_grad * pre[rows, q], axis=1, keepdims=True)
            proj[rows, q] = (query_grad * roots[rows]).astype(BF16)
            key_sum[:keys] += dot(raw, qkv[rows, q], TN)
            value_sum[:keys] += dot(mix, att_low[rows, here], TN)
        for at, summed in ((k, key_sum), (v, value_sum)):
            grad = summed[...] * silu_slope(pre[:, at])
            totals[...] += jnp.sum(grad * pre[:, at], axis=1, keepdims=True)
            proj[:, at] = (grad * roots).astype(BF16)
    sent.start(proj, proj_out)
    row = to_row(totals[:, :1])
    next_stat[...] = row
    for j, place in enumerate(row_places):
        for p in range(pieces):
            at = slice(p * width, (p + 1) * width)
            value = dot(proj[:, : 3 * width], packs[j][at, :], NT)
            value = value + dot(proj[:, 3 * width : 4 * width], gate_packs[j][at, :width], NT)
            made[place * pieces + p, :token_count] = value.astype(BF16)
    send_parts(sent, made, parts, col_places, row[:1])
    sent.land()


def token_grad_kernel(model_width, middle_grad, tokens, inverse, stat, own, forward, backward, out):
    t = tokens.shape[0]
    inverse_first = inverse[:, :1]
    total = stat[:1] + stat_total(forward[t:], t) + stat_total(backward[t:], t)
    mean = to_column(total / model_width)
    normed = tokens[...].astype(F32) * inverse_first
    summed = own[...].astype(F32) + forward[:t].astype(F32) + backward[:t].astype(F32)
    out[...] = middle_grad[...] + (summed - inverse_first * normed * mean)


def weight_grad_kernel(y_size, columns, flipped, act, act_other, low, low_other, *outs):
    block = act.shape[1] // y_size
    outs = iter(outs)
    for start, width in columns:
        for dy in range(y_size):
            out = next(outs)
            for first, size in tiles(block if flipped else width):
                if flipped:
                    a = slice(dy * block + first, dy * block + first + size)
                    l = slice(start, start + width)
                    value = dot(low[:, l], act[:, a], TN) + dot(low_other[:, l], act_other[:, a], TN)
                else:
                    a = slice(dy * block, (dy + 1) * block)
                    l = slice(start + first, start + first + size)
                    value = dot(act[:, a], low[:, l], TN) + dot(act_other[:, a], low_other[:, l], TN)
                out[:, first : first + size] = value.astype(out.dtype)


def ring_order(mesh):
    n = mesh.shape["cols"]
    plain = list(range(n))
    try:
        devices = np.moveaxis(mesh.devices, mesh.axis_names.index("cols"), -1)
        devices = devices.reshape(-1, n)[0]
        coords = [tuple(d.coords) for d in devices]
    except (AttributeError, TypeError):
        return plain
    varying = [d for d in range(len(coords[0])) if len({c[d] for c in coords}) > 1]
    if len(varying) != 2:
        return plain
    a, b = varying
    sizes = [len({c[d] for c in coords}) for d in (a, b)]
    if sizes[0] % 2:
        a, b, sizes = b, a, sizes[::-1]
    if sizes[0] % 2 or sizes[0] * sizes[1] != n or sizes[1] < 2:
        return plain
    lows = [min(c[d] for c in coords) for d in (a, b)]
    index = {(c[a] - lows[0], c[b] - lows[1]): i for i, c in enumerate(coords)}
    walk = []
    for i in range(sizes[0]):
        across = range(1, sizes[1])
        walk += [(i, j) for j in (across if i % 2 == 0 else reversed(across))]
    walk += [(i, 0) for i in reversed(range(sizes[0]))]
    if set(walk) != set(index):
        return plain
    return [index[spot] for spot in walk]


def call(kernel, outs, scratch, limit, flops, moved, *args):
    return pl.pallas_call(
        kernel,
        out_shape=[jax.ShapeDtypeStruct(out[0], out[1]) for out in outs],
        in_specs=[spec for spec, _ in args],
        out_specs=[(*out, VMEM)[2] for out in outs],
        scratch_shapes=scratch,
        compiler_params=pltpu.CompilerParams(vmem_limit_bytes=limit),
        cost_estimate=pl.CostEstimate(flops=int(flops), bytes_accessed=int(moved), transcendentals=0),
    )(*[pltpu.with_memory_space_constraint(arg, pltpu.HBM) if spec is ANY else arg for spec, arg in args])


def each(spec, arrays):
    return [(spec, a) for a in arrays]


def shards(cycle, y_size, *args):
    (
        tokens,
        cotangent,
        lengths,
        decay_rate,
        query_weight,
        key_weight,
        value_weight,
        gate_weight,
        out_weight,
        first_weight,
        second_weight,
        down_weight,
    ) = args
    n, r = len(cycle), 2 * y_size
    half = n // 2
    token_count, width = tokens.shape
    model_width = width * n
    block = query_weight.shape[0]
    hidden_width = first_weight.shape[1]
    count = lengths.shape[1]
    dma = pltpu.SemaphoreType.DMA

    ahead = [(cycle[i], cycle[(i + 1) % n]) for i in range(n)]
    back = [(b, a) for a, b in ahead]
    core_swap = [(i, i ^ 1) for i in range(r)]

    def y_shift(by):
        return [(y * 2 + c, (y + by) % y_size * 2 + c) for y in range(y_size) for c in range(2)]

    place = {c: i for i, c in enumerate(cycle)}
    col_table = np.array([[cycle[(place[c] + i) % n] for i in range(n)] for c in range(n)], np.int32)
    row_table = np.array(
        [[((q // 2 + j // 2) % y_size) * 2 + ((q % 2) ^ (j % 2)) for j in range(r)] for q in range(r)], np.int32
    )

    def places_of(lengths, rates):
        idx = jnp.concatenate(
            [
                lax.dynamic_index_in_dim(jnp.asarray(col_table), lax.axis_index("cols"), 0, False),
                lax.dynamic_index_in_dim(jnp.asarray(row_table), lax.axis_index("rows"), 0, False),
            ]
        )
        places = jnp.arange(count, dtype=jnp.int32)
        bounds = jnp.sum(jnp.where(places[None, :] <= places[:, None], lengths[0][None, :], 0), axis=1)
        return idx, jnp.concatenate([bounds.astype(F32), rates])

    def cols(array, pairs):
        return lax.ppermute(array, "cols", pairs)

    def swap(array):
        return lax.ppermute(array, "rows", core_swap)

    def add(a, b):
        return (a.astype(F32) + b.astype(F32)).astype(BF16)

    plan, due, done = {}, {}, {}

    def task(slot, name, until, inputs, work):
        plan.setdefault(slot, []).append((name, until, inputs, work))

    def clock(slot, array, backward=None):
        tie = lax.optimization_barrier
        ending = due.pop(slot, [])
        if ending or backward is not None:
            array, backward, results = tie((array, backward, [done[name] for name in ending]))
            done.update(zip(ending, results))
        for name, until, inputs, work in plan.pop(slot, []):
            _, given = tie((array, inputs()))
            done[name] = work(*given)
            due.setdefault(until, []).append(name)
        return array if backward is None else (array, backward)

    def ring_gather(array, letter):
        parts = [array] + [None] * (n - 1)
        forward = backward = array
        for k in range(1, half + 1):
            if k < half:
                forward, backward = clock(f"{letter}{k - 1}", forward, backward)
                parts[k] = backward = cols(backward, back)
            else:
                forward, backward = lax.optimization_barrier((forward, backward))
                forward = clock(f"{letter}{k - 1}", forward)
            parts[n - k] = forward = cols(forward, ahead)
        return parts

    def ring_scatter(parts, letter, long_way=ahead, short_way=back):
        if long_way is back:
            parts = [parts[-i] for i in range(n)]
        forward, backward = parts[half], parts[half + 1]
        for k in range(half - 1):
            forward, backward = clock(f"{letter}{k}", forward, backward)
            forward = add(cols(forward, long_way), parts[half - 1 - k])
            backward = cols(backward, short_way)
            if k < half - 2:
                backward = add(backward, parts[half + 2 + k])
        forward, backward = lax.optimization_barrier((forward, backward))
        forward = cols(clock(f"{letter}{half - 1}", forward), long_way)
        return parts[0], forward, backward

    def spread(spots, count):
        return [spots[min(k, len(spots) - 1)] for k in range(count)]

    def side_gather(name, array, back_spots, ahead_spots):
        for way, pairs, spots in (("b", back, spread(back_spots, half)), ("f", ahead, spread(ahead_spots, half - 1))):
            for k, (start, until) in enumerate(spots, 1):

                def inputs(before=f"{name}_{way}{k - 1}"):
                    return [done.get(before, array)]

                task(start, f"{name}_{way}{k}", until, inputs, functools.partial(cols, pairs=pairs))

    def side_gathered(name, array):
        return [
            array,
            *(done[f"{name}_b{k}"] for k in range(1, half + 1)),
            *(done[f"{name}_f{n - k}"] for k in range(half + 1, n)),
        ]

    def side_scatter(name, parts_name, back_spots, ahead_spots):
        for way, pairs, spots, first, by in (
            ("b", back, spread(back_spots, half), half, 1),
            ("f", ahead, spread(ahead_spots, half - 1), half - 1, -1),
        ):
            for k, (start, until) in enumerate(spots):

                def inputs(k=k, way=way, first=first, by=by):
                    mine = done[parts_name][first + by * k]
                    return [add(done[f"{name}_{way}{k - 1}"], mine) if k else mine]

                task(start, f"{name}_{way}{k}", until, inputs, functools.partial(cols, pairs=pairs))

    def send_y(name, source, first, start, until):
        task(
            start,
            name,
            until,
            lambda: [done[source][first + dy] for dy in range(1, y_size)],
            lambda *a: [lax.ppermute(v, "rows", y_shift(dy)) for dy, v in enumerate(a, 1)],
        )

    def y_total(name, source, first):
        total = done[source][first]
        for value in done[name]:
            total = total + value.astype(F32)
        return total

    first_across, second_across = first_weight.T, second_weight.T
    end = half - 1
    packs = call(
        pack_kernel,
        [((block, 3 * width), BF16, ANY), ((block, 2 * width), BF16, ANY)],
        [dma((4 + block // width,))],
        4 * MIB,
        0,
        MIB,
        *each(ANY, (query_weight, key_weight, value_weight, gate_weight, out_weight)),
    )
    y_gather = lambda a: [lax.ppermute(a, "rows", y_shift(-dy)) for dy in range(1, y_size)]
    for name, pack, y_spot, own_spot, other_spot in (
        ("pack", packs[0], ("T0", f"T{end}"), ("T1", "T2"), (f"T{end}", "F")),
        ("gate_pack", packs[1], ("T2", "O"), ("T2", f"T{end}"), ("O", "P")),
        ("first", first_across, ("F", "R0"), ("T1", "T2"), ("R1", "R2")),
        ("second", second_across, ("R1", f"R{end}"), ("T2", f"T{end}"), (f"R{end}", "A0")),
        ("down", down_weight, (f"R{end}", "A1"), (f"T{end}", "F"), ("A1", "A2")),
    ):
        task(y_spot[0], name + "_y", y_spot[1], lambda pack=pack: [pack], y_gather)
        task(own_spot[0], name + "_own", own_spot[1], lambda pack=pack: [pack], swap)
        task(
            other_spot[0],
            name + "_other",
            other_spot[1],
            lambda name=name: done[name + "_y"],
            lambda *a: [swap(v) for v in a],
        )

    def blocks_of(name, pack):
        blocks = [pack, done[name + "_own"]]
        for a, b in zip(done[name + "_y"], done[name + "_other"]):
            blocks += [a, b]
        return blocks

    side_gather(
        "dy",
        cotangent,
        [(f"T{end}", "F"), ("F", "O"), ("O", "R0"), (f"A{end}", "G")],
        [("F", "O"), ("O", "R0"), (f"R{end}", "A0")],
    )

    token_half = (token_count, model_width // 2)
    local = (token_count, width)
    row = (8, token_count)
    stat_rows = 2 * token_count // width
    high = token_count + half * stat_rows
    with_stat = [(local, BF16, ANY)] + [((high, width), BF16, ANY)] * (n - 1)
    full_shape = (token_count, model_width)
    dense = token_count * model_width * width

    task("T0", "places", "T1", lambda: [lengths, decay_rate], places_of)
    token_parts = ring_gather(tokens, "T")
    idx, numbers = done["places"]
    token_parts[0] = clock("F", token_parts[0])
    tokens_keep, tokens_send, inverse_first, pre, qkv, attended, squares = call(
        functools.partial(front_kernel, n, r, count),
        [
            (token_half, BF16, ANY),
            (token_half, BF16, ANY),
            ((token_count, 128), F32),
            ((token_count, 3 * width), F32, ANY),
            ((token_count, 3 * width), BF16, ANY),
            (local, F32),
            (row, F32),
        ],
        [
            pltpu.VMEM(full_shape, BF16),
            pltpu.VMEM((token_count, 3 * width), F32),
            pltpu.VMEM((token_count, 3 * width), BF16),
            dma((n,)),
            dma((r + 2,)),
        ],
        14 * MIB,
        dense // 8,
        MIB,
        (SMEM, idx),
        (SMEM, numbers),
        *each(FREE, token_parts),
        *each(VMEM, blocks_of("pack", packs[0])),
    )
    attended = clock("O", attended)
    attended = clock("P", attended)
    gate_blocks = blocks_of("gate_pack", packs[1])
    pre_gate, *partial = call(
        functools.partial(gate_kernel, n, r),
        [(local, F32), *with_stat],
        [pltpu.VMEM(local, BF16), pltpu.VMEM((n, high, width), BF16), dma((n,))],
        14 * MIB,
        dense // 8,
        MIB,
        (SMEM, idx),
        *each(VMEM, (tokens_keep, tokens_send, inverse_first, attended, squares)),
        *each(VMEM, gate_blocks),
    )
    own, forward, backward = ring_scatter(partial, "R", back, ahead)
    middle, middle_low, inverse_attn = call(
        functools.partial(middle_kernel, model_width),
        [(local, F32), (local, BF16), (row, F32)],
        [],
        8 * MIB,
        0,
        MIB,
        *each(VMEM, (tokens, squares, own, forward, backward)),
    )
    task(f"A{end}", "tokens_swap", "G", lambda: [tokens_send], swap)
    middle_parts = ring_gather(middle_low, "A")
    middle_parts[0] = clock("G", middle_parts[0])
    padded = -(-hidden_width // 128) * 128
    grad_parts = side_gathered("dy", cotangent)
    down_blocks = blocks_of("down", down_weight)
    m_keep, m_send, dy_keep, dy_send, lows, inverse_second, second_stat, *partial = call(
        functools.partial(ffn_kernel, n, r, hidden_width),
        [
            *[(token_half, BF16, ANY)] * 4,
            ((token_count, 3 * padded), BF16, ANY),
            ((token_count, 128), F32),
            (row, F32),
            *with_stat,
        ],
        [
            pltpu.VMEM(full_shape, BF16),
            pltpu.VMEM(full_shape, BF16),
            pltpu.VMEM((token_count, hidden_width), F32),
            pltpu.VMEM((token_count, hidden_width), F32),
            pltpu.VMEM((token_count, 3 * padded), BF16),
            pltpu.VMEM((n, high, width), BF16),
            dma((2 * n,)),
            dma((2 * r + 1 + n,)),
        ],
        22 * MIB,
        dense // 8,
        MIB,
        (SMEM, idx),
        *each(FREE, middle_parts),
        *each(ANY, grad_parts),
        *each(VMEM, (*blocks_of("first", first_across), *blocks_of("second", second_across), *down_blocks)),
    )

    def weight_grads(columns, flipped):
        def work(act, act_other, low, low_other):
            shapes = [(w, block) if flipped else (block, w) for _, w in columns]
            return call(
                functools.partial(weight_grad_kernel, y_size, columns, flipped),
                [(shape, BF16 if dy else F32) for shape in shapes for dy in range(y_size)],
                [],
                14 * MIB,
                4 * token_count * block * y_size * sum(w for _, w in columns),
                8 * MIB,
                *each(VMEM, (act, act_other, low, low_other)),
            )

        return work

    task("Q0", "dy_swap", "Q1", lambda: [dy_send], swap)
    task("Q0", "lows_swap", "Q1", lambda: [lows], swap)
    task(
        "Q0",
        "ffn_parts",
        "Q1",
        lambda: [lows],
        lambda low: call(
            functools.partial(down_kernel, n, r, hidden_width),
            [(local, BF16, ANY)] * n,
            [pltpu.VMEM((n, *local), BF16), dma((n,))],
            14 * MIB,
            2 * token_count * model_width * hidden_width,
            8 * MIB,
            (SMEM, idx),
            (VMEM, low),
            *each(VMEM, down_blocks),
        ),
    )
    task("Q1", "m_swap", "Q2", lambda: [m_send], swap)
    for slot, until, name, act, other, at in (
        ("Q1", "Q2", "down", dy_keep, "dy_swap", 0),
        ("Q2", f"Q{end}", "first", m_keep, "m_swap", padded),
        (f"Q{end}", "B0", "second", m_keep, "m_swap", 2 * padded),
    ):
        task(
            slot,
            name + "_grad",
            until,
            lambda act=act, other=other: [act, done[other], lows, done["lows_swap"]],
            weight_grads([(at, hidden_width)], True),
        )
    send_y("down_sent", "down_grad", 0, "Q2", "B0")
    send_y("first_sent", "first_grad", 0, "B0", "B2")
    send_y("second_sent", "second_grad", 0, "B2", "N0")
    side_scatter(
        "ffn",
        "ffn_parts",
        [(f"B{end}", "K"), ("K", "N0"), (f"N{end}", "E"), ("E", "END")],
        [(f"Q{end}", "B0"), ("K", "N0"), ("E", "END")],
    )
    own, forward, backward = ring_scatter(partial, "Q", back, ahead)
    low_rows = -(-stat_rows // 16) * 16
    middle_grad, middle_grad_low = call(
        functools.partial(middle_grad_kernel, model_width),
        [(local, F32), ((token_count + low_rows, width), BF16)],
        [],
        8 * MIB,
        0,
        MIB,
        *each(VMEM, (cotangent, tokens, middle, middle_low, inverse_second, second_stat, own, forward, backward)),
    )
    branch_parts = ring_gather(middle_grad_low, "B")
    branch_parts[0] = clock("K", branch_parts[0])
    br_keep, br_send, proj, first_stat, *partial = call(
        functools.partial(back_kernel, n, r, count, model_width),
        [
            (token_half, BF16, ANY),
            (token_half, BF16, ANY),
            ((token_count, 5 * width), BF16, ANY),
            (row, F32),
            *with_stat,
        ],
        [
            pltpu.VMEM(full_shape, BF16),
            pltpu.VMEM((token_count, 5 * width), BF16),
            pltpu.VMEM((n, low_rows, width), BF16),
            pltpu.VMEM(local, BF16),
            pltpu.VMEM((token_count, HEAD), F32),
            pltpu.VMEM((token_count, HEAD), F32),
            pltpu.VMEM((token_count, HEAD), F32),
            pltpu.VMEM((n, high, width), BF16),
            dma((2 * n,)),
            dma((r + 1 + n,)),
        ],
        16 * MIB,
        dense // 8,
        MIB,
        (SMEM, idx),
        (SMEM, numbers),
        *each(VMEM, (pre, pre_gate, qkv, attended, inverse_attn, inverse_first)),
        *each(FREE, branch_parts),
        *each(VMEM, blocks_of("pack", packs[0])),
        *each(VMEM, gate_blocks),
    )
    task("N0", "proj_swap", "N1", lambda: [proj], swap)
    task("N0", "br_swap", "N1", lambda: [br_send], swap)
    for name, act, other, columns, flipped in (
        ("proj_grad", tokens_keep, lambda: done["tokens_swap"], [(0, 2 * width), (2 * width, 2 * width)], False),
        ("out_grad", br_keep, lambda: done["br_swap"], [(4 * width, width)], True),
    ):
        task(
            "N0",
            name,
            "N1",
            lambda act=act, other=other: [act, other(), proj, done["proj_swap"]],
            weight_grads(columns, flipped),
        )
    send_y("proj_sent0", "proj_grad", 0, "N1", f"N{end}")
    send_y("proj_sent1", "proj_grad", y_size, "N2", "END")
    send_y("out_sent", "out_grad", 0, "N2", "END")
    own, forward, backward = ring_scatter(partial, "N")
    forward = clock("E", forward)
    [token_grad] = call(
        functools.partial(token_grad_kernel, model_width),
        [(local, F32)],
        [],
        8 * MIB,
        0,
        MIB,
        *each(VMEM, (middle_grad, tokens, inverse_first, first_stat, own, forward, backward)),
    )
    token_grad = clock("END", token_grad)
    ffn_total = done["ffn_parts"][0].astype(F32) + done[f"ffn_b{half - 1}"].astype(F32) + done[f"ffn_f{half - 2}"].astype(F32)
    layer_out = (middle + ffn_total).astype(BF16)
    pairs_of_grads = [y_total(f"proj_sent{i}", "proj_grad", i * y_size) for i in range(2)]
    return (
        layer_out,
        token_grad,
        *(pairs_of_grads[i // 2][:, i % 2 * width : (i % 2 + 1) * width] for i in range(4)),
        y_total("out_sent", "out_grad", 0),
        y_total("first_sent", "first_grad", 0).T,
        y_total("second_sent", "second_grad", 0).T,
        y_total("down_sent", "down_grad", 0),
    )


def solution(mesh):
    both, flipped = P("rows", "cols"), P("cols", "rows")
    return jax.shard_map(
        functools.partial(shards, ring_order(mesh), mesh.shape["rows"] // 2),
        mesh=mesh,
        in_specs=(both, both, P("rows", None), P("cols"), both, both, both, both, flipped, both, both, flipped),
        out_specs=(both, both, both, both, both, both, flipped, both, both, flipped),
        check_vma=False,
    )
```

```python
import functools

import jax
import jax.numpy as jnp
import numpy as np
from jax import lax
from jax.experimental import pallas as pl
from jax.experimental.pallas import tpu as pltpu
from jax.sharding import PartitionSpec as P

HEAD = 128
EPSILON = 1e-06
F32, BF16 = jnp.float32, jnp.bfloat16
NN, NT, TN = ((1,), (0,)), ((1,), (1,)), ((0,), (0,))
ANY = pl.BlockSpec(memory_space=pltpu.HBM)
FREE = pl.BlockSpec(memory_space=pl.ANY)
VMEM = pl.BlockSpec(memory_space=pltpu.VMEM)
SMEM = pl.BlockSpec(memory_space=pltpu.SMEM)
MIB = 1 << 20


def dot(left, right, dims):
    return lax.dot_general(left, right, (dims, ((), ())), preferred_element_type=F32)


def silu_slope(values):
    sigmoid_of = jax.nn.sigmoid(values)
    return sigmoid_of * (1.0 + values * (1.0 - sigmoid_of))


def to_row(column):
    return jnp.broadcast_to(column, (column.shape[0], 128)).T[:8]


def to_column(row):
    return jnp.broadcast_to(row[:1], (128, row.shape[1])).T[:, :1]


def tiles(size, step=256):
    return [(at, min(step, size - at)) for at in range(0, size, step)]


class Copies:
    def __init__(self, semaphores, first=0):
        self.semaphores, self.first, self.started, self.waited = semaphores, first, [], 0

    def start(self, source, target):
        copy = pltpu.make_async_copy(source, target, self.semaphores.at[self.first + len(self.started)])
        copy.start()
        self.started.append(copy)

    def land(self):
        for copy in self.started[self.waited :]:
            copy.wait()
        self.waited = len(self.started)


def span(place, size):
    return pl.ds(pl.multiple_of(place * size, size), size)


def fetch_chunks(copies, chunks, target, places):
    rows, width = target.shape[0], chunks[0].shape[1]
    for chunk, place in zip(chunks, places):
        source = chunk if chunk.shape[0] == rows else chunk.at[:rows]
        copies.start(source, target.at[:, span(place, width)])


def stat_block(row, rows, width, slot):
    pieces = row.shape[1] // width
    at = lax.broadcasted_iota(jnp.int32, (rows, width), 0)
    block = jnp.zeros((rows, width), F32)
    for k in range(pieces):
        value = row[:, k * width : (k + 1) * width]
        high = value.astype(BF16).astype(F32)
        for j, part in enumerate((high, value - high)):
            here = at == slot * 2 * pieces + j * pieces + k
            block = jnp.where(here, jnp.broadcast_to(part, (rows, width)), block)
    return block.astype(BF16)


def stat_total(block, tokens):
    rows, width = block.shape
    pieces = tokens // width
    at = lax.rem(lax.broadcasted_iota(jnp.int32, (rows, width), 0), pieces)
    values = block.astype(F32)
    parts = [jnp.sum(jnp.where(at == k, values, 0.0), axis=0, keepdims=True) for k in range(pieces)]
    return jnp.concatenate(parts, axis=1)


def by_blocks(array, places, blocks, rows, columns, dims):
    total = None
    for place, block in zip(places, blocks):
        size = block.shape[0 if dims is NN else 1]
        value = dot(array[:, span(place, size)], block[rows, columns], dims)
        total = value if total is None else total + value
    return total


def send_parts(sent, made, parts, places, stat):
    n = len(parts)
    tokens, width = made.shape[1:]
    if stat is not None:
        tokens = stat.shape[1]
        for i in range(1, n):
            made[places[i], tokens:] = stat_block(stat, made.shape[1] - tokens, width, min(i, n - i) - 1)
    for i, part in enumerate(parts):
        rows = part.shape[0]
        sent.start(made.at[places[i], :rows], part)


def inverse_roots(array):
    values = array.astype(F32)
    return lax.rsqrt(jnp.mean(values * values, axis=1, keepdims=True) + EPSILON)


def split_blocks(copies, array, row_places, keep, send):
    block = keep.shape[1] // (len(row_places) // 2)
    for dy in range(len(row_places) // 2):
        for dc, out in ((0, keep), (1, send)):
            copies.start(array.at[:, span(row_places[dy * 2 + dc], block)], out.at[:, dy * block : (dy + 1) * block])


def decay(first, rows, keys, numbers, count, head):
    t = first + lax.broadcasted_iota(jnp.int32, (rows, keys), 0)
    s = lax.broadcasted_iota(jnp.int32, (rows, keys), 1)
    start = jnp.zeros((rows, keys), jnp.int32)
    for i in range(count):
        bound = numbers[i].astype(jnp.int32)
        start = jnp.where(t >= bound, bound, start)
    distance = (t - s).astype(F32)
    allowed = (s >= start) & (s <= t)
    return jnp.where(allowed, jnp.exp(-numbers[count + head] * jnp.maximum(distance, 0.0)), 0.0)


def pack_kernel(query, key, value, gate, out, first, second, sems):
    copies = Copies(sems)
    width = query.shape[1]
    for p, weight in enumerate((query, key, value)):
        copies.start(weight, first.at[:, p * width : (p + 1) * width])
    copies.start(gate, second.at[:, :width])
    for p in range(out.shape[1] // width):
        at = slice(p * width, (p + 1) * width)
        copies.start(out.at[:, at], second.at[at, width:])
    copies.land()


def front_kernel(n, r, count, idx, numbers, *refs):
    x, weights = refs[:n], refs[n : n + r]
    keep, send, inverse, pre_out, qkv_out, attended, squares, full, pre, qkv, sems, out_sems = refs[n + r :]
    token_count = full.shape[0]
    width = attended.shape[1]
    row_places = [idx[n + j] for j in range(r)]
    copies, sent = Copies(sems), Copies(out_sems)
    fetch_chunks(copies, x, full, [idx[i] for i in range(n)])
    copies.land()
    split_blocks(sent, full, row_places, keep, send)
    roots = inverse_roots(full[...])
    inverse[...] = jnp.broadcast_to(roots, inverse.shape)
    for p in range(3):
        at = slice(p * width, (p + 1) * width)
        values = by_blocks(full, row_places, weights, slice(None), at, NN) * roots
        pre[:, at] = values
        qkv[:, at] = (values * jax.nn.sigmoid(values)).astype(BF16)
    sent.start(pre, pre_out)
    sent.start(qkv, qkv_out)
    block = min(256, token_count)
    for head in range(width // HEAD):
        q, k, v = (slice(p * width + head * HEAD, p * width + (head + 1) * HEAD) for p in range(3))
        for first in range(0, token_count, block):
            keys = first + block
            decays = decay(first, block, keys, numbers, count, head)
            scores = dot(qkv[first:keys, q], qkv[:keys, k], NT)
            mix = (scores * decays).astype(BF16)
            attended[first:keys, head * HEAD : (head + 1) * HEAD] = dot(mix, qkv[:keys, v], NN)
    values = attended[...]
    squares[...] = to_row(jnp.sum(values * values, axis=1, keepdims=True))
    sent.land()


def gate_kernel(n, r, idx, keep, send, inverse, attended, stat, *refs):
    packs, pre_gate, parts, (gate_low, made, sems) = refs[:r], refs[r], refs[r + 1 : r + 1 + n], refs[r + 1 + n :]
    token_count, width = attended.shape
    size = packs[0].shape[0]
    pieces = size // width
    sent = Copies(sems)
    total = None
    for j, pack in enumerate(packs):
        source = (keep, send)[j % 2]
        value = dot(source[:, j // 2 * size : (j // 2 + 1) * size], pack[:, :width], NN)
        total = value if total is None else total + value
    total = total * inverse[:, :1]
    pre_gate[...] = total
    gate_low[...] = (attended[...] * jax.nn.sigmoid(total)).astype(BF16)
    for j, pack in enumerate(packs):
        for p in range(pieces):
            value = dot(gate_low[...], pack[p * width : (p + 1) * width, width:], NN)
            made[idx[n + j] * pieces + p, :token_count] = value.astype(BF16)
    send_parts(sent, made, parts, [idx[i] for i in range(n)], stat[:1])
    sent.land()


def down_kernel(n, r, depth, idx, low, *refs):
    blocks, parts, (made, sems) = refs[:r], refs[r : r + n], refs[r + n :]
    width = made.shape[2]
    pieces = blocks[0].shape[1] // width
    sent = Copies(sems)
    for j, block in enumerate(blocks):
        for p in range(pieces):
            value = dot(low[:, :depth], block[:, p * width : (p + 1) * width], NN)
            made[idx[n + j] * pieces + p] = value.astype(BF16)
    send_parts(sent, made, parts, [idx[i] for i in range(n)], None)
    sent.land()


def middle_kernel(model_width, tokens, squares, own, forward, backward, middle, middle_low, inverse_row):
    t = tokens.shape[0]
    total = squares[:1] + stat_total(forward[t:], t) + stat_total(backward[t:], t)
    inverse = lax.rsqrt(total / model_width + EPSILON)
    inverse_row[...] = jnp.broadcast_to(inverse, inverse_row.shape)
    summed = own[...].astype(F32) + forward[:t].astype(F32) + backward[:t].astype(F32)
    value = tokens[...].astype(F32) + summed * to_column(inverse)
    middle[...] = value
    middle_low[...] = value.astype(BF16)


def early_ffn_kernel(n, r, idx, *refs):
    m, dy, refs = refs[: n - 1], refs[n - 1 : 2 * n - 2], refs[2 * n - 2 :]
    (w1, w2, wd), refs = (refs[j * r : (j + 1) * r] for j in range(3)), refs[3 * r :]
    raw1, raw2, raw_grad, squares, m_full, dy_full, sems = refs
    col_places = [idx[i] for i in range(n) if i != n // 2]
    row_places = [idx[n + j] for j in range(r)]
    copies, second = Copies(sems), Copies(sems, n - 1)
    fetch_chunks(copies, m, m_full, col_places)
    fetch_chunks(second, dy, dy_full, col_places)
    width = m[0].shape[1]
    for c in range(n):

        @pl.when(idx[n // 2] == c)
        def _(c=c):
            for full in (m_full, dy_full):
                full[:, c * width : (c + 1) * width] = jnp.zeros((full.shape[0], width), full.dtype)

    copies.land()
    values = m_full[...].astype(F32)
    squares[...] = jnp.broadcast_to(jnp.sum(values * values, axis=1, keepdims=True), squares.shape)
    spans = [slice(first, first + size) for first, size in tiles(raw1.shape[1])]
    for at in spans:
        raw1[:, at] = by_blocks(m_full, row_places, w1, at, slice(None), NT)
        raw2[:, at] = by_blocks(m_full, row_places, w2, at, slice(None), NT)
    second.land()
    for at in spans:
        raw_grad[:, at] = by_blocks(dy_full, row_places, wd, at, slice(None), NT)


def ffn_kernel(n, r, hidden, idx, m_last, dy_last, raw1, raw2, raw_grad, squares, *refs):
    m, dy, refs = refs[:n], refs[n : 2 * n], refs[2 * n :]
    (w1, w2, wd), refs = (refs[j * r : (j + 1) * r] for j in range(3)), refs[3 * r :]
    m_keep, m_send, dy_keep, dy_send, lows_out, inverse, stat = refs[:7]
    parts, scratch = refs[7 : 7 + n], refs[7 + n :]
    m_full, dy_full, act1, act2, grads, lows, made, sems, out_sems = scratch
    col_places = [idx[i] for i in range(n)]
    row_places = [idx[n + j] for j in range(r)]
    width = m[0].shape[1]
    pieces = w1[0].shape[1] // width
    padded = lows.shape[1] // 3
    copies, sent = Copies(sems), Copies(out_sems)
    fetch_chunks(copies, m, m_full, col_places)
    fetch_chunks(copies, dy, dy_full, col_places)
    spans = [slice(first, first + size) for first, size in tiles(hidden)]
    for j, place in enumerate(row_places):
        for p in range(pieces):

            @pl.when(col_places[n // 2] == place * pieces + p)
            def _(j=j, p=p):
                columns = slice(p * width, (p + 1) * width)
                for at in spans:
                    act1[:, at] = raw1[:, at] + dot(m_last[...], w1[j][at, columns], NT)
                    act2[:, at] = raw2[:, at] + dot(m_last[...], w2[j][at, columns], NT)
                    grads[:, at] = raw_grad[:, at] + dot(dy_last[...], wd[j][at, columns], NT)

    values = m_last[...].astype(F32)
    sums = squares[:, :1] + jnp.sum(values * values, axis=1, keepdims=True)
    roots = lax.rsqrt(sums / (width * n) + EPSILON)
    inverse[...] = jnp.broadcast_to(roots, inverse.shape)
    total = None
    for at in spans:
        first_act, second_act, grad = act1[:, at] * roots, act2[:, at] * roots, grads[:, at]
        product = first_act * second_act
        part = jnp.sum(grad * product, axis=1, keepdims=True)
        total = part if total is None else total + part
        grad = grad * roots
        for k, value in enumerate((product, grad * second_act, grad * first_act)):
            lows[:, k * padded + at.start : k * padded + at.stop] = value.astype(BF16)
    if padded > hidden:
        for j in range(3):
            blank = jnp.zeros((lows.shape[0], padded - hidden), BF16)
            lows[:, j * padded + hidden : (j + 1) * padded] = blank
    sent.start(lows, lows_out)
    row = to_row(2.0 * total)
    stat[...] = row
    copies.land()
    split_blocks(sent, m_full, row_places, m_keep, m_send)
    split_blocks(sent, dy_full, row_places, dy_keep, dy_send)
    for j, place in enumerate(row_places):
        for p in range(pieces):
            at = slice(p * width, (p + 1) * width)
            value = dot(lows[:, padded : padded + hidden], w1[j][:, at], NN)
            value = value + dot(lows[:, 2 * padded : 2 * padded + hidden], w2[j][:, at], NN)
            made[place * pieces + p, : m_full.shape[0]] = value.astype(BF16)
    send_parts(sent, made, parts, col_places, row[:1])
    sent.land()


def middle_grad_kernel(
    model_width, cotangent, tokens, middle, middle_low, inverse, stat, own, forward, backward, grad, grad_low
):
    t = tokens.shape[0]
    inverse_two = inverse[:, :1]
    total = stat[:1] + stat_total(forward[t:], t) + stat_total(backward[t:], t)
    mean = to_column(total / model_width)
    normed = middle_low[...].astype(F32) * inverse_two
    summed = own[...].astype(F32) + forward[:t].astype(F32) + backward[:t].astype(F32)
    value = cotangent[...].astype(F32) + (summed - inverse_two * normed * mean)
    low = value.astype(BF16)
    grad[...] = value
    grad_low[:t] = low
    branch = middle[...] - tokens[...].astype(F32)
    row = to_row(jnp.sum(low.astype(F32) * branch, axis=1, keepdims=True))[:1]
    grad_low[t:] = stat_block(row, grad_low.shape[0] - t, grad_low.shape[1], 0)


def back_kernel(n, r, count, model_width, idx, numbers, pre, pre_gate, qkv, attended, inverse_row, first_inverse, *refs):
    br, packs, gate_packs, refs = refs[:n], refs[n : n + r], refs[n + r : n + 2 * r], refs[n + 2 * r :]
    keep, send, proj_out, next_stat = refs[:4]
    parts, scratch = refs[4 : 4 + n], refs[4 + n :]
    full, proj, stats, att_low, key_sum, value_sum, totals, made, sems, out_sems = scratch
    col_places = [idx[i] for i in range(n)]
    row_places = [idx[n + j] for j in range(r)]
    token_count, width = attended.shape
    pieces = packs[0].shape[0] // width
    copies, sent = Copies(sems), Copies(out_sems)
    fetch_chunks(copies, br, full, col_places)
    extra = stats.shape[1]
    for i in range(n):
        copies.start(br[i].at[token_count:], stats.at[i])
    copies.land()
    split_blocks(sent, full, row_places, keep, send)
    gated_grad = None
    for j, place in enumerate(row_places):
        for p in range(pieces):
            piece = gate_packs[j][p * width : (p + 1) * width, width:]
            value = dot(full[:, span(place * pieces + p, width)], piece, NT)
            gated_grad = value if gated_grad is None else gated_grad + value
    inverse = to_column(inverse_row[...])
    mean = to_column(stat_total(stats[...].reshape(n * extra, width), token_count) / model_width)
    roots = first_inverse[:, :1]
    values = pre_gate[...]
    gate = jax.nn.sigmoid(values)
    normed = attended[...] * inverse
    proj[:, 4 * width :] = (normed * gate).astype(BF16)
    inner = gated_grad * gate
    gate_grad = inner * normed * (1.0 - gate)
    proj[:, 3 * width : 4 * width] = (gate_grad * roots).astype(BF16)
    att_low[...] = (inverse * (inner - normed * mean)).astype(BF16)
    totals[...] = jnp.broadcast_to(jnp.sum(gate_grad * values, axis=1, keepdims=True), totals.shape)
    block = min(256, token_count)
    for head in range(width // HEAD):
        here = slice(head * HEAD, (head + 1) * HEAD)
        q, k, v = (slice(p * width + head * HEAD, p * width + (head + 1) * HEAD) for p in range(3))
        key_sum[...] = jnp.zeros_like(key_sum)
        value_sum[...] = jnp.zeros_like(value_sum)
        for first in range(0, token_count, block):
            keys = first + block
            rows = slice(first, keys)
            decays = decay(first, block, keys, numbers, count, head)
            scores = dot(qkv[rows, q], qkv[:keys, k], NT)
            mix = (scores * decays).astype(BF16)
            score_grad = dot(att_low[rows, here], qkv[:keys, v], NT)
            raw = (score_grad * decays).astype(BF16)
            query_sum = dot(raw, qkv[:keys, k], NN)
            query_grad = query_sum * silu_slope(pre[rows, q])
            totals[rows] += jnp.sum(query_grad * pre[rows, q], axis=1, keepdims=True)
            proj[rows, q] = (query_grad * roots[rows]).astype(BF16)
            key_sum[:keys] += dot(raw, qkv[rows, q], TN)
            value_sum[:keys] += dot(mix, att_low[rows, here], TN)
        for at, summed in ((k, key_sum), (v, value_sum)):
            grad = summed[...] * silu_slope(pre[:, at])
            totals[...] += jnp.sum(grad * pre[:, at], axis=1, keepdims=True)
            proj[:, at] = (grad * roots).astype(BF16)
    sent.start(proj, proj_out)
    row = to_row(totals[:, :1])
    next_stat[...] = row
    for j, place in enumerate(row_places):
        for p in range(pieces):
            at = slice(p * width, (p + 1) * width)
            value = dot(proj[:, : 3 * width], packs[j][at, :], NT)
            value = value + dot(proj[:, 3 * width : 4 * width], gate_packs[j][at, :width], NT)
            made[place * pieces + p, :token_count] = value.astype(BF16)
    send_parts(sent, made, parts, col_places, row[:1])
    sent.land()


def token_grad_kernel(model_width, middle_grad, tokens, inverse, stat, own, forward, backward, out):
    t = tokens.shape[0]
    inverse_first = inverse[:, :1]
    total = stat[:1] + stat_total(forward[t:], t) + stat_total(backward[t:], t)
    mean = to_column(total / model_width)
    normed = tokens[...].astype(F32) * inverse_first
    summed = own[...].astype(F32) + forward[:t].astype(F32) + backward[:t].astype(F32)
    out[...] = middle_grad[...] + (summed - inverse_first * normed * mean)


def weight_grad_kernel(y_size, columns, flipped, act, act_other, low, low_other, *outs):
    block = act.shape[1] // y_size
    outs = iter(outs)
    for start, width in columns:
        for dy in range(y_size):
            out = next(outs)
            for first, size in tiles(block if flipped else width):
                if flipped:
                    a = slice(dy * block + first, dy * block + first + size)
                    l = slice(start, start + width)
                    value = dot(low[:, l], act[:, a], TN) + dot(low_other[:, l], act_other[:, a], TN)
                else:
                    a = slice(dy * block, (dy + 1) * block)
                    l = slice(start + first, start + first + size)
                    value = dot(act[:, a], low[:, l], TN) + dot(act_other[:, a], low_other[:, l], TN)
                out[:, first : first + size] = value.astype(out.dtype)


def ring_order(mesh):
    n = mesh.shape["cols"]
    plain = list(range(n))
    try:
        devices = np.moveaxis(mesh.devices, mesh.axis_names.index("cols"), -1)
        devices = devices.reshape(-1, n)[0]
        coords = [tuple(d.coords) for d in devices]
    except (AttributeError, TypeError):
        return plain
    varying = [d for d in range(len(coords[0])) if len({c[d] for c in coords}) > 1]
    if len(varying) != 2:
        return plain
    a, b = varying
    sizes = [len({c[d] for c in coords}) for d in (a, b)]
    if sizes[0] % 2:
        a, b, sizes = b, a, sizes[::-1]
    if sizes[0] % 2 or sizes[0] * sizes[1] != n or sizes[1] < 2:
        return plain
    lows = [min(c[d] for c in coords) for d in (a, b)]
    index = {(c[a] - lows[0], c[b] - lows[1]): i for i, c in enumerate(coords)}
    walk = []
    for i in range(sizes[0]):
        across = range(1, sizes[1])
        walk += [(i, j) for j in (across if i % 2 == 0 else reversed(across))]
    walk += [(i, 0) for i in reversed(range(sizes[0]))]
    if set(walk) != set(index):
        return plain
    return [index[spot] for spot in walk]


def call(kernel, outs, scratch, limit, flops, moved, *args):
    return pl.pallas_call(
        kernel,
        out_shape=[jax.ShapeDtypeStruct(out[0], out[1]) for out in outs],
        in_specs=[spec for spec, _ in args],
        out_specs=[(*out, VMEM)[2] for out in outs],
        scratch_shapes=scratch,
        compiler_params=pltpu.CompilerParams(vmem_limit_bytes=limit),
        cost_estimate=pl.CostEstimate(flops=int(flops), bytes_accessed=int(moved), transcendentals=0),
    )(*[pltpu.with_memory_space_constraint(arg, pltpu.HBM) if spec is ANY else arg for spec, arg in args])


def each(spec, arrays):
    return [(spec, a) for a in arrays]


def shards(cycle, y_size, *args):
    (
        tokens,
        cotangent,
        lengths,
        decay_rate,
        query_weight,
        key_weight,
        value_weight,
        gate_weight,
        out_weight,
        first_weight,
        second_weight,
        down_weight,
    ) = args
    n, r = len(cycle), 2 * y_size
    half = n // 2
    token_count, width = tokens.shape
    model_width = width * n
    block = query_weight.shape[0]
    hidden_width = first_weight.shape[1]
    count = lengths.shape[1]
    dma = pltpu.SemaphoreType.DMA

    ahead = [(cycle[i], cycle[(i + 1) % n]) for i in range(n)]
    back = [(b, a) for a, b in ahead]
    core_swap = [(i, i ^ 1) for i in range(r)]

    def y_shift(by):
        return [(y * 2 + c, (y + by) % y_size * 2 + c) for y in range(y_size) for c in range(2)]

    place = {c: i for i, c in enumerate(cycle)}
    col_table = np.array([[cycle[(place[c] + i) % n] for i in range(n)] for c in range(n)], np.int32)
    row_table = np.array(
        [[((q // 2 + j // 2) % y_size) * 2 + ((q % 2) ^ (j % 2)) for j in range(r)] for q in range(r)], np.int32
    )

    def places_of(lengths, rates):
        idx = jnp.concatenate(
            [
                lax.dynamic_index_in_dim(jnp.asarray(col_table), lax.axis_index("cols"), 0, False),
                lax.dynamic_index_in_dim(jnp.asarray(row_table), lax.axis_index("rows"), 0, False),
            ]
        )
        places = jnp.arange(count, dtype=jnp.int32)
        bounds = jnp.sum(jnp.where(places[None, :] <= places[:, None], lengths[0][None, :], 0), axis=1)
        return idx, jnp.concatenate([bounds.astype(F32), rates])

    def cols(array, pairs):
        return lax.ppermute(array, "cols", pairs)

    def swap(array):
        return lax.ppermute(array, "rows", core_swap)

    def add(a, b):
        return (a.astype(F32) + b.astype(F32)).astype(BF16)

    plan, due, done = {}, {}, {}

    def task(slot, name, until, inputs, work):
        plan.setdefault(slot, []).append((name, until, inputs, work))

    def clock(slot, array, backward=None):
        tie = lax.optimization_barrier
        ending = due.pop(slot, [])
        if ending or backward is not None:
            array, backward, results = tie((array, backward, [done[name] for name in ending]))
            done.update(zip(ending, results))
        for name, until, inputs, work in plan.pop(slot, []):
            _, given = tie((array, inputs()))
            done[name] = work(*given)
            due.setdefault(until, []).append(name)
        return array if backward is None else (array, backward)

    def ring_gather(array, letter, parts=None):
        parts = [None] * n if parts is None else parts
        parts[0] = array
        forward = backward = array
        for k in range(1, half + 1):
            if k < half:
                forward, backward = clock(f"{letter}{k - 1}", forward, backward)
                parts[k] = backward = cols(backward, back)
            else:
                forward, backward = lax.optimization_barrier((forward, backward))
                forward = clock(f"{letter}{k - 1}", forward)
            parts[n - k] = forward = cols(forward, ahead)
        return parts

    def ring_scatter(parts, letter, long_way=ahead, short_way=back):
        if long_way is back:
            parts = [parts[-i] for i in range(n)]
        forward, backward = parts[half], parts[half + 1]
        for k in range(half - 1):
            forward, backward = clock(f"{letter}{k}", forward, backward)
            forward = add(cols(forward, long_way), parts[half - 1 - k])
            backward = cols(backward, short_way)
            if k < half - 2:
                backward = add(backward, parts[half + 2 + k])
        forward, backward = lax.optimization_barrier((forward, backward))
        forward = cols(clock(f"{letter}{half - 1}", forward), long_way)
        return parts[0], forward, backward

    def spread(spots, count):
        return [spots[min(k, len(spots) - 1)] for k in range(count)]

    def side_gather(name, array, back_spots, ahead_spots):
        for way, pairs, spots in (("b", back, spread(back_spots, half)), ("f", ahead, spread(ahead_spots, half - 1))):
            for k, (start, until) in enumerate(spots, 1):

                def inputs(before=f"{name}_{way}{k - 1}"):
                    return [done.get(before, array)]

                task(start, f"{name}_{way}{k}", until, inputs, functools.partial(cols, pairs=pairs))

    def side_gathered(name, array):
        return [
            array,
            *(done.get(f"{name}_b{k}") for k in range(1, half + 1)),
            *(done[f"{name}_f{n - k}"] for k in range(half + 1, n)),
        ]

    def side_scatter(name, parts_name, back_spots, ahead_spots):
        for way, pairs, spots, first, by in (
            ("b", back, spread(back_spots, half), half, 1),
            ("f", ahead, spread(ahead_spots, half - 1), half - 1, -1),
        ):
            for k, (start, until) in enumerate(spots):

                def inputs(k=k, way=way, first=first, by=by):
                    mine = done[parts_name][first + by * k]
                    return [add(done[f"{name}_{way}{k - 1}"], mine) if k else mine]

                task(start, f"{name}_{way}{k}", until, inputs, functools.partial(cols, pairs=pairs))

    def send_y(name, source, first, start, until):
        task(
            start,
            name,
            until,
            lambda: [done[source][first + dy] for dy in range(1, y_size)],
            lambda *a: [lax.ppermute(v, "rows", y_shift(dy)) for dy, v in enumerate(a, 1)],
        )

    def y_total(name, source, first):
        total = done[source][first]
        for value in done[name]:
            total = total + value.astype(F32)
        return total

    first_across, second_across = first_weight.T, second_weight.T
    end = half - 1
    packs = call(
        pack_kernel,
        [((block, 3 * width), BF16, ANY), ((block, 2 * width), BF16, ANY)],
        [dma((4 + block // width,))],
        4 * MIB,
        0,
        MIB,
        *each(ANY, (query_weight, key_weight, value_weight, gate_weight, out_weight)),
    )
    y_gather = lambda a: [lax.ppermute(a, "rows", y_shift(-dy)) for dy in range(1, y_size)]
    for name, pack, y_spot, own_spot, other_spot in (
        ("pack", packs[0], ("T0", f"T{end}"), ("T1", "T2"), (f"T{end}", "F")),
        ("gate_pack", packs[1], ("T2", "O"), ("T2", f"T{end}"), ("O", "P")),
        ("first", first_across, ("F", "R0"), ("T1", "T2"), ("R1", "R2")),
        ("second", second_across, ("R1", f"R{end}"), ("T2", f"T{end}"), (f"R{end}", "A0")),
        ("down", down_weight, (f"R{end}", "A1"), (f"T{end}", "F"), ("A1", "A2")),
    ):
        task(y_spot[0], name + "_y", y_spot[1], lambda pack=pack: [pack], y_gather)
        task(own_spot[0], name + "_own", own_spot[1], lambda pack=pack: [pack], swap)
        task(
            other_spot[0],
            name + "_other",
            other_spot[1],
            lambda name=name: done[name + "_y"],
            lambda *a: [swap(v) for v in a],
        )

    def blocks_of(name, pack):
        blocks = [pack, done[name + "_own"]]
        for a, b in zip(done[name + "_y"], done[name + "_other"]):
            blocks += [a, b]
        return blocks

    side_gather(
        "dy",
        cotangent,
        [(f"T{end}", "F"), ("F", "O"), ("O", "R0"), (f"A{end}", "G")],
        [("F", "O"), ("O", "R0"), (f"R{end}", "A0")],
    )

    token_half = (token_count, model_width // 2)
    local = (token_count, width)
    row = (8, token_count)
    stat_rows = 2 * token_count // width
    high = token_count + half * stat_rows
    with_stat = [(local, BF16, ANY)] + [((high, width), BF16, ANY)] * (n - 1)
    full_shape = (token_count, model_width)
    dense = token_count * model_width * width

    task("T0", "places", "T1", lambda: [lengths, decay_rate], places_of)
    token_parts = ring_gather(tokens, "T")
    idx, numbers = done["places"]
    token_parts[0] = clock("F", token_parts[0])
    tokens_keep, tokens_send, inverse_first, pre, qkv, attended, squares = call(
        functools.partial(front_kernel, n, r, count),
        [
            (token_half, BF16, ANY),
            (token_half, BF16, ANY),
            ((token_count, 128), F32),
            ((token_count, 3 * width), F32, ANY),
            ((token_count, 3 * width), BF16, ANY),
            (local, F32),
            (row, F32),
        ],
        [
            pltpu.VMEM(full_shape, BF16),
            pltpu.VMEM((token_count, 3 * width), F32),
            pltpu.VMEM((token_count, 3 * width), BF16),
            dma((n,)),
            dma((r + 2,)),
        ],
        14 * MIB,
        dense // 8,
        MIB,
        (SMEM, idx),
        (SMEM, numbers),
        *each(FREE, token_parts),
        *each(VMEM, blocks_of("pack", packs[0])),
    )
    attended = clock("O", attended)
    attended = clock("P", attended)
    gate_blocks = blocks_of("gate_pack", packs[1])
    pre_gate, *partial = call(
        functools.partial(gate_kernel, n, r),
        [(local, F32), *with_stat],
        [pltpu.VMEM(local, BF16), pltpu.VMEM((n, high, width), BF16), dma((n,))],
        14 * MIB,
        dense // 8,
        MIB,
        (SMEM, idx),
        *each(VMEM, (tokens_keep, tokens_send, inverse_first, attended, squares)),
        *each(VMEM, gate_blocks),
    )
    own, forward, backward = ring_scatter(partial, "R", back, ahead)
    middle, middle_low, inverse_attn = call(
        functools.partial(middle_kernel, model_width),
        [(local, F32), (local, BF16), (row, F32)],
        [],
        8 * MIB,
        0,
        MIB,
        *each(VMEM, (tokens, squares, own, forward, backward)),
    )
    task(f"A{end}", "tokens_swap", "G", lambda: [tokens_send], swap)
    wide_shape = ((token_count, hidden_width), F32)
    task(
        f"A{end}",
        "early",
        "G",
        lambda: [
            [a for i, a in enumerate(middle_sofar) if i != half],
            [a for i, a in enumerate(side_gathered("dy", cotangent)) if i != half],
            [*blocks_of("first", first_across), *blocks_of("second", second_across), *blocks_of("down", down_weight)],
        ],
        lambda m, dy, blocks: call(
            functools.partial(early_ffn_kernel, n, r),
            [wide_shape, wide_shape, wide_shape, ((token_count, 128), F32)],
            [pltpu.VMEM(full_shape, BF16), pltpu.VMEM(full_shape, BF16), dma((2 * n - 2,))],
            14 * MIB,
            6 * token_count * model_width * hidden_width,
            16 * MIB,
            (SMEM, idx),
            *each(FREE, m),
            *each(ANY, dy),
            *each(VMEM, blocks),
        ),
    )
    middle_sofar = [None] * n
    middle_parts = ring_gather(middle_low, "A", middle_sofar)
    middle_parts[0] = clock("G", middle_parts[0])
    padded = -(-hidden_width // 128) * 128
    grad_parts = side_gathered("dy", cotangent)
    down_blocks = blocks_of("down", down_weight)
    m_keep, m_send, dy_keep, dy_send, lows, inverse_second, second_stat, *partial = call(
        functools.partial(ffn_kernel, n, r, hidden_width),
        [
            *[(token_half, BF16, ANY)] * 4,
            ((token_count, 3 * padded), BF16, ANY),
            ((token_count, 128), F32),
            (row, F32),
            *with_stat,
        ],
        [
            pltpu.VMEM(full_shape, BF16),
            pltpu.VMEM(full_shape, BF16),
            pltpu.VMEM((token_count, hidden_width), F32),
            pltpu.VMEM((token_count, hidden_width), F32),
            pltpu.VMEM((token_count, hidden_width), F32),
            pltpu.VMEM((token_count, 3 * padded), BF16),
            pltpu.VMEM((n, high, width), BF16),
            dma((2 * n,)),
            dma((2 * r + 1 + n,)),
        ],
        22 * MIB,
        dense // 8,
        MIB,
        (SMEM, idx),
        *each(VMEM, (middle_parts[half], grad_parts[half], *done["early"])),
        *each(FREE, middle_parts),
        *each(ANY, grad_parts),
        *each(VMEM, (*blocks_of("first", first_across), *blocks_of("second", second_across), *down_blocks)),
    )

    def weight_grads(columns, flipped):
        def work(act, act_other, low, low_other):
            shapes = [(w, block) if flipped else (block, w) for _, w in columns]
            return call(
                functools.partial(weight_grad_kernel, y_size, columns, flipped),
                [(shape, BF16 if dy else F32) for shape in shapes for dy in range(y_size)],
                [],
                14 * MIB,
                4 * token_count * block * y_size * sum(w for _, w in columns),
                8 * MIB,
                *each(VMEM, (act, act_other, low, low_other)),
            )

        return work

    task("Q0", "dy_swap", "Q1", lambda: [dy_send], swap)
    task("Q0", "lows_swap", "Q1", lambda: [lows], swap)
    task(
        "Q0",
        "ffn_parts",
        "Q1",
        lambda: [lows],
        lambda low: call(
            functools.partial(down_kernel, n, r, hidden_width),
            [(local, BF16, ANY)] * n,
            [pltpu.VMEM((n, *local), BF16), dma((n,))],
            14 * MIB,
            2 * token_count * model_width * hidden_width,
            8 * MIB,
            (SMEM, idx),
            (VMEM, low),
            *each(VMEM, down_blocks),
        ),
    )
    task("Q1", "m_swap", "Q2", lambda: [m_send], swap)
    for slot, until, name, act, other, at in (
        ("Q1", "Q2", "down", dy_keep, "dy_swap", 0),
        ("Q2", f"Q{end}", "first", m_keep, "m_swap", padded),
        (f"Q{end}", "B0", "second", m_keep, "m_swap", 2 * padded),
    ):
        task(
            slot,
            name + "_grad",
            until,
            lambda act=act, other=other: [act, done[other], lows, done["lows_swap"]],
            weight_grads([(at, hidden_width)], True),
        )
    send_y("down_sent", "down_grad", 0, "Q2", "B0")
    send_y("first_sent", "first_grad", 0, "B0", "B2")
    send_y("second_sent", "second_grad", 0, "B2", "N0")
    side_scatter(
        "ffn",
        "ffn_parts",
        [(f"B{end}", "K"), ("K", "N0"), (f"N{end}", "E"), ("E", "END")],
        [(f"Q{end}", "B0"), ("K", "N0"), ("E", "END")],
    )
    own, forward, backward = ring_scatter(partial, "Q", back, ahead)
    low_rows = -(-stat_rows // 16) * 16
    middle_grad, middle_grad_low = call(
        functools.partial(middle_grad_kernel, model_width),
        [(local, F32), ((token_count + low_rows, width), BF16)],
        [],
        8 * MIB,
        0,
        MIB,
        *each(VMEM, (cotangent, tokens, middle, middle_low, inverse_second, second_stat, own, forward, backward)),
    )
    branch_parts = ring_gather(middle_grad_low, "B")
    branch_parts[0] = clock("K", branch_parts[0])
    br_keep, br_send, proj, first_stat, *partial = call(
        functools.partial(back_kernel, n, r, count, model_width),
        [
            (token_half, BF16, ANY),
            (token_half, BF16, ANY),
            ((token_count, 5 * width), BF16, ANY),
            (row, F32),
            *with_stat,
        ],
        [
            pltpu.VMEM(full_shape, BF16),
            pltpu.VMEM((token_count, 5 * width), BF16),
            pltpu.VMEM((n, low_rows, width), BF16),
            pltpu.VMEM(local, BF16),
            pltpu.VMEM((token_count, HEAD), F32),
            pltpu.VMEM((token_count, HEAD), F32),
            pltpu.VMEM((token_count, HEAD), F32),
            pltpu.VMEM((n, high, width), BF16),
            dma((2 * n,)),
            dma((r + 1 + n,)),
        ],
        16 * MIB,
        dense // 8,
        MIB,
        (SMEM, idx),
        (SMEM, numbers),
        *each(VMEM, (pre, pre_gate, qkv, attended, inverse_attn, inverse_first)),
        *each(FREE, branch_parts),
        *each(VMEM, blocks_of("pack", packs[0])),
        *each(VMEM, gate_blocks),
    )
    task("N0", "proj_swap", "N1", lambda: [proj], swap)
    task("N0", "br_swap", "N1", lambda: [br_send], swap)
    for name, act, other, columns, flipped in (
        ("proj_grad", tokens_keep, lambda: done["tokens_swap"], [(0, 2 * width), (2 * width, 2 * width)], False),
        ("out_grad", br_keep, lambda: done["br_swap"], [(4 * width, width)], True),
    ):
        task(
            "N0",
            name,
            "N1",
            lambda act=act, other=other: [act, other(), proj, done["proj_swap"]],
            weight_grads(columns, flipped),
        )
    send_y("proj_sent0", "proj_grad", 0, "N1", f"N{end}")
    send_y("proj_sent1", "proj_grad", y_size, "N2", "END")
    send_y("out_sent", "out_grad", 0, "N2", "END")
    own, forward, backward = ring_scatter(partial, "N")
    forward = clock("E", forward)
    [token_grad] = call(
        functools.partial(token_grad_kernel, model_width),
        [(local, F32)],
        [],
        8 * MIB,
        0,
        MIB,
        *each(VMEM, (middle_grad, tokens, inverse_first, first_stat, own, forward, backward)),
    )
    token_grad = clock("END", token_grad)
    ffn_total = done["ffn_parts"][0].astype(F32) + done[f"ffn_b{half - 1}"].astype(F32) + done[f"ffn_f{half - 2}"].astype(F32)
    layer_out = (middle + ffn_total).astype(BF16)
    pairs_of_grads = [y_total(f"proj_sent{i}", "proj_grad", i * y_size) for i in range(2)]
    return (
        layer_out,
        token_grad,
        *(pairs_of_grads[i // 2][:, i % 2 * width : (i % 2 + 1) * width] for i in range(4)),
        y_total("out_sent", "out_grad", 0),
        y_total("first_sent", "first_grad", 0).T,
        y_total("second_sent", "second_grad", 0).T,
        y_total("down_sent", "down_grad", 0),
    )


def solution(mesh):
    both, flipped = P("rows", "cols"), P("cols", "rows")
    return jax.shard_map(
        functools.partial(shards, ring_order(mesh), mesh.shape["rows"] // 2),
        mesh=mesh,
        in_specs=(both, both, P("rows", None), P("cols"), both, both, both, both, flipped, both, both, flipped),
        out_specs=(both, both, both, both, both, both, flipped, both, both, flipped),
        check_vma=False,
    )
```

```python
import functools

import jax
import jax.numpy as jnp
import numpy as np
from jax import lax
from jax.experimental import pallas as pl
from jax.experimental.pallas import tpu as pltpu
from jax.sharding import PartitionSpec as P

HEAD = 128
EPSILON = 1e-06
F32, BF16 = jnp.float32, jnp.bfloat16
NN, NT, TN = ((1,), (0,)), ((1,), (1,)), ((0,), (0,))
ANY = pl.BlockSpec(memory_space=pltpu.HBM)
FREE = pl.BlockSpec(memory_space=pl.ANY)
VMEM = pl.BlockSpec(memory_space=pltpu.VMEM)
SMEM = pl.BlockSpec(memory_space=pltpu.SMEM)
MIB = 1 << 20


def dot(left, right, dims):
    return lax.dot_general(left, right, (dims, ((), ())), preferred_element_type=F32)


def silu_slope(values):
    sigmoid_of = jax.nn.sigmoid(values)
    return sigmoid_of * (1.0 + values * (1.0 - sigmoid_of))


def to_row(column):
    return jnp.broadcast_to(column, (column.shape[0], 128)).T[:8]


def to_column(row):
    return jnp.broadcast_to(row[:1], (128, row.shape[1])).T[:, :1]


def tiles(size, step=256):
    return [(at, min(step, size - at)) for at in range(0, size, step)]


class Copies:
    def __init__(self, semaphores, first=0):
        self.semaphores, self.first, self.started, self.waited = semaphores, first, [], 0

    def start(self, source, target):
        copy = pltpu.make_async_copy(source, target, self.semaphores.at[self.first + len(self.started)])
        copy.start()
        self.started.append(copy)

    def land(self):
        for copy in self.started[self.waited :]:
            copy.wait()
        self.waited = len(self.started)


def span(place, size):
    return pl.ds(pl.multiple_of(place * size, size), size)


def fetch_chunks(copies, chunks, target, places):
    rows, width = target.shape[0], chunks[0].shape[1]
    for chunk, place in zip(chunks, places):
        source = chunk if chunk.shape[0] == rows else chunk.at[:rows]
        copies.start(source, target.at[:, span(place, width)])


def stat_block(row, rows, width, slot):
    pieces = row.shape[1] // width
    at = lax.broadcasted_iota(jnp.int32, (rows, width), 0)
    block = jnp.zeros((rows, width), F32)
    for k in range(pieces):
        value = row[:, k * width : (k + 1) * width]
        high = value.astype(BF16).astype(F32)
        for j, part in enumerate((high, value - high)):
            here = at == slot * 2 * pieces + j * pieces + k
            block = jnp.where(here, jnp.broadcast_to(part, (rows, width)), block)
    return block.astype(BF16)


def stat_total(block, tokens):
    rows, width = block.shape
    pieces = tokens // width
    at = lax.rem(lax.broadcasted_iota(jnp.int32, (rows, width), 0), pieces)
    values = block.astype(F32)
    parts = [jnp.sum(jnp.where(at == k, values, 0.0), axis=0, keepdims=True) for k in range(pieces)]
    return jnp.concatenate(parts, axis=1)


def by_blocks(array, places, blocks, rows, columns, dims):
    total = None
    for place, block in zip(places, blocks):
        size = block.shape[0 if dims is NN else 1]
        value = dot(array[:, span(place, size)], block[rows, columns], dims)
        total = value if total is None else total + value
    return total


def send_parts(sent, made, parts, places, stat):
    n = len(parts)
    tokens, width = made.shape[1:]
    if stat is not None:
        tokens = stat.shape[1]
        for i in range(1, n):
            made[places[i], tokens:] = stat_block(stat, made.shape[1] - tokens, width, min(i, n - i) - 1)
    for i, part in enumerate(parts):
        rows = part.shape[0]
        sent.start(made.at[places[i], :rows], part)


def inverse_roots(array):
    values = array.astype(F32)
    return lax.rsqrt(jnp.mean(values * values, axis=1, keepdims=True) + EPSILON)


def split_blocks(copies, array, row_places, keep, send):
    block = keep.shape[1] // (len(row_places) // 2)
    for dy in range(len(row_places) // 2):
        for dc, out in ((0, keep), (1, send)):
            copies.start(array.at[:, span(row_places[dy * 2 + dc], block)], out.at[:, dy * block : (dy + 1) * block])


def decay(first, rows, keys, numbers, count, head):
    t = first + lax.broadcasted_iota(jnp.int32, (rows, keys), 0)
    s = lax.broadcasted_iota(jnp.int32, (rows, keys), 1)
    start = jnp.zeros((rows, keys), jnp.int32)
    for i in range(count):
        bound = numbers[i].astype(jnp.int32)
        start = jnp.where(t >= bound, bound, start)
    distance = (t - s).astype(F32)
    allowed = (s >= start) & (s <= t)
    return jnp.where(allowed, jnp.exp(-numbers[count + head] * jnp.maximum(distance, 0.0)), 0.0)


def pack_kernel(query, key, value, gate, out, first, second, sems):
    copies = Copies(sems)
    width = query.shape[1]
    for p, weight in enumerate((query, key, value)):
        copies.start(weight, first.at[:, p * width : (p + 1) * width])
    copies.start(gate, second.at[:, :width])
    for p in range(out.shape[1] // width):
        at = slice(p * width, (p + 1) * width)
        copies.start(out.at[:, at], second.at[at, width:])
    copies.land()


def front_kernel(n, r, count, idx, numbers, *refs):
    x, weights = refs[:n], refs[n : n + r]
    keep, send, inverse, pre_out, qkv_out, attended, squares, full, pre, qkv, sems, out_sems = refs[n + r :]
    token_count = full.shape[0]
    width = attended.shape[1]
    row_places = [idx[n + j] for j in range(r)]
    copies, sent = Copies(sems), Copies(out_sems)
    fetch_chunks(copies, x, full, [idx[i] for i in range(n)])
    copies.land()
    split_blocks(sent, full, row_places, keep, send)
    roots = inverse_roots(full[...])
    inverse[...] = jnp.broadcast_to(roots, inverse.shape)
    for p in range(3):
        at = slice(p * width, (p + 1) * width)
        values = by_blocks(full, row_places, weights, slice(None), at, NN) * roots
        pre[:, at] = values
        qkv[:, at] = (values * jax.nn.sigmoid(values)).astype(BF16)
    sent.start(pre, pre_out)
    sent.start(qkv, qkv_out)
    block = min(256, token_count)
    for head in range(width // HEAD):
        q, k, v = (slice(p * width + head * HEAD, p * width + (head + 1) * HEAD) for p in range(3))
        for first in range(0, token_count, block):
            keys = first + block
            decays = decay(first, block, keys, numbers, count, head)
            scores = dot(qkv[first:keys, q], qkv[:keys, k], NT)
            mix = (scores * decays).astype(BF16)
            attended[first:keys, head * HEAD : (head + 1) * HEAD] = dot(mix, qkv[:keys, v], NN)
    values = attended[...]
    squares[...] = to_row(jnp.sum(values * values, axis=1, keepdims=True))
    sent.land()


def gate_kernel(n, r, idx, keep, send, inverse, attended, stat, *refs):
    packs, pre_gate, parts, (gate_low, made, sems) = refs[:r], refs[r], refs[r + 1 : r + 1 + n], refs[r + 1 + n :]
    token_count, width = attended.shape
    size = packs[0].shape[0]
    pieces = size // width
    sent = Copies(sems)
    total = None
    for j, pack in enumerate(packs):
        source = (keep, send)[j % 2]
        value = dot(source[:, j // 2 * size : (j // 2 + 1) * size], pack[:, :width], NN)
        total = value if total is None else total + value
    total = total * inverse[:, :1]
    pre_gate[...] = total
    gate_low[...] = (attended[...] * jax.nn.sigmoid(total)).astype(BF16)
    for j, pack in enumerate(packs):
        for p in range(pieces):
            value = dot(gate_low[...], pack[p * width : (p + 1) * width, width:], NN)
            made[idx[n + j] * pieces + p, :token_count] = value.astype(BF16)
    send_parts(sent, made, parts, [idx[i] for i in range(n)], stat[:1])
    sent.land()


def down_kernel(n, r, depth, idx, low, *refs):
    blocks, parts, (made, sems) = refs[:r], refs[r : r + n], refs[r + n :]
    width = made.shape[2]
    pieces = blocks[0].shape[1] // width
    sent = Copies(sems)
    for j, block in enumerate(blocks):
        for p in range(pieces):
            value = dot(low[:, :depth], block[:, p * width : (p + 1) * width], NN)
            made[idx[n + j] * pieces + p] = value.astype(BF16)
    send_parts(sent, made, parts, [idx[i] for i in range(n)], None)
    sent.land()


def middle_kernel(model_width, tokens, squares, own, forward, backward, middle, middle_low, inverse_row):
    t = tokens.shape[0]
    total = squares[:1] + stat_total(forward[t:], t) + stat_total(backward[t:], t)
    inverse = lax.rsqrt(total / model_width + EPSILON)
    inverse_row[...] = jnp.broadcast_to(inverse, inverse_row.shape)
    summed = own[...].astype(F32) + forward[:t].astype(F32) + backward[:t].astype(F32)
    value = tokens[...].astype(F32) + summed * to_column(inverse)
    middle[...] = value
    middle_low[...] = value.astype(BF16)


def early_ffn_kernel(n, r, idx, *refs):
    m, dy, refs = refs[: n - 1], refs[n - 1 : 2 * n - 2], refs[2 * n - 2 :]
    (w1, w2, wd), refs = (refs[j * r : (j + 1) * r] for j in range(3)), refs[3 * r :]
    raw1, raw2, raw_grad, squares, m_full, dy_full, sems = refs
    col_places = [idx[i] for i in range(n) if i != n // 2]
    row_places = [idx[n + j] for j in range(r)]
    copies, second = Copies(sems), Copies(sems, n - 1)
    fetch_chunks(copies, m, m_full, col_places)
    fetch_chunks(second, dy, dy_full, col_places)
    width = m[0].shape[1]
    for c in range(n):

        @pl.when(idx[n // 2] == c)
        def _(c=c):
            for full in (m_full, dy_full):
                full[:, c * width : (c + 1) * width] = jnp.zeros((full.shape[0], width), full.dtype)

    copies.land()
    values = m_full[...].astype(F32)
    squares[...] = jnp.broadcast_to(jnp.sum(values * values, axis=1, keepdims=True), squares.shape)
    spans = [slice(first, first + size) for first, size in tiles(raw1.shape[1])]
    for at in spans:
        raw1[:, at] = by_blocks(m_full, row_places, w1, at, slice(None), NT)
        raw2[:, at] = by_blocks(m_full, row_places, w2, at, slice(None), NT)
    second.land()
    for at in spans:
        raw_grad[:, at] = by_blocks(dy_full, row_places, wd, at, slice(None), NT)


def ffn_kernel(n, r, hidden, idx, m_last, dy_last, raw1, raw2, raw_grad, squares, *refs):
    m, dy, refs = refs[:n], refs[n : 2 * n], refs[2 * n :]
    (w1, w2, wd), refs = (refs[j * r : (j + 1) * r] for j in range(3)), refs[3 * r :]
    m_keep, m_send, dy_keep, dy_send, lows_out, inverse, stat = refs[:7]
    parts, scratch = refs[7 : 7 + n], refs[7 + n :]
    m_full, dy_full, act1, act2, grads, lows, made, sems, out_sems = scratch
    col_places = [idx[i] for i in range(n)]
    row_places = [idx[n + j] for j in range(r)]
    width = m[0].shape[1]
    pieces = w1[0].shape[1] // width
    padded = lows.shape[1] // 3
    copies, sent = Copies(sems), Copies(out_sems)
    fetch_chunks(copies, m, m_full, col_places)
    fetch_chunks(copies, dy, dy_full, col_places)
    spans = [slice(first, first + size) for first, size in tiles(hidden)]
    for j, place in enumerate(row_places):
        for p in range(pieces):

            @pl.when(col_places[n // 2] == place * pieces + p)
            def _(j=j, p=p):
                columns = slice(p * width, (p + 1) * width)
                for at in spans:
                    act1[:, at] = raw1[:, at] + dot(m_last[...], w1[j][at, columns], NT)
                    act2[:, at] = raw2[:, at] + dot(m_last[...], w2[j][at, columns], NT)
                    grads[:, at] = raw_grad[:, at] + dot(dy_last[...], wd[j][at, columns], NT)

    values = m_last[...].astype(F32)
    sums = squares[:, :1] + jnp.sum(values * values, axis=1, keepdims=True)
    roots = lax.rsqrt(sums / (width * n) + EPSILON)
    inverse[...] = jnp.broadcast_to(roots, inverse.shape)
    total = None
    for at in spans:
        first_act, second_act, grad = act1[:, at] * roots, act2[:, at] * roots, grads[:, at]
        product = first_act * second_act
        part = jnp.sum(grad * product, axis=1, keepdims=True)
        total = part if total is None else total + part
        grad = grad * roots
        for k, value in enumerate((product, grad * second_act, grad * first_act)):
            lows[:, k * padded + at.start : k * padded + at.stop] = value.astype(BF16)
    if padded > hidden:
        for j in range(3):
            blank = jnp.zeros((lows.shape[0], padded - hidden), BF16)
            lows[:, j * padded + hidden : (j + 1) * padded] = blank
    sent.start(lows, lows_out)
    row = to_row(2.0 * total)
    stat[...] = row
    copies.land()
    split_blocks(sent, m_full, row_places, m_keep, m_send)
    split_blocks(sent, dy_full, row_places, dy_keep, dy_send)
    for j, place in enumerate(row_places):
        for p in range(pieces):
            at = slice(p * width, (p + 1) * width)
            value = dot(lows[:, padded : padded + hidden], w1[j][:, at], NN)
            value = value + dot(lows[:, 2 * padded : 2 * padded + hidden], w2[j][:, at], NN)
            made[place * pieces + p, : m_full.shape[0]] = value.astype(BF16)
    send_parts(sent, made, parts, col_places, row[:1])
    sent.land()


def middle_grad_kernel(
    model_width, cotangent, tokens, middle, middle_low, inverse, stat, own, forward, backward, grad, grad_low
):
    t = tokens.shape[0]
    inverse_two = inverse[:, :1]
    total = stat[:1] + stat_total(forward[t:], t) + stat_total(backward[t:], t)
    mean = to_column(total / model_width)
    normed = middle_low[...].astype(F32) * inverse_two
    summed = own[...].astype(F32) + forward[:t].astype(F32) + backward[:t].astype(F32)
    value = cotangent[...].astype(F32) + (summed - inverse_two * normed * mean)
    low = value.astype(BF16)
    grad[...] = value
    grad_low[:t] = low
    branch = middle[...] - tokens[...].astype(F32)
    row = to_row(jnp.sum(low.astype(F32) * branch, axis=1, keepdims=True))[:1]
    grad_low[t:] = stat_block(row, grad_low.shape[0] - t, grad_low.shape[1], 0)


def back_kernel(n, r, count, model_width, idx, numbers, pre, pre_gate, qkv, attended, inverse_row, first_inverse, *refs):
    br, packs, gate_packs, refs = refs[:n], refs[n : n + r], refs[n + r : n + 2 * r], refs[n + 2 * r :]
    keep, send, proj_out, next_stat = refs[:4]
    parts, scratch = refs[4 : 4 + n], refs[4 + n :]
    full, proj, stats, att_low, key_sum, value_sum, totals, made, sems, out_sems = scratch
    col_places = [idx[i] for i in range(n)]
    row_places = [idx[n + j] for j in range(r)]
    token_count, width = attended.shape
    pieces = packs[0].shape[0] // width
    copies, sent = Copies(sems), Copies(out_sems)
    fetch_chunks(copies, br, full, col_places)
    extra = stats.shape[1]
    for i in range(n):
        copies.start(br[i].at[token_count:], stats.at[i])
    copies.land()
    split_blocks(sent, full, row_places, keep, send)
    gated_grad = None
    for j, place in enumerate(row_places):
        for p in range(pieces):
            piece = gate_packs[j][p * width : (p + 1) * width, width:]
            value = dot(full[:, span(place * pieces + p, width)], piece, NT)
            gated_grad = value if gated_grad is None else gated_grad + value
    inverse = to_column(inverse_row[...])
    mean = to_column(stat_total(stats[...].reshape(n * extra, width), token_count) / model_width)
    roots = first_inverse[:, :1]
    values = pre_gate[...]
    gate = jax.nn.sigmoid(values)
    normed = attended[...] * inverse
    proj[:, 4 * width :] = (normed * gate).astype(BF16)
    inner = gated_grad * gate
    gate_grad = inner * normed * (1.0 - gate)
    proj[:, 3 * width : 4 * width] = (gate_grad * roots).astype(BF16)
    att_low[...] = (inverse * (inner - normed * mean)).astype(BF16)
    totals[...] = jnp.broadcast_to(jnp.sum(gate_grad * values, axis=1, keepdims=True), totals.shape)
    block = min(256, token_count)
    for head in range(width // HEAD):
        here = slice(head * HEAD, (head + 1) * HEAD)
        q, k, v = (slice(p * width + head * HEAD, p * width + (head + 1) * HEAD) for p in range(3))
        key_sum[...] = jnp.zeros_like(key_sum)
        value_sum[...] = jnp.zeros_like(value_sum)
        for first in range(0, token_count, block):
            keys = first + block
            rows = slice(first, keys)
            decays = decay(first, block, keys, numbers, count, head)
            scores = dot(qkv[rows, q], qkv[:keys, k], NT)
            mix = (scores * decays).astype(BF16)
            score_grad = dot(att_low[rows, here], qkv[:keys, v], NT)
            raw = (score_grad * decays).astype(BF16)
            query_sum = dot(raw, qkv[:keys, k], NN)
            query_grad = query_sum * silu_slope(pre[rows, q])
            totals[rows] += jnp.sum(query_grad * pre[rows, q], axis=1, keepdims=True)
            proj[rows, q] = (query_grad * roots[rows]).astype(BF16)
            key_sum[:keys] += dot(raw, qkv[rows, q], TN)
            value_sum[:keys] += dot(mix, att_low[rows, here], TN)
        for at, summed in ((k, key_sum), (v, value_sum)):
            grad = summed[...] * silu_slope(pre[:, at])
            totals[...] += jnp.sum(grad * pre[:, at], axis=1, keepdims=True)
            proj[:, at] = (grad * roots).astype(BF16)
    sent.start(proj, proj_out)
    row = to_row(totals[:, :1])
    next_stat[...] = row
    for j, place in enumerate(row_places):
        for p in range(pieces):
            at = slice(p * width, (p + 1) * width)
            value = dot(proj[:, : 3 * width], packs[j][at, :], NT)
            value = value + dot(proj[:, 3 * width : 4 * width], gate_packs[j][at, :width], NT)
            made[place * pieces + p, :token_count] = value.astype(BF16)
    send_parts(sent, made, parts, col_places, row[:1])
    sent.land()


def token_grad_kernel(model_width, middle_grad, tokens, inverse, stat, own, forward, backward, out):
    t = tokens.shape[0]
    inverse_first = inverse[:, :1]
    total = stat[:1] + stat_total(forward[t:], t) + stat_total(backward[t:], t)
    mean = to_column(total / model_width)
    normed = tokens[...].astype(F32) * inverse_first
    summed = own[...].astype(F32) + forward[:t].astype(F32) + backward[:t].astype(F32)
    out[...] = middle_grad[...] + (summed - inverse_first * normed * mean)


def weight_grad_kernel(y_size, columns, flipped, act, act_other, low, low_other, *outs):
    block = act.shape[1] // y_size
    outs = iter(outs)
    for start, width in columns:
        for dy in range(y_size):
            out = next(outs)
            for first, size in tiles(block if flipped else width):
                if flipped:
                    a = slice(dy * block + first, dy * block + first + size)
                    l = slice(start, start + width)
                    value = dot(low[:, l], act[:, a], TN) + dot(low_other[:, l], act_other[:, a], TN)
                else:
                    a = slice(dy * block, (dy + 1) * block)
                    l = slice(start + first, start + first + size)
                    value = dot(act[:, a], low[:, l], TN) + dot(act_other[:, a], low_other[:, l], TN)
                out[:, first : first + size] = value.astype(out.dtype)


def ring_order(mesh):
    n = mesh.shape["cols"]
    plain = list(range(n))
    try:
        devices = np.moveaxis(mesh.devices, mesh.axis_names.index("cols"), -1)
        devices = devices.reshape(-1, n)[0]
        coords = [tuple(d.coords) for d in devices]
    except (AttributeError, TypeError):
        return plain
    varying = [d for d in range(len(coords[0])) if len({c[d] for c in coords}) > 1]
    if len(varying) != 2:
        return plain
    a, b = varying
    sizes = [len({c[d] for c in coords}) for d in (a, b)]
    if sizes[0] % 2:
        a, b, sizes = b, a, sizes[::-1]
    if sizes[0] % 2 or sizes[0] * sizes[1] != n or sizes[1] < 2:
        return plain
    lows = [min(c[d] for c in coords) for d in (a, b)]
    index = {(c[a] - lows[0], c[b] - lows[1]): i for i, c in enumerate(coords)}
    walk = []
    for i in range(sizes[0]):
        across = range(1, sizes[1])
        walk += [(i, j) for j in (across if i % 2 == 0 else reversed(across))]
    walk += [(i, 0) for i in reversed(range(sizes[0]))]
    if set(walk) != set(index):
        return plain
    return [index[spot] for spot in walk]


def call(kernel, outs, scratch, limit, flops, moved, *args):
    return pl.pallas_call(
        kernel,
        out_shape=[jax.ShapeDtypeStruct(out[0], out[1]) for out in outs],
        in_specs=[spec for spec, _ in args],
        out_specs=[(*out, VMEM)[2] for out in outs],
        scratch_shapes=scratch,
        compiler_params=pltpu.CompilerParams(vmem_limit_bytes=limit),
        cost_estimate=pl.CostEstimate(flops=int(flops), bytes_accessed=int(moved), transcendentals=0),
    )(*[pltpu.with_memory_space_constraint(arg, pltpu.HBM) if spec is ANY else arg for spec, arg in args])


def each(spec, arrays):
    return [(spec, a) for a in arrays]


def shards(cycle, y_size, *args):
    (
        tokens,
        cotangent,
        lengths,
        decay_rate,
        query_weight,
        key_weight,
        value_weight,
        gate_weight,
        out_weight,
        first_weight,
        second_weight,
        down_weight,
    ) = args
    n, r = len(cycle), 2 * y_size
    half = n // 2
    token_count, width = tokens.shape
    model_width = width * n
    block = query_weight.shape[0]
    hidden_width = first_weight.shape[1]
    count = lengths.shape[1]
    dma = pltpu.SemaphoreType.DMA

    ahead = [(cycle[i], cycle[(i + 1) % n]) for i in range(n)]
    back = [(b, a) for a, b in ahead]
    core_swap = [(i, i ^ 1) for i in range(r)]

    def y_shift(by):
        return [(y * 2 + c, (y + by) % y_size * 2 + c) for y in range(y_size) for c in range(2)]

    place = {c: i for i, c in enumerate(cycle)}
    col_table = np.array([[cycle[(place[c] + i) % n] for i in range(n)] for c in range(n)], np.int32)
    row_table = np.array(
        [[((q // 2 + j // 2) % y_size) * 2 + ((q % 2) ^ (j % 2)) for j in range(r)] for q in range(r)], np.int32
    )

    def places_of(lengths, rates):
        idx = jnp.concatenate(
            [
                lax.dynamic_index_in_dim(jnp.asarray(col_table), lax.axis_index("cols"), 0, False),
                lax.dynamic_index_in_dim(jnp.asarray(row_table), lax.axis_index("rows"), 0, False),
            ]
        )
        places = jnp.arange(count, dtype=jnp.int32)
        bounds = jnp.sum(jnp.where(places[None, :] <= places[:, None], lengths[0][None, :], 0), axis=1)
        return idx, jnp.concatenate([bounds.astype(F32), rates])

    def cols(array, pairs):
        return lax.ppermute(array, "cols", pairs)

    def swap(array):
        return lax.ppermute(array, "rows", core_swap)

    def add(a, b):
        return (a.astype(F32) + b.astype(F32)).astype(BF16)

    plan, due, done = {}, {}, {}

    def task(slot, name, until, inputs, work):
        plan.setdefault(slot, []).append((name, until, inputs, work))

    def clock(slot, array, backward=None):
        tie = lax.optimization_barrier
        ending = due.pop(slot, [])
        if ending or backward is not None:
            array, backward, results = tie((array, backward, [done[name] for name in ending]))
            done.update(zip(ending, results))
        for name, until, inputs, work in plan.pop(slot, []):
            _, given = tie((array, inputs()))
            done[name] = work(*given)
            due.setdefault(until, []).append(name)
        return array if backward is None else (array, backward)

    def ring_gather(array, letter, parts=None):
        parts = [None] * n if parts is None else parts
        parts[0] = array
        forward = backward = array
        for k in range(1, half + 1):
            if k < half:
                forward, backward = clock(f"{letter}{k - 1}", forward, backward)
                parts[k] = backward = cols(backward, back)
            else:
                forward, backward = lax.optimization_barrier((forward, backward))
                forward = clock(f"{letter}{k - 1}", forward)
            parts[n - k] = forward = cols(forward, ahead)
        return parts

    def ring_scatter(parts, letter, long_way=ahead, short_way=back):
        if long_way is back:
            parts = [parts[-i] for i in range(n)]
        forward, backward = parts[half], parts[half + 1]
        for k in range(half - 1):
            forward, backward = clock(f"{letter}{k}", forward, backward)
            forward = add(cols(forward, long_way), parts[half - 1 - k])
            backward = cols(backward, short_way)
            if k < half - 2:
                backward = add(backward, parts[half + 2 + k])
        forward, backward = lax.optimization_barrier((forward, backward))
        forward = cols(clock(f"{letter}{half - 1}", forward), long_way)
        return parts[0], forward, backward

    def spread(spots, count):
        return [spots[min(k, len(spots) - 1)] for k in range(count)]

    def side_gather(name, array, back_spots, ahead_spots):
        for way, pairs, spots in (("b", back, spread(back_spots, half)), ("f", ahead, spread(ahead_spots, half - 1))):
            for k, (start, until) in enumerate(spots, 1):

                def inputs(before=f"{name}_{way}{k - 1}"):
                    return [done.get(before, array)]

                task(start, f"{name}_{way}{k}", until, inputs, functools.partial(cols, pairs=pairs))

    def side_gathered(name, array):
        return [
            array,
            *(done.get(f"{name}_b{k}") for k in range(1, half + 1)),
            *(done[f"{name}_f{n - k}"] for k in range(half + 1, n)),
        ]

    def side_scatter(name, parts_name, back_spots, ahead_spots):
        for way, pairs, spots, first, by in (
            ("b", back, spread(back_spots, half), half, 1),
            ("f", ahead, spread(ahead_spots, half - 1), half - 1, -1),
        ):
            for k, (start, until) in enumerate(spots):

                def inputs(k=k, way=way, first=first, by=by):
                    mine = done[parts_name][first + by * k]
                    return [add(done[f"{name}_{way}{k - 1}"], mine) if k else mine]

                task(start, f"{name}_{way}{k}", until, inputs, functools.partial(cols, pairs=pairs))

    def send_y(name, source, first, start, until):
        task(
            start,
            name,
            until,
            lambda: [done[source][first + dy] for dy in range(1, y_size)],
            lambda *a: [lax.ppermute(v, "rows", y_shift(dy)) for dy, v in enumerate(a, 1)],
        )

    def y_total(name, source, first):
        total = done[source][first]
        for value in done[name]:
            total = total + value.astype(F32)
        return total

    first_across, second_across = first_weight.T, second_weight.T
    end = half - 1
    packs = call(
        pack_kernel,
        [((block, 3 * width), BF16, ANY), ((block, 2 * width), BF16, ANY)],
        [dma((4 + block // width,))],
        4 * MIB,
        0,
        MIB,
        *each(ANY, (query_weight, key_weight, value_weight, gate_weight, out_weight)),
    )
    y_gather = lambda a: [lax.ppermute(a, "rows", y_shift(-dy)) for dy in range(1, y_size)]
    for name, pack, y_spot, own_spot, other_spot in (
        ("pack", packs[0], ("T0", f"T{end}"), ("T1", "T2"), (f"T{end}", "F")),
        ("gate_pack", packs[1], ("T2", "O"), ("T2", f"T{end}"), ("O", "P")),
        ("first", first_across, ("F", "R0"), ("T1", "T2"), ("R1", "R2")),
        ("second", second_across, ("R1", f"R{end}"), ("T2", f"T{end}"), (f"R{end}", "A0")),
        ("down", down_weight, (f"R{end}", "A1"), (f"T{end}", "F"), ("A1", "A2")),
    ):
        task(y_spot[0], name + "_y", y_spot[1], lambda pack=pack: [pack], y_gather)
        task(own_spot[0], name + "_own", own_spot[1], lambda pack=pack: [pack], swap)
        task(
            other_spot[0],
            name + "_other",
            other_spot[1],
            lambda name=name: done[name + "_y"],
            lambda *a: [swap(v) for v in a],
        )

    def blocks_of(name, pack):
        blocks = [pack, done[name + "_own"]]
        for a, b in zip(done[name + "_y"], done[name + "_other"]):
            blocks += [a, b]
        return blocks

    side_gather(
        "dy",
        cotangent,
        [(f"T{end}", "F"), ("F", "O"), ("O", "R0"), (f"A{end}", "G")],
        [("F", "O"), ("O", "R0"), (f"R{end}", "A0")],
    )

    token_half = (token_count, model_width // 2)
    local = (token_count, width)
    row = (8, token_count)
    stat_rows = 2 * token_count // width
    high = token_count + half * stat_rows
    with_stat = [(local, BF16, ANY)] + [((high, width), BF16, ANY)] * (n - 1)
    full_shape = (token_count, model_width)
    dense = token_count * model_width * width

    task("T0", "places", "T1", lambda: [lengths, decay_rate], places_of)
    token_parts = ring_gather(tokens, "T")
    idx, numbers = done["places"]
    token_parts[0] = clock("F", token_parts[0])
    tokens_keep, tokens_send, inverse_first, pre, qkv, attended, squares = call(
        functools.partial(front_kernel, n, r, count),
        [
            (token_half, BF16, ANY),
            (token_half, BF16, ANY),
            ((token_count, 128), F32),
            ((token_count, 3 * width), F32, ANY),
            ((token_count, 3 * width), BF16, ANY),
            (local, F32),
            (row, F32),
        ],
        [
            pltpu.VMEM(full_shape, BF16),
            pltpu.VMEM((token_count, 3 * width), F32),
            pltpu.VMEM((token_count, 3 * width), BF16),
            dma((n,)),
            dma((r + 2,)),
        ],
        14 * MIB,
        dense // 8,
        MIB,
        (SMEM, idx),
        (SMEM, numbers),
        *each(FREE, token_parts),
        *each(VMEM, blocks_of("pack", packs[0])),
    )
    attended = clock("O", attended)
    attended = clock("P", attended)
    gate_blocks = blocks_of("gate_pack", packs[1])
    pre_gate, *partial = call(
        functools.partial(gate_kernel, n, r),
        [(local, F32), *with_stat],
        [pltpu.VMEM(local, BF16), pltpu.VMEM((n, high, width), BF16), dma((n,))],
        14 * MIB,
        dense // 8,
        MIB,
        (SMEM, idx),
        *each(VMEM, (tokens_keep, tokens_send, inverse_first, attended, squares)),
        *each(VMEM, gate_blocks),
    )
    own, forward, backward = ring_scatter(partial, "R", back, ahead)
    middle, middle_low, inverse_attn = call(
        functools.partial(middle_kernel, model_width),
        [(local, F32), (local, BF16), (row, F32)],
        [],
        8 * MIB,
        0,
        MIB,
        *each(VMEM, (tokens, squares, own, forward, backward)),
    )
    task(f"A{end}", "tokens_swap", "G", lambda: [tokens_send], swap)
    wide_shape = ((token_count, hidden_width), F32)
    task(
        f"A{end}",
        "early",
        "G",
        lambda: [
            [a for i, a in enumerate(middle_sofar) if i != half],
            [a for i, a in enumerate(side_gathered("dy", cotangent)) if i != half],
            [*blocks_of("first", first_across), *blocks_of("second", second_across), *blocks_of("down", down_weight)],
        ],
        lambda m, dy, blocks: call(
            functools.partial(early_ffn_kernel, n, r),
            [wide_shape, wide_shape, wide_shape, ((token_count, 128), F32)],
            [pltpu.VMEM(full_shape, BF16), pltpu.VMEM(full_shape, BF16), dma((2 * n - 2,))],
            14 * MIB,
            6 * token_count * model_width * hidden_width,
            16 * MIB,
            (SMEM, idx),
            *each(FREE, m),
            *each(FREE, dy),
            *each(VMEM, blocks),
        ),
    )
    middle_sofar = [None] * n
    middle_parts = ring_gather(middle_low, "A", middle_sofar)
    middle_parts[0] = clock("G", middle_parts[0])
    padded = -(-hidden_width // 128) * 128
    grad_parts = side_gathered("dy", cotangent)
    down_blocks = blocks_of("down", down_weight)
    m_keep, m_send, dy_keep, dy_send, lows, inverse_second, second_stat, *partial = call(
        functools.partial(ffn_kernel, n, r, hidden_width),
        [
            *[(token_half, BF16, ANY)] * 4,
            ((token_count, 3 * padded), BF16, ANY),
            ((token_count, 128), F32),
            (row, F32),
            *with_stat,
        ],
        [
            pltpu.VMEM(full_shape, BF16),
            pltpu.VMEM(full_shape, BF16),
            pltpu.VMEM((token_count, hidden_width), F32),
            pltpu.VMEM((token_count, hidden_width), F32),
            pltpu.VMEM((token_count, hidden_width), F32),
            pltpu.VMEM((token_count, 3 * padded), BF16),
            pltpu.VMEM((n, high, width), BF16),
            dma((2 * n,)),
            dma((2 * r + 1 + n,)),
        ],
        22 * MIB,
        dense // 8,
        MIB,
        (SMEM, idx),
        *each(VMEM, (middle_parts[half], grad_parts[half], *done["early"])),
        *each(FREE, middle_parts),
        *each(FREE, grad_parts),
        *each(VMEM, (*blocks_of("first", first_across), *blocks_of("second", second_across), *down_blocks)),
    )

    def weight_grads(columns, flipped):
        def work(act, act_other, low, low_other):
            shapes = [(w, block) if flipped else (block, w) for _, w in columns]
            return call(
                functools.partial(weight_grad_kernel, y_size, columns, flipped),
                [(shape, BF16 if dy else F32) for shape in shapes for dy in range(y_size)],
                [],
                14 * MIB,
                4 * token_count * block * y_size * sum(w for _, w in columns),
                8 * MIB,
                *each(VMEM, (act, act_other, low, low_other)),
            )

        return work

    task("Q0", "dy_swap", "Q1", lambda: [dy_send], swap)
    task("Q0", "lows_swap", "Q1", lambda: [lows], swap)
    task(
        "Q0",
        "ffn_parts",
        "Q1",
        lambda: [lows],
        lambda low: call(
            functools.partial(down_kernel, n, r, hidden_width),
            [(local, BF16, ANY)] * n,
            [pltpu.VMEM((n, *local), BF16), dma((n,))],
            14 * MIB,
            2 * token_count * model_width * hidden_width,
            8 * MIB,
            (SMEM, idx),
            (VMEM, low),
            *each(VMEM, down_blocks),
        ),
    )
    task("Q1", "m_swap", "Q2", lambda: [m_send], swap)
    for slot, until, name, act, other, at in (
        ("Q1", "Q2", "down", dy_keep, "dy_swap", 0),
        ("Q2", f"Q{end}", "first", m_keep, "m_swap", padded),
        (f"Q{end}", "B0", "second", m_keep, "m_swap", 2 * padded),
    ):
        task(
            slot,
            name + "_grad",
            until,
            lambda act=act, other=other: [act, done[other], lows, done["lows_swap"]],
            weight_grads([(at, hidden_width)], True),
        )
    send_y("down_sent", "down_grad", 0, "Q2", "B0")
    send_y("first_sent", "first_grad", 0, "B0", "B2")
    send_y("second_sent", "second_grad", 0, "B2", "N0")
    side_scatter(
        "ffn",
        "ffn_parts",
        [(f"B{end}", "K"), ("K", "N0"), (f"N{end}", "E"), ("E", "END")],
        [(f"Q{end}", "B0"), ("K", "N0"), ("E", "END")],
    )
    own, forward, backward = ring_scatter(partial, "Q", back, ahead)
    low_rows = -(-stat_rows // 16) * 16
    middle_grad, middle_grad_low = call(
        functools.partial(middle_grad_kernel, model_width),
        [(local, F32), ((token_count + low_rows, width), BF16)],
        [],
        8 * MIB,
        0,
        MIB,
        *each(VMEM, (cotangent, tokens, middle, middle_low, inverse_second, second_stat, own, forward, backward)),
    )
    branch_parts = ring_gather(middle_grad_low, "B")
    branch_parts[0] = clock("K", branch_parts[0])
    br_keep, br_send, proj, first_stat, *partial = call(
        functools.partial(back_kernel, n, r, count, model_width),
        [
            (token_half, BF16, ANY),
            (token_half, BF16, ANY),
            ((token_count, 5 * width), BF16, ANY),
            (row, F32),
            *with_stat,
        ],
        [
            pltpu.VMEM(full_shape, BF16),
            pltpu.VMEM((token_count, 5 * width), BF16),
            pltpu.VMEM((n, low_rows, width), BF16),
            pltpu.VMEM(local, BF16),
            pltpu.VMEM((token_count, HEAD), F32),
            pltpu.VMEM((token_count, HEAD), F32),
            pltpu.VMEM((token_count, HEAD), F32),
            pltpu.VMEM((n, high, width), BF16),
            dma((2 * n,)),
            dma((r + 1 + n,)),
        ],
        16 * MIB,
        dense // 8,
        MIB,
        (SMEM, idx),
        (SMEM, numbers),
        *each(VMEM, (pre, pre_gate, qkv, attended, inverse_attn, inverse_first)),
        *each(FREE, branch_parts),
        *each(VMEM, blocks_of("pack", packs[0])),
        *each(VMEM, gate_blocks),
    )
    task("N0", "proj_swap", "N1", lambda: [proj], swap)
    task("N0", "br_swap", "N1", lambda: [br_send], swap)
    for name, act, other, columns, flipped in (
        ("proj_grad", tokens_keep, lambda: done["tokens_swap"], [(0, 2 * width), (2 * width, 2 * width)], False),
        ("out_grad", br_keep, lambda: done["br_swap"], [(4 * width, width)], True),
    ):
        task(
            "N0",
            name,
            "N1",
            lambda act=act, other=other: [act, other(), proj, done["proj_swap"]],
            weight_grads(columns, flipped),
        )
    send_y("proj_sent0", "proj_grad", 0, "N1", f"N{end}")
    send_y("proj_sent1", "proj_grad", y_size, "N2", "END")
    send_y("out_sent", "out_grad", 0, "N2", "END")
    own, forward, backward = ring_scatter(partial, "N")
    forward = clock("E", forward)
    [token_grad] = call(
        functools.partial(token_grad_kernel, model_width),
        [(local, F32)],
        [],
        8 * MIB,
        0,
        MIB,
        *each(VMEM, (middle_grad, tokens, inverse_first, first_stat, own, forward, backward)),
    )
    token_grad = clock("END", token_grad)
    ffn_total = done["ffn_parts"][0].astype(F32) + done[f"ffn_b{half - 1}"].astype(F32) + done[f"ffn_f{half - 2}"].astype(F32)
    layer_out = (middle + ffn_total).astype(BF16)
    pairs_of_grads = [y_total(f"proj_sent{i}", "proj_grad", i * y_size) for i in range(2)]
    return (
        layer_out,
        token_grad,
        *(pairs_of_grads[i // 2][:, i % 2 * width : (i % 2 + 1) * width] for i in range(4)),
        y_total("out_sent", "out_grad", 0),
        y_total("first_sent", "first_grad", 0).T,
        y_total("second_sent", "second_grad", 0).T,
        y_total("down_sent", "down_grad", 0),
    )


def solution(mesh):
    both, flipped = P("rows", "cols"), P("cols", "rows")
    return jax.shard_map(
        functools.partial(shards, ring_order(mesh), mesh.shape["rows"] // 2),
        mesh=mesh,
        in_specs=(both, both, P("rows", None), P("cols"), both, both, both, both, flipped, both, both, flipped),
        out_specs=(both, both, both, both, both, both, flipped, both, both, flipped),
        check_vma=False,
    )
```
